256 devices in a mesh: gz: 32 (over z, x_lo, core), gy: 8 (over y, x_hi).
Axes of the slice: x: 4 (x_hi: 2, x_lo: 2; x = x_hi * 2 + x_lo), y: 4, z: 8, core: 2. Of those that a mesh axis runs over, the one named last changes fastest.
Arguments:
- vorticity: float32 [512, 512, 512], P('gz', 'gy'), may hold values from -12 to 12
- keep_one: int32 [7, 256, 256, 256], P(None, 'gz', 'gy'), may hold values 0 or 1
- keep_two: int32 [7, 128, 128, 128], P(None, 'gz', 'gy'), may hold values 0 or 1
- keep_three: int32 [7, 64, 64, 64], P(None, 'gz', 'gy'), may hold values 0 or 1
- keep_four: int32 [7, 32, 32, 32], P(None, 'gz', 'gy'), may hold values 0 or 1
- keep_coarse: int32 [32, 32, 32], P('gz', 'gy'), may hold values 0 or 1
Outputs:
- coherent: float32 [512, 512, 512], P('gz', 'gy')
The draws below stay inside these ranges and needn't reach their ends.
All inputs are finite; a program needn't handle non-finite values. No bound on the sum of `keep_one` or of `keep_two` or of `keep_three` or of `keep_four` or of `keep_coarse` on one device may be relied on, other than what follows from the above.
Results may differ from the reference program's by a relative error of at most 0.00017.
Values sent between devices are 32-bit elements; how exact they have to be, the bound alone decides.
No kernel may reach another device: no remote copies, remote signals or barrier semaphores. Data moves between devices by JAX's collectives and lax.ppermute only.
A program may use at most 128 MiB of HBM per device.

```python
import math
import jax
import jax.numpy as jnp
from jax import lax

NX = 512
NZ = 512
NY = 512


def draw_vorticity(key, part):
    rough_key = jax.random.fold_in(key, 11)
    z_key = jax.random.fold_in(key, 12)
    y_key = jax.random.fold_in(key, 13)
    x_key = jax.random.fold_in(key, 14)
    phase_key = jax.random.fold_in(key, 15)
    waves_z = jax.random.randint(z_key, (6,), 1, 22).astype(jnp.float32)
    waves_y = jax.random.randint(y_key, (6,), 1, 22).astype(jnp.float32)
    waves_x = jax.random.randint(x_key, (6,), 0, max(2, NX // 24)).astype(jnp.float32)
    phases = jax.random.uniform(phase_key, (6,), jnp.float32, 0.0, 2.0 * math.pi)
    z_pos = jnp.arange(NZ, dtype=jnp.float32)[:, None, None] / NZ
    y_pos = jnp.arange(NY, dtype=jnp.float32)[None, :, None] / NY
    x_pos = jnp.arange(NX, dtype=jnp.float32)[None, None, :] / NX
    smooth = jnp.zeros((NZ, NY, NX), jnp.float32)
    for mode_no in range(6):
        argument = 2.0 * math.pi * (waves_z[mode_no] * z_pos + waves_y[mode_no] * y_pos + waves_x[mode_no] * x_pos)
        smooth = smooth + jnp.sin(argument + phases[mode_no])
    rough = jnp.clip(jax.random.normal(rough_key, (NZ, NY, NX), jnp.float32), -6.0, 6.0)
    return rough + 0.8 * smooth


def with_ends(array, rng, least, largest):
    shape = array.shape
    index_at = [jax.random.randint(jax.random.fold_in(rng, axis), (), 0, shape[axis]) for axis in range(len(shape))]
    array = array.at[tuple(index_at)].set(least)
    longest = shape.index(max(shape))
    index_at[longest] = (index_at[longest] + 1) % shape[longest]
    return array.at[tuple(index_at)].set(largest)


def setup_inputs(seed: int = 0) -> dict:
    key_of = jax.random.split(jax.random.key(seed), 7)
    return {
        "vorticity": draw_vorticity(jax.random.fold_in(key_of[6], 71), 0),
        "keep_one": with_ends((jax.random.randint(key_of[1], (7, NZ // 2, NY // 2, NX // 2), 0, 2) < 1).astype(jnp.int32), jax.random.fold_in(key_of[1], 1), 0, 1),
        "keep_two": with_ends((jax.random.randint(key_of[2], (7, NZ // 4, NY // 4, NX // 4), 0, 2) < 1).astype(jnp.int32), jax.random.fold_in(key_of[2], 1), 0, 1),
        "keep_three": with_ends((jax.random.randint(key_of[3], (7, NZ // 8, NY // 8, NX // 8), 0, 2) < 1).astype(jnp.int32), jax.random.fold_in(key_of[3], 1), 0, 1),
        "keep_four": with_ends((jax.random.randint(key_of[4], (7, NZ // 16, NY // 16, NX // 16), 0, 2) < 1).astype(jnp.int32), jax.random.fold_in(key_of[4], 1), 0, 1),
        "keep_coarse": with_ends((jax.random.randint(key_of[5], (NZ // 16, NY // 16, NX // 16), 0, 2) < 1).astype(jnp.int32), jax.random.fold_in(key_of[5], 1), 0, 1),
    }


low_taps = (0.11154074335008017, 0.4946238903983854, 0.7511339080215775, 0.3152503517092432,
            -0.22626469396516913, -0.12976686756709563, 0.09750160558707936, 0.02752286553001629,
            -0.031582039318031156, 0.0005538422009938016, 0.004777257511010651, -0.00107730108499558)
high_taps = tuple(((-1.0) ** k) * low_taps[11 - k] for k in range(12))


def wrap_right(source, axis_dim, rim_width):
    length = source.shape[axis_dim]
    copies = 1 + (rim_width + length - 1) // length
    repeated = jnp.concatenate([source] * copies, axis=axis_dim)
    return lax.slice_in_dim(repeated, 0, length + rim_width, axis=axis_dim)


def wrap_left(source, axis_dim, rim_width):
    length = source.shape[axis_dim]
    copies = 1 + (rim_width + length - 1) // length
    repeated = jnp.concatenate([source] * copies, axis=axis_dim)
    total_len = copies * length
    return lax.slice_in_dim(repeated, total_len - length - rim_width, total_len, axis=axis_dim)


def split_pair(extended, axis_dim, length):
    low_part = None
    high_part = None
    for k in range(12):
        sliced = lax.slice_in_dim(extended, k, k + length - 1, stride=2, axis=axis_dim)
        if k == 0:
            low_part = low_taps[k] * sliced
            high_part = high_taps[k] * sliced
        else:
            low_part = low_part + low_taps[k] * sliced
            high_part = high_part + high_taps[k] * sliced
    return low_part, high_part


def merge_pair(low_ext, high_ext, axis_dim, coarse_len):
    even_part = None
    odd_part = None
    for t in range(6):
        low_slice = lax.slice_in_dim(low_ext, 5 - t, 5 - t + coarse_len, axis=axis_dim)
        high_slice = lax.slice_in_dim(high_ext, 5 - t, 5 - t + coarse_len, axis=axis_dim)
        even_term = low_taps[2 * t] * low_slice + high_taps[2 * t] * high_slice
        odd_term = low_taps[2 * t + 1] * low_slice + high_taps[2 * t + 1] * high_slice
        if t == 0:
            even_part = even_term
            odd_part = odd_term
        else:
            even_part = even_part + even_term
            odd_part = odd_part + odd_term
    paired = jnp.stack([even_part, odd_part], axis=axis_dim + 1)
    new_shape = even_part.shape[:axis_dim] + (2 * coarse_len,) + even_part.shape[axis_dim + 1:]
    return paired.reshape(new_shape)


def analyse(source, axis_dim):
    return split_pair(wrap_right(source, axis_dim, 10), axis_dim, source.shape[axis_dim])


def synthesize(low_part, high_part, axis_dim):
    coarse_len = low_part.shape[axis_dim]
    return merge_pair(wrap_left(low_part, axis_dim, 5), wrap_left(high_part, axis_dim, 5), axis_dim, coarse_len)


def reference(vorticity, keep_one, keep_two, keep_three, keep_four, keep_coarse):
    keep_list = (keep_one, keep_two, keep_three, keep_four)
    approx = vorticity
    kept_list = []
    for level_no in range(4):
        subbands = list(analyse(approx, 2))
        for axis_dim in (1, 0):
            pair_list = [analyse(member, axis_dim) for member in subbands]
            subbands = [p[0] for p in pair_list] + [p[1] for p in pair_list]
        kept_list.append(jnp.stack(subbands[1:]) * keep_list[level_no].astype(jnp.float32))
        approx = subbands[0]
    rebuilt = approx * keep_coarse.astype(jnp.float32)
    for level_no in (3, 2, 1, 0):
        subbands = [rebuilt] + [kept_list[level_no][b] for b in range(7)]
        subbands = [synthesize(subbands[b], subbands[b + 4], 0) for b in range(4)]
        subbands = [synthesize(subbands[b], subbands[b + 2], 1) for b in range(2)]
        rebuilt = synthesize(subbands[0], subbands[1], 2)
    return rebuilt
```

```python
import functools

import jax
import jax.numpy as jnp
import ml_dtypes
import numpy as np
from jax import lax
from jax.experimental import pallas as pl
from jax.experimental.pallas import tpu as pltpu
from jax.sharding import PartitionSpec as P

low_taps = (
    0.11154074335008017,
    0.4946238903983854,
    0.7511339080215775,
    0.3152503517092432,
    -0.22626469396516913,
    -0.12976686756709563,
    0.09750160558707936,
    0.02752286553001629,
    -0.031582039318031156,
    0.0005538422009938016,
    0.004777257511010651,
    -0.00107730108499558,
)
high_taps = tuple(((-1.0) ** k * low_taps[11 - k] for k in range(12)))

GZ, GY = 32, 8
MEMBERS = 4
F32, BF16 = jnp.float32, jnp.bfloat16


def tail_of(s):
    return (s + 11) // 2


def band(taps, n, s):
    t = tail_of(s)
    out = np.zeros((t + n // 2, s + n))
    for row in range(t + n // 2):
        for col in range(s + n):
            k = (col - s) - 2 * (row - t)
            if 0 <= k < 12:
                out[row, col] = taps[k]
    return out


def periodic(taps, n):
    out = np.zeros((n // 2, n))
    for i in range(n // 2):
        for k in range(12):
            out[i, (2 * i + k) % n] += taps[k]
    return out


def rank_five():
    block = np.concatenate([band(low_taps, 10, 0)[:5], band(high_taps, 10, 0)[:5]])
    u, sing, vt = np.linalg.svd(block)
    return u[:, :5] * sing[:5], vt[:5]


def pair(matrix):
    high = matrix.astype(ml_dtypes.bfloat16)
    low = (matrix - high.astype(np.float64)).astype(ml_dtypes.bfloat16)
    return np.stack([high, low])


def padded(matrix, rows, cols):
    out = np.zeros((rows, cols))
    out[: matrix.shape[0], : matrix.shape[1]] = matrix
    return out


@functools.lru_cache(None)
def tables():
    spread, basis = rank_five()
    mats = {}
    x1 = np.concatenate([periodic(low_taps, 512), periodic(high_taps, 512)])
    mats["x1f"], mats["x1i"] = x1.T, x1
    lo2 = periodic(low_taps, 256)
    lo3 = periodic(low_taps, 128) @ lo2
    xm = np.concatenate(
        [
            lo2,
            periodic(high_taps, 256),
            lo3,
            periodic(high_taps, 128) @ lo2,
            periodic(low_taps, 64) @ lo3,
            periodic(high_taps, 64) @ lo3,
            np.zeros((64, 256)),
        ]
    )
    mats["xmf"], mats["xmi"] = xm.T, xm
    y1 = np.concatenate([band(low_taps, 64, 0)[5:], band(high_taps, 64, 0)[5:]])
    mats["y1f"] = np.kron(np.eye(4), y1)
    mats["y1i"] = mats["y1f"].T
    pick = padded(basis, 5, 64)
    mats["y1q"] = padded(np.kron(np.eye(8), pick), 48, 512)
    mats["y1qt"] = mats["y1q"].T
    put = np.zeros((64, 5))
    put[27:32], put[59:64] = spread[:5], spread[5:]
    mats["y1u"] = padded(np.kron(np.eye(8), put), 512, 48)
    mats["y1ut"] = mats["y1u"].T
    z1 = np.concatenate([band(low_taps, 16, 0)[5:], band(high_taps, 16, 0)[5:]])
    mats["z1f"] = np.kron(z1, np.eye(16))
    mats["z1i"] = mats["z1f"].T
    zput = np.zeros((16, 5))
    zput[3:8], zput[11:16] = spread[:5], spread[5:]
    mats["z1u"] = np.kron(zput, np.eye(16))
    zpick = padded(basis, 5, 16)
    mats["z1qt"] = np.kron(zpick.T, np.eye(16))
    lo_a = band(low_taps, 32, 0)
    lo_b = band(low_taps, 16, 5) @ lo_a
    lev2 = [lo_a, band(high_taps, 32, 0)]
    lev3 = [lo_b, band(high_taps, 16, 5) @ lo_a]
    lev4 = [band(low_taps, 8, 8) @ lo_b, band(high_taps, 8, 8) @ lo_b]

    def row2(b, i):
        return lev2[b][i + 5]

    def row3(b, i):
        return lev3[b][i + 8]

    def row4(b, i):
        return lev4[b][i + 9]

    pick32 = padded(basis, 5, 32)
    put2 = np.zeros((2, 16, 5))
    put2[0, 11:], put2[1, 11:] = spread[:5], spread[5:]

    y2 = np.zeros((256, 256))
    y2u = np.zeros((256, 64))
    y34 = np.zeros((592, 512))
    y2q = np.kron(np.eye(8), padded(pick32, 8, 32))
    for m in range(4):
        for z in range(8):
            cells = slice(z * 32, z * 32 + 32)
            cells4 = slice(256 + z * 32, 256 + z * 32 + 32)
            for r in range(8):
                row = (m * 8 + z) * 8 + r
                y2[row, cells] = row2(r // 4, 4 * m + r % 4)
                y2u[row, z * 8 : z * 8 + 5] = put2[r // 4, 4 * m + r % 4]
                if r < 4:
                    y34[row, cells] = row3(r // 2, 2 * m + r % 2)
                    y34[256 + row, cells] = row3(r // 2, 2 * m + r % 2 - 8)
                elif r < 6:
                    y34[row, cells4] = row4(r - 4, m)
                    y34[256 + row, cells4] = row4(r - 4, m - 4)
    y34p = np.zeros((256, 80))
    for z in range(8):
        cells4 = slice(256 + z * 32, 256 + z * 32 + 32)
        for by in range(2):
            for i in range(4):
                y34[512 + z * 8 + by * 4 + i, cells4] = row4(by, i - 8)
                y34p[(i * 8 + z) * 8 + 4 + by, z * 8 + by * 4 + i] = 1.0
            y34[576 + z * 2 + by, cells4] = row4(by, -9)
            y34p[(3 * 8 + z) * 8 + 4 + by, 64 + z * 2 + by] = 1.0
    mats["y2"], mats["y2t"] = y2, y2.T
    mats["y2u"], mats["y2ut"] = y2u, y2u.T
    mats["y2q"], mats["y2qt"] = y2q, y2q.T
    mats["y34"], mats["y34t"] = y34, y34.T
    mats["y34p"], mats["y34pt"] = y34p, y34p.T

    eye8 = np.eye(8)
    z2 = np.kron(np.array([row2(b, i) for b in range(2) for i in range(16)]), eye8)
    z2q = padded(np.kron(pick32, eye8), 48, 256)
    z2u = padded(np.kron(put2.reshape(32, 5), eye8), 256, 48)
    z34 = np.zeros((288, 32, 8))
    z34p = np.zeros((128, 32))
    for b in range(2):
        for i in range(8):
            for r in range(4):
                z34[(b * 8 + i) * 8 + r, :, r] = row3(b, i)
                z34[128 + (b * 8 + i) * 8 + r, :, r] = row3(b, i - 8)
        for by in range(2):
            for i in range(4):
                slot = b * 4 + i
                z34[slot * 8 + 4 + by, :, 4 + by] = row4(b, i)
                z34[128 + slot * 8 + 4 + by, :, 4 + by] = row4(b, i - 4)
                z34[256 + slot * 2 + by, :, 4 + by] = row4(b, i - 8)
                z34p[slot * 8 + 4 + by, slot * 2 + by] = 1.0
            z34[272 + b * 2 + by, :, 4 + by] = row4(b, -9)
            z34p[(b * 4 + 3) * 8 + 4 + by, 16 + b * 2 + by] = 1.0
    z34 = z34.reshape(288, 256)
    mats["z2"], mats["z2t"] = z2, z2.T
    mats["z2q"], mats["z2qt"] = z2q, z2q.T
    mats["z2u"], mats["z2ut"] = z2u, z2u.T
    mats["z34"], mats["z34t"] = z34, z34.T
    mats["z34p"], mats["z34pt"] = z34p, z34p.T
    return {name: pair(matrix) for name, matrix in mats.items()}


SPREAD, BASIS = rank_five()
Z1LO = band(low_taps, 16, 0)[5:]


def halves(value):
    high = value.astype(BF16)
    return high, (value - high.astype(F32)).astype(BF16)


def dot(a, b):
    return lax.dot_general(a, b, (((1,), (0,)), ((), ())), preferred_element_type=F32)


def left(table, value):
    vh, vl = halves(value)
    return dot(table[0], vh) + dot(table[0], vl) + dot(table[1], vh)


def right(value, table):
    vh, vl = halves(value)
    return dot(vh, table[0]) + dot(vl, table[0]) + dot(vh, table[1])


def combine(weights, planes):
    total = None
    for weight, plane in zip(weights, planes):
        if weight == 0.0:
            continue
        term = float(weight) * plane()
        total = term if total is None else total + term
    return total


def call(kernel, outs, *operands):
    spec = pl.BlockSpec(memory_space=pltpu.VMEM)
    shapes = [jax.ShapeDtypeStruct(shape, F32) for shape in outs]
    return pl.pallas_call(
        kernel,
        out_shape=shapes,
        in_specs=[spec] * len(operands),
        out_specs=[spec] * len(outs),
        compiler_params=pltpu.CompilerParams(vmem_limit_bytes=48 * 2**20),
    )(*operands)


def x_split(v, x1f, y1q, f, q):
    for c in range(4):
        part = v[4 * c : 4 * c + 4].reshape(256, 512)
        f[4 * c : 4 * c + 4] = right(part, x1f).reshape(4, 64, 512)
    for half in range(2):
        part = f[8 * half : 8 * half + 8].reshape(512, 512)
        q[half] = left(y1q, part)[:40]


def y_split(f, q, y1f, y1u, g, qa, qb):
    for half in range(2):
        rim = jnp.concatenate([q[half], jnp.zeros((8, 512), F32)], axis=0)
        extra = left(y1u, rim)
        for c in range(2):
            z = 8 * half + 4 * c
            part = left(y1f, f[z : z + 4].reshape(256, 512))
            g[z : z + 4] = (part + extra[256 * c : 256 * c + 256]).reshape(4, 64, 512)
    for n in range(5):
        plane = combine(BASIS[n], [lambda j=j: g[j] for j in range(10)])
        qa[n] = plane[:32, :256]
        qb[n, :, :256] = plane[:32, 256:]
        qb[n, :, 256:] = plane[32:]


def deep_split(g, qa, xmf, y2, y2q, y34, own, m1, m2, m3, low):
    for i in range(8):
        plane = combine(Z1LO[i], [lambda j=j: g[j, :32, :256] for j in range(16)])
        if i >= 3:
            plane = plane + combine(SPREAD[i - 3], [lambda n=n: qa[n] for n in range(5)])
        low[i] = plane
    wide = right(low[...].reshape(256, 256), xmf)
    own[:, :256] = left(y2, wide[:, :256])
    rim = left(y2q, wide[:, :256])
    m1[256:320] = rim[:, :128]
    m1[320:384] = rim[:, 128:]
    rest = left(y34, jnp.concatenate([wide[:, 256:384], wide[:, 384:]], axis=0))
    own[:, 256:] = rest[:256]
    m1[:256] = rest[256:512]
    m2[...] = rest[512:576]
    m3[...] = rest[576:592]


def y_gather(own, m1, m2, m3, y2u, y34p, w):
    rim = jnp.concatenate([m1[256:320], m1[320:384]], axis=1)
    w[:, :256] = own[:, :256] + left(y2u, rim)
    far = jnp.concatenate([m2[...], m3[...]], axis=0)
    w[:, 256:] = own[:, 256:] + m1[:256] + left(y34p, far)


def z_split(w, z2, z2q, z34, own2, own34, n1, n2, n3):
    own2[...] = left(z2, w[:, :256])
    rim = left(z2q, w[:, :256])
    n1[128:168] = rim[:40, :128]
    n1[168:208] = rim[:40, 128:]
    rest = left(z34, w[:, 256:])
    own34[...] = rest[:128]
    n1[:128] = rest[128:256]
    n2[...] = rest[256:272]
    n3[...] = rest[272:280]


def z_mask(own2, own34, n1, n2, n3, keep2, keep34, z2u, z34p, z2ut, z34pt, c2, c34, s1, s2, s3):
    zeros = jnp.zeros((8, 256), F32)
    rim = jnp.concatenate([n1[128:168], n1[168:208]], axis=1)
    rim = jnp.concatenate([rim, zeros], axis=0)
    part2 = (own2[...] + left(z2u, rim)) * keep2[...]
    far = jnp.concatenate([n2[...], n3[...], jnp.zeros((8, 128), F32)], axis=0)
    part34 = (own34[...] + n1[:128] + left(z34p, far)) * keep34[...]
    c2[...] = part2
    c34[...] = part34
    back = left(z2ut, part2)
    s1[:128] = part34
    s1[128:168] = back[:40, :128]
    s1[168:208] = back[:40, 128:]
    back = left(z34pt, part34)
    s2[...] = back[:16]
    s3[...] = back[16:24]


def z_join(c2, c34, s1, s2, s3, z2t, z2qt, z34t, w):
    rim = jnp.concatenate([s1[128:168], s1[168:208]], axis=1)
    rim = jnp.concatenate([rim, jnp.zeros((8, 256), F32)], axis=0)
    w[:, :256] = left(z2t, c2[...]) + left(z2qt, rim)
    rows = [c34[...], s1[:128], s2[...], s3[...], jnp.zeros((8, 128), F32)]
    w[:, 256:] = left(z34t, jnp.concatenate(rows, axis=0))


def y_send(w, y2ut, y34pt, m1, m2, m3):
    m1[:256] = w[:, 256:]
    rim = left(y2ut, w[:, :256])
    m1[256:320] = rim[:, :128]
    m1[320:384] = rim[:, 128:]
    far = left(y34pt, w[:, 256:])
    m2[...] = far[:64]
    m3[...] = far[64:]


def deep_join(w, m1, m2, m3, xmi, y2t, y2qt, y34t, kept_hi, low, pa):
    rim = jnp.concatenate([m1[256:320], m1[320:384]], axis=1)
    first = left(y2t, w[:, :256]) + left(y2qt, rim)
    rows = [w[:, 256:], m1[:256], m2[...], m3[...]]
    rest = left(y34t, jnp.concatenate(rows, axis=0))
    wide = jnp.concatenate([first, rest[:256], rest[256:]], axis=1)
    low[...] = right(wide, xmi).reshape(8, 32, 256)
    for n in range(5):
        lows = combine(SPREAD[:5, n], [lambda i=i: low[i + 3] for i in range(5)])
        highs = combine(SPREAD[5:, n], [lambda i=i: kept_hi[i + 3, :32, :256] for i in range(5)])
        pa[n] = lows + highs


def details(g, qa, qb, keep, z1f, z1u, kept_lo, kept_hi, pb):
    for c in range(4):
        rows = slice(16 * c, 16 * c + 16)
        if c < 2:
            rim = jnp.concatenate([qa[:, rows], qb[:, rows, :256]], axis=2)
        else:
            rim = qb[:, 16 * c - 32 : 16 * c - 16, 256:]
        out = left(z1f, g[:, rows].reshape(256, 512)) + left(z1u, rim.reshape(80, 512))
        out = out.reshape(16, 16, 512)
        by = c // 2
        at = slice(16 * (c % 2), 16 * (c % 2) + 16)
        for bz in range(2):
            target = kept_hi if bz else kept_lo
            for bx in range(2):
                cols = slice(256 * bx, 256 * bx + 256)
                number = 4 * bz + 2 * by + bx
                if number:
                    mask = keep[number - 1, :, at].astype(F32)
                    target[:, rows, cols] = out[8 * bz : 8 * bz + 8, :, cols] * mask
                else:
                    target[:, rows, cols] = jnp.zeros((8, 16, 256), F32)
    for n in range(5):
        plane = combine(SPREAD[:5, n], [lambda i=i: kept_lo[i + 3] for i in range(5)])
        plane = plane + combine(SPREAD[5:, n], [lambda i=i: kept_hi[i + 3] for i in range(5)])
        pb[n, :, :256] = plane[:32, 256:]
        pb[n, :, 256:] = plane[32:]


def z_merge(kept_lo, kept_hi, low, pa, pb, z1i, z1qt, y1ut, g, q):
    for c in range(4):
        rows = slice(16 * c, 16 * c + 16)
        if c < 2:
            rim = jnp.concatenate([pa[:, rows], pb[:, rows, :256]], axis=2)
            lows = jnp.concatenate([low[:, rows], kept_lo[:, rows, 256:]], axis=2)
        else:
            rim = pb[:, 16 * c - 32 : 16 * c - 16, 256:]
            lows = kept_lo[:, rows]
        both = jnp.concatenate([lows, kept_hi[:, rows]], axis=0).reshape(256, 512)
        out = left(z1i, both) + left(z1qt, rim.reshape(80, 512))
        g[:, rows] = out.reshape(16, 16, 512)
    for half in range(2):
        part = g[8 * half : 8 * half + 8].reshape(512, 512)
        q[half] = left(y1ut, part)[:40]


def x_merge(g, q, y1i, y1qt, x1i, out):
    for half in range(2):
        rim = jnp.concatenate([q[half], jnp.zeros((8, 512), F32)], axis=0)
        extra = left(y1qt, rim)
        for c in range(2):
            z = 8 * half + 4 * c
            part = left(y1i, g[z : z + 4].reshape(256, 512)) + extra[256 * c : 256 * c + 256]
            out[z : z + 4] = right(part, x1i).reshape(4, 64, 512)


def shifted(value, axis, by):
    count = GZ if axis == "gz" else GY
    return lax.ppermute(value, axis, [(i, (i + by) % count) for i in range(count)])


def regroup(value):
    groups = [[MEMBERS * g + a for a in range(MEMBERS)] for g in range(GZ // MEMBERS)]
    return lax.all_to_all(value, "gz", 0, 0, axis_index_groups=groups)


def coarse_masks(keep_two, keep_three, keep_four, keep_coarse):
    def grouped(keep, first, each):
        zs, ys, xs = keep.shape[1:]
        full = jnp.concatenate([first, keep], axis=0).astype(F32)
        full = full.reshape(2, 2, 2, zs, 4, each, xs)
        full = full.transpose(4, 0, 3, 1, 5, 2, 6)
        return full.reshape(4, 2, zs, 2 * each, 2 * xs)

    two = grouped(keep_two, jnp.zeros_like(keep_two[:1]), 4).reshape(4, 64, 256)
    three = grouped(keep_three, jnp.zeros_like(keep_three[:1]), 2).reshape(4, 16, 128)
    four = grouped(keep_four, keep_coarse[None], 1).reshape(4, 4, 64)
    four = jnp.pad(four, ((0, 0), (0, 4), (0, 64)))
    two = jnp.concatenate([two[:, :, :128], two[:, :, 128:]], axis=1)
    sent = regroup(jnp.concatenate([two, three, four], axis=1))
    two = jnp.concatenate([sent[:, :64], sent[:, 64:128]], axis=2)
    two = two.reshape(4, 2, 4 * 8, 256).transpose(1, 0, 2, 3).reshape(256, 256)
    three = sent[:, 128:144].reshape(4, 2, 2, 4, 128).transpose(1, 0, 2, 3, 4)
    three = three.reshape(16, 4, 128)
    four = sent[:, 144:148].reshape(4, 2, 2, 128).transpose(1, 0, 2, 3).reshape(8, 2, 128)
    four = jnp.pad(four, ((0, 8), (0, 2), (0, 0)))
    return two, jnp.concatenate([three, four], axis=1).reshape(128, 128)


def on_device(vorticity, keep_one, keep_two, keep_three, keep_four, keep_coarse):
    table = {name: jnp.asarray(matrix) for name, matrix in tables().items()}
    keep2, keep34 = coarse_masks(keep_two, keep_three, keep_four, keep_coarse)

    f, q = call(x_split, [(16, 64, 512), (2, 40, 512)], vorticity, table["x1f"], table["y1q"])
    q = shifted(q, "gy", -1)
    g, qa, qb = call(
        y_split,
        [(16, 64, 512), (5, 32, 256), (5, 32, 768)],
        f,
        q,
        table["y1f"],
        table["y1u"],
    )
    qa = shifted(qa, "gz", -1)
    qb = shifted(qb, "gz", -1)
    own, m1, m2, m3, _ = call(
        deep_split,
        [(256, 384), (384, 128), (64, 128), (16, 128), (8, 32, 256)],
        g,
        qa,
        table["xmf"],
        table["y2"],
        table["y2q"],
        table["y34"],
    )
    m1, m2, m3 = shifted(m1, "gy", -1), shifted(m2, "gy", -2), shifted(m3, "gy", -3)
    (w,) = call(y_gather, [(256, 384)], own, m1, m2, m3, table["y2u"], table["y34p"])
    w = regroup(w.reshape(4, 64, 384)).reshape(256, 384)
    own2, own34, n1, n2, n3 = call(
        z_split,
        [(256, 256), (128, 128), (208, 128), (16, 128), (8, 128)],
        w,
        table["z2"],
        table["z2q"],
        table["z34"],
    )
    n1, n2, n3 = shifted(n1, "gz", -4), shifted(n2, "gz", -8), shifted(n3, "gz", -12)

    kept_lo, kept_hi, pb = call(
        details,
        [(8, 64, 512), (8, 64, 512), (5, 32, 768)],
        g,
        qa,
        qb,
        keep_one,
        table["z1f"],
        table["z1u"],
    )
    pb = shifted(pb, "gz", 1)

    c2, c34, s1, s2, s3 = call(
        z_mask,
        [(256, 256), (128, 128), (208, 128), (16, 128), (8, 128)],
        own2,
        own34,
        n1,
        n2,
        n3,
        keep2,
        keep34,
        table["z2u"],
        table["z34p"],
        table["z2ut"],
        table["z34pt"],
    )
    s1, s2, s3 = shifted(s1, "gz", 4), shifted(s2, "gz", 8), shifted(s3, "gz", 12)
    (w,) = call(z_join, [(256, 384)], c2, c34, s1, s2, s3, table["z2t"], table["z2qt"], table["z34t"])
    w = regroup(w.reshape(4, 64, 384)).reshape(256, 384)
    m1, m2, m3 = call(
        y_send, [(384, 128), (64, 128), (16, 128)], w, table["y2ut"], table["y34pt"]
    )
    m1, m2, m3 = shifted(m1, "gy", 1), shifted(m2, "gy", 2), shifted(m3, "gy", 3)
    low, pa = call(
        deep_join,
        [(8, 32, 256), (5, 32, 256)],
        w,
        m1,
        m2,
        m3,
        table["xmi"],
        table["y2t"],
        table["y2qt"],
        table["y34t"],
        kept_hi,
    )
    pa = shifted(pa, "gz", 1)
    g, q = call(
        z_merge,
        [(16, 64, 512), (2, 40, 512)],
        kept_lo,
        kept_hi,
        low,
        pa,
        pb,
        table["z1i"],
        table["z1qt"],
        table["y1ut"],
    )
    q = shifted(q, "gy", 1)
    (out,) = call(x_merge, [(16, 64, 512)], g, q, table["y1i"], table["y1qt"], table["x1i"])
    return out


def solution(mesh):
    in_specs = (
        P("gz", "gy", None),
        P(None, "gz", "gy", None),
        P(None, "gz", "gy", None),
        P(None, "gz", "gy", None),
        P(None, "gz", "gy", None),
        P("gz", "gy", None),
    )
    out_specs = P("gz", "gy", None)
    return jax.shard_map(
        on_device, mesh=mesh, in_specs=in_specs, out_specs=out_specs, check_vma=False
    )
```

```python
import functools

import jax
import jax.numpy as jnp
import ml_dtypes
import numpy as np
from jax import lax
from jax.experimental import pallas as pl
from jax.experimental.pallas import tpu as pltpu
from jax.sharding import PartitionSpec as P

low_taps = (
    0.11154074335008017,
    0.4946238903983854,
    0.7511339080215775,
    0.3152503517092432,
    -0.22626469396516913,
    -0.12976686756709563,
    0.09750160558707936,
    0.02752286553001629,
    -0.031582039318031156,
    0.0005538422009938016,
    0.004777257511010651,
    -0.00107730108499558,
)
high_taps = tuple(((-1.0) ** k * low_taps[11 - k] for k in range(12)))

GZ, GY = 32, 8
MEMBERS = 4
F32, BF16 = jnp.float32, jnp.bfloat16


def tail_of(s):
    return (s + 11) // 2


def band(taps, n, s):
    t = tail_of(s)
    out = np.zeros((t + n // 2, s + n))
    for row in range(t + n // 2):
        for col in range(s + n):
            k = (col - s) - 2 * (row - t)
            if 0 <= k < 12:
                out[row, col] = taps[k]
    return out


def periodic(taps, n):
    out = np.zeros((n // 2, n))
    for i in range(n // 2):
        for k in range(12):
            out[i, (2 * i + k) % n] += taps[k]
    return out


def rank_five():
    block = np.concatenate([band(low_taps, 10, 0)[:5], band(high_taps, 10, 0)[:5]])
    u, sing, vt = np.linalg.svd(block)
    return u[:, :5] * sing[:5], vt[:5]


def pair(matrix):
    high = matrix.astype(ml_dtypes.bfloat16)
    low = (matrix - high.astype(np.float64)).astype(ml_dtypes.bfloat16)
    return np.stack([high, low])


def padded(matrix, rows, cols):
    out = np.zeros((rows, cols))
    out[: matrix.shape[0], : matrix.shape[1]] = matrix
    return out


@functools.lru_cache(None)
def tables():
    spread, basis = rank_five()
    mats = {}
    x1 = np.concatenate([periodic(low_taps, 512), periodic(high_taps, 512)])
    mats["x1f"], mats["x1i"], mats["x1l"] = x1.T, x1, x1[:256]
    lo2 = periodic(low_taps, 256)
    lo3 = periodic(low_taps, 128) @ lo2
    xm = np.concatenate(
        [
            lo2,
            periodic(high_taps, 256),
            lo3,
            periodic(high_taps, 128) @ lo2,
            periodic(low_taps, 64) @ lo3,
            periodic(high_taps, 64) @ lo3,
            np.zeros((64, 256)),
        ]
    )
    mats["xmf"], mats["xmi"] = xm.T, xm
    y1 = np.concatenate([band(low_taps, 64, 0)[5:], band(high_taps, 64, 0)[5:]])
    mats["y1f"] = np.kron(np.eye(4), y1)
    mats["y1i"] = mats["y1f"].T
    pick = padded(basis, 5, 64)
    mats["y1q"] = padded(np.kron(np.eye(8), pick), 48, 512)
    mats["y1qt"] = mats["y1q"].T
    put = np.zeros((64, 5))
    put[27:32], put[59:64] = spread[:5], spread[5:]
    mats["y1u"] = padded(np.kron(np.eye(8), put), 512, 48)
    mats["y1ut"] = mats["y1u"].T
    mats["y1l"] = np.kron(np.eye(4), y1[:32])
    mats["y1lt"] = mats["y1l"].T
    mats["y1ul"] = padded(np.kron(np.eye(8), put[:32]), 256, 48)
    mats["y1ult"] = mats["y1ul"].T
    corner = np.kron(np.eye(5), padded(pick, 8, 64))
    mats["r5l"] = np.concatenate([np.kron(np.eye(5), y1[:32]), corner])
    mats["r5h"] = np.kron(np.eye(5), y1[32:])
    mats["r5u"] = np.kron(np.eye(5), padded(put, 64, 8))
    mats["r5ut"] = mats["r5u"].T
    mats["r5ul"] = np.kron(np.eye(5), padded(put[:32], 32, 8))
    mats["r5ult"] = mats["r5ul"].T
    far = np.zeros((2, 48, 40))
    for z in range(10):
        for k in range(5):
            far[z // 8, (z % 8) * 5 + k, k::8] = basis[:, z]
    mats["r5z"] = far.reshape(96, 40)
    z1 = np.concatenate([band(low_taps, 16, 0)[5:], band(high_taps, 16, 0)[5:]])
    mats["z1f"] = np.kron(z1, np.eye(16))
    mats["z1i"] = mats["z1f"].T
    zput = np.zeros((16, 5))
    zput[3:8], zput[11:16] = spread[:5], spread[5:]
    mats["z1u"] = np.kron(zput, np.eye(16))
    zpick = padded(basis, 5, 16)
    mats["z1qt"] = np.kron(zpick.T, np.eye(16))
    lo_a = band(low_taps, 32, 0)
    lo_b = band(low_taps, 16, 5) @ lo_a
    lev2 = [lo_a, band(high_taps, 32, 0)]
    lev3 = [lo_b, band(high_taps, 16, 5) @ lo_a]
    lev4 = [band(low_taps, 8, 8) @ lo_b, band(high_taps, 8, 8) @ lo_b]

    def row2(b, i):
        return lev2[b][i + 5]

    def row3(b, i):
        return lev3[b][i + 8]

    def row4(b, i):
        return lev4[b][i + 9]

    pick32 = padded(basis, 5, 32)
    put2 = np.zeros((2, 16, 5))
    put2[0, 11:], put2[1, 11:] = spread[:5], spread[5:]

    y2 = np.zeros((256, 256))
    y2u = np.zeros((256, 64))
    y34 = np.zeros((592, 512))
    y2q = np.kron(np.eye(8), padded(pick32, 8, 32))
    for m in range(4):
        for z in range(8):
            cells = slice(z * 32, z * 32 + 32)
            cells4 = slice(256 + z * 32, 256 + z * 32 + 32)
            for r in range(8):
                row = (m * 8 + z) * 8 + r
                y2[row, cells] = row2(r // 4, 4 * m + r % 4)
                y2u[row, z * 8 : z * 8 + 5] = put2[r // 4, 4 * m + r % 4]
                if r < 4:
                    y34[row, cells] = row3(r // 2, 2 * m + r % 2)
                    y34[256 + row, cells] = row3(r // 2, 2 * m + r % 2 - 8)
                elif r < 6:
                    y34[row, cells4] = row4(r - 4, m)
                    y34[256 + row, cells4] = row4(r - 4, m - 4)
    y34p = np.zeros((256, 80))
    for z in range(8):
        cells4 = slice(256 + z * 32, 256 + z * 32 + 32)
        for by in range(2):
            for i in range(4):
                y34[512 + z * 8 + by * 4 + i, cells4] = row4(by, i - 8)
                y34p[(i * 8 + z) * 8 + 4 + by, z * 8 + by * 4 + i] = 1.0
            y34[576 + z * 2 + by, cells4] = row4(by, -9)
            y34p[(3 * 8 + z) * 8 + 4 + by, 64 + z * 2 + by] = 1.0
    mats["y2"], mats["y2t"] = y2, y2.T
    mats["y2u"], mats["y2ut"] = y2u, y2u.T
    mats["y2q"], mats["y2qt"] = y2q, y2q.T
    mats["y34"], mats["y34t"] = y34, y34.T
    mats["y34p"], mats["y34pt"] = y34p, y34p.T

    eye8 = np.eye(8)
    z2 = np.kron(np.array([row2(b, i) for b in range(2) for i in range(16)]), eye8)
    z2q = padded(np.kron(pick32, eye8), 48, 256)
    z2u = padded(np.kron(put2.reshape(32, 5), eye8), 256, 48)
    z34 = np.zeros((288, 32, 8))
    z34p = np.zeros((128, 32))
    for b in range(2):
        for i in range(8):
            for r in range(4):
                z34[(b * 8 + i) * 8 + r, :, r] = row3(b, i)
                z34[128 + (b * 8 + i) * 8 + r, :, r] = row3(b, i - 8)
        for by in range(2):
            for i in range(4):
                slot = b * 4 + i
                z34[slot * 8 + 4 + by, :, 4 + by] = row4(b, i)
                z34[128 + slot * 8 + 4 + by, :, 4 + by] = row4(b, i - 4)
                z34[256 + slot * 2 + by, :, 4 + by] = row4(b, i - 8)
                z34p[slot * 8 + 4 + by, slot * 2 + by] = 1.0
            z34[272 + b * 2 + by, :, 4 + by] = row4(b, -9)
            z34p[(b * 4 + 3) * 8 + 4 + by, 16 + b * 2 + by] = 1.0
    z34 = z34.reshape(288, 256)
    mats["z2"], mats["z2t"] = z2, z2.T
    mats["z2q"], mats["z2qt"] = z2q, z2q.T
    mats["z2u"], mats["z2ut"] = z2u, z2u.T
    mats["z34"], mats["z34t"] = z34, z34.T
    mats["z34p"], mats["z34pt"] = z34p, z34p.T
    return mats


SPREAD, BASIS = rank_five()
Z1LO = band(low_taps, 16, 0)[5:]


def packed(shelves):
    mats = tables()
    places, rows, width = {}, 0, 0
    for shelf in shelves:
        col = tall = 0
        for name in shelf:
            height, wide = mats[name].shape
            places[name] = (rows, height, col, wide)
            col += -(-wide // 128) * 128
            tall = max(tall, -(-height // 16) * 16)
        rows, width = rows + tall, max(width, col)
    out = np.zeros((rows, width))
    for name, (row, height, col, wide) in places.items():
        out[row : row + height, col : col + wide] = mats[name]
    return pair(out), places


class Tables:
    def __init__(self, ref, places):
        self.ref, self.places = ref, places

    def __call__(self, name):
        row, height, col, wide = self.places[name]
        return [self.ref[k, row : row + height, col : col + wide] for k in range(2)]


SPREAD, BASIS = rank_five()
Z1LO = band(low_taps, 16, 0)[5:]


def halves(value):
    high = value.astype(BF16)
    return high, (value - high.astype(F32)).astype(BF16)


def dot(a, b):
    return lax.dot_general(a, b, (((1,), (0,)), ((), ())), preferred_element_type=F32)


def left(table, value):
    vh, vl = halves(value)
    return dot(table[0], vh) + dot(table[0], vl) + dot(table[1], vh)


def right(value, table):
    vh, vl = halves(value)
    return dot(vh, table[0]) + dot(vl, table[0]) + dot(vh, table[1])


def combine(weights, planes):
    total = None
    for weight, plane in zip(weights, planes):
        if weight == 0.0:
            continue
        term = float(weight) * plane()
        total = term if total is None else total + term
    return total


def taller(value, rows):
    return jnp.concatenate([value, jnp.zeros((rows, value.shape[1]), F32)], axis=0)


def call(kernel, micros, outs, *operands, shelves=None, index=None, scratch=()):
    spec = pl.BlockSpec(memory_space=pltpu.VMEM)
    specs = [spec] * len(operands)
    operands = list(operands)
    places = None
    if index is not None:
        operands.append(index)
        specs.append(pl.BlockSpec(memory_space=pltpu.SMEM))
    if shelves is not None:
        table, places = packed(shelves)
        operands.append(jnp.asarray(table))
        specs.append(spec)

    def body(*refs):
        refs = list(refs)
        count = len(operands)
        if places is not None:
            refs[count - 1] = Tables(refs[count - 1], places)
        kernel(*refs)

    return pl.pallas_call(
        body,
        name=kernel.__name__,
        out_shape=[jax.ShapeDtypeStruct(shape, F32) for shape in outs],
        in_specs=specs,
        out_specs=[spec] * len(outs),
        scratch_shapes=[pltpu.VMEM(shape, F32) for shape in scratch],
        cost_estimate=pl.CostEstimate(
            flops=int(micros * 1.1e9), transcendentals=0, bytes_accessed=int(micros * 3.6e6)
        ),
        compiler_params=pltpu.CompilerParams(vmem_limit_bytes=24 * 2**20),
    )(*operands)


def member(index, by):
    return lax.rem(index[0] + by + MEMBERS, MEMBERS)


def block(index, by, rows=64):
    return pl.ds(pl.multiple_of(member(index, by) * rows, rows), rows)


def x_split(v, t, f, q, b, qa, qc):
    for c in range(4):
        part = v[4 * c : 4 * c + 4].reshape(256, 512)
        f[4 * c : 4 * c + 4] = right(part, t("x1f")).reshape(4, 64, 512)
    for half in range(2):
        part = f[8 * half : 8 * half + 8].reshape(512, 512)
        q[half] = left(t("y1q"), part)[:40]
    for n in range(5):
        b[n] = combine(BASIS[n], [lambda j=j: f[j] for j in range(10)])
    rim = left(t("r5l"), b[:, :, :256].reshape(320, 256))
    qa[...] = rim[:160].reshape(5, 32, 256)
    qc[...] = rim[160:]


def rim_split(b, t, qb, qd):
    rim = left(t("r5l"), b[:, :, 256:].reshape(320, 256))
    qb[:, :, :256] = rim[:160].reshape(5, 32, 256)
    qd[...] = rim[160:]
    qb[:, :, 256:] = left(t("r5h"), b[...].reshape(320, 512)).reshape(5, 32, 512)


def deep_split(f, q, qa, qc, t, own, m1, m2, m3, g, low):
    for half in range(2):
        extra = left(t("y1ul"), taller(q[half, :, :256], 8))
        for c in range(2):
            z = 8 * half + 4 * c
            part = left(t("y1l"), f[z : z + 4, :, :256].reshape(256, 256))
            g[z : z + 4] = (part + extra[128 * c : 128 * c + 128]).reshape(4, 32, 256)
    rim = (qa[...].reshape(160, 256) + left(t("r5ul"), qc[...])).reshape(5, 32, 256)
    for i in range(8):
        plane = combine(Z1LO[i], [lambda j=j: g[j] for j in range(16)])
        if i >= 3:
            plane = plane + combine(SPREAD[i - 3], [lambda n=n: rim[n] for n in range(5)])
        low[i] = plane
    wide = right(low[...].reshape(256, 256), t("xmf"))
    rim = left(t("y2q"), wide[:, :256])
    m1[256:320] = rim[:, :128]
    m1[320:384] = rim[:, 128:]
    rest = left(t("y34"), jnp.concatenate([wide[:, 256:384], wide[:, 384:]], axis=0))
    own[:, 256:] = rest[:256]
    m1[:256] = rest[256:512]
    m2[...] = rest[512:576]
    m3[...] = rest[576:592]
    own[:, :256] = left(t("y2"), wide[:, :256])


def y_gather(own, m1, m2, m3, index, t, p0, p1, p2, p3, w):
    rim = jnp.concatenate([m1[256:320], m1[320:384]], axis=1)
    w[:, :256] = own[:, :256] + left(t("y2u"), rim)
    far = jnp.concatenate([m2[...], m3[...]], axis=0)
    w[:, 256:] = own[:, 256:] + m1[:256] + left(t("y34p"), far)
    for s, piece in enumerate((p0, p1, p2, p3)):
        piece[...] = w[block(index, s)]


def z_split(p0, p1, p2, p3, index, t, own2, own34, n1, n2, n3, w):
    for s, piece in enumerate((p0, p1, p2, p3)):
        w[block(index, -s)] = piece[...]
    rim = left(t("z2q"), w[:, :256])
    n1[128:168] = rim[:40, :128]
    n1[168:208] = rim[:40, 128:]
    rest = left(t("z34"), w[:, 256:])
    own34[...] = rest[:128]
    n1[:128] = rest[128:256]
    n2[...] = rest[256:272]
    n3[...] = rest[272:280]
    own2[...] = left(t("z2"), w[:, :256])


def mask_pack(two, three, four, coarse, index, k0, k1, k2, k3, full):
    def plain(ref, b, z):
        if b == 0:
            return jnp.zeros(ref.shape[2:], F32)
        return ref[b - 1, z].astype(F32)

    for bz in range(2):
        for z in range(4):
            for bx in range(2):
                rows = [plain(two, 4 * bz + 2 * by + bx, z) for by in range(2)]
                at = bx * 64 + (bz * 4 + z) * 8
                for m in range(4):
                    full[m, at : at + 8] = jnp.concatenate(
                        [part[4 * m : 4 * m + 4] for part in rows], axis=0
                    )
        for z in range(2):
            rows = [
                jnp.concatenate([plain(three, 4 * bz + 2 * by + bx, z) for bx in range(2)], axis=1)
                for by in range(2)
            ]
            at = 128 + (bz * 2 + z) * 8
            for m in range(4):
                parts = [part[2 * m : 2 * m + 2] for part in rows]
                full[m, at : at + 8] = jnp.concatenate(parts + [jnp.zeros((4, 128), F32)], axis=0)
        rows = []
        for by in range(2):
            parts = [
                coarse[0].astype(F32) if bz + by + bx == 0 else plain(four, 4 * bz + 2 * by + bx, 0)
                for bx in range(2)
            ]
            rows.append(jnp.concatenate(parts + [jnp.zeros((4, 64), F32)], axis=1))
        at = 160 + bz * 8
        for m in range(4):
            parts = [jnp.zeros((4, 128), F32)] + [part[m : m + 1] for part in rows]
            full[m, at : at + 8] = jnp.concatenate(parts + [jnp.zeros((2, 128), F32)], axis=0)
    for s, piece in enumerate((k0, k1, k2, k3)):
        piece[...] = full[member(index, s)]


def z_mask(own2, own34, n1, n2, n3, k0, k1, k2, k3, index, t, c2, c34, s1, s2, s3, full, keep2):
    for s, piece in enumerate((k0, k1, k2, k3)):
        full[member(index, -s)] = piece[...]
    for a in range(4):
        for bz in range(2):
            for bx in range(2):
                at = bz * 128 + a * 32
                rows = full[a, bx * 64 + bz * 32 : bx * 64 + bz * 32 + 32]
                keep2[at : at + 32, bx * 128 : bx * 128 + 128] = rows
    tiles = []
    for slot in range(16):
        bz, a, z = slot // 8, slot // 2 % 4, slot % 2
        tile = full[a, 128 + (bz * 2 + z) * 8 : 136 + (bz * 2 + z) * 8]
        if slot < 8:
            bz, a = slot // 4, slot % 4
            tile = tile + full[a, 160 + bz * 8 : 168 + bz * 8]
        tiles.append(tile)
    keep34 = jnp.concatenate(tiles, axis=0)

    far = taller(jnp.concatenate([n2[...], n3[...]], axis=0), 8)
    part34 = (own34[...] + n1[:128] + left(t("z34p"), far)) * keep34
    c34[...] = part34
    s1[:128] = part34
    back = left(t("z34pt"), part34)
    s2[...] = back[:16]
    s3[...] = back[16:24]
    rim = taller(jnp.concatenate([n1[128:168], n1[168:208]], axis=1), 8)
    part2 = (own2[...] + left(t("z2u"), rim)) * keep2[...]
    c2[...] = part2
    back = left(t("z2ut"), part2)
    s1[128:168] = back[:40, :128]
    s1[168:208] = back[:40, 128:]


def z_join(c2, c34, s1, s2, s3, index, t, p0, p1, p2, p3, w):
    rim = taller(jnp.concatenate([s1[128:168], s1[168:208]], axis=1), 8)
    w[:, :256] = left(t("z2t"), c2[...]) + left(t("z2qt"), rim)
    rows = jnp.concatenate([c34[...], s1[:128], s2[...], s3[...]], axis=0)
    w[:, 256:] = left(t("z34t"), taller(rows, 8))
    for s, piece in enumerate((p0, p1, p2, p3)):
        piece[...] = w[block(index, s)]


def y_send(p0, p1, p2, p3, index, t, w, m1, m2, m3):
    for s, piece in enumerate((p0, p1, p2, p3)):
        w[block(index, -s)] = piece[...]
    m1[:256] = w[:, 256:]
    rim = left(t("y2ut"), w[:, :256])
    m1[256:320] = rim[:, :128]
    m1[320:384] = rim[:, 128:]
    far = left(t("y34pt"), w[:, 256:])
    m2[...] = far[:64]
    m3[...] = far[64:]


def deep_join(w, m1, m2, m3, t, g, pz, py, pc, low):
    rim = jnp.concatenate([m1[256:320], m1[320:384]], axis=1)
    first = left(t("y2t"), w[:, :256]) + left(t("y2qt"), rim)
    rows = [w[:, 256:], m1[:256], m2[...], m3[...]]
    rest = left(t("y34t"), jnp.concatenate(rows, axis=0))
    wide = jnp.concatenate([first, rest[:256], rest[256:]], axis=1)
    low[...] = right(wide, t("xmi")).reshape(8, 32, 256)
    for n in range(5):
        pz[n] = combine(SPREAD[:5, n], [lambda i=i: low[i + 3] for i in range(5)])
    pc[...] = left(t("r5ult"), pz[...].reshape(160, 256))
    for z in range(16):
        g[z] = combine(Z1LO[:, z], [lambda i=i: low[i] for i in range(8)])
    for half in range(2):
        part = g[8 * half : 8 * half + 8].reshape(256, 256)
        py[half] = left(t("y1ult"), part)[:40]


def finish(base, g, pz, py, pc, t, out):
    far = left(t("r5z"), pc[...])
    for half in range(2):
        rim = taller(py[half], 8) + far[48 * half : 48 * half + 48]
        extra = left(t("y1qt"), rim)
        for c in range(2):
            z = 8 * half + 4 * c
            planes = []
            for k in range(z, z + 4):
                plane = g[k]
                if k < 10:
                    plane = plane + combine(BASIS[:, k], [lambda n=n: pz[n] for n in range(5)])
                planes.append(plane)
            part = left(t("y1lt"), jnp.concatenate(planes, axis=0))
            part = part + extra[256 * c : 256 * c + 256]
            out[z : z + 4] = base[z : z + 4] + right(part, t("x1l")).reshape(4, 64, 512)


def details(f, q, qa, qc, qb, qd, keep, t, g, pz, kept):
    for half in range(2):
        extra = left(t("y1u"), taller(q[half], 8))
        for c in range(2):
            z = 8 * half + 4 * c
            part = left(t("y1f"), f[z : z + 4].reshape(256, 512))
            g[z : z + 4] = (part + extra[256 * c : 256 * c + 256]).reshape(4, 64, 512)
    corner = left(t("r5u"), jnp.concatenate([qc[...], qd[...]], axis=1)).reshape(5, 64, 512)
    for c in range(4):
        rows = slice(16 * c, 16 * c + 16)
        if c < 2:
            rim = jnp.concatenate([qa[:, rows], qb[:, rows, :256]], axis=2)
        else:
            rim = qb[:, 16 * c - 32 : 16 * c - 16, 256:]
        rim = (rim + corner[:, rows]).reshape(80, 512)
        out = left(t("z1f"), g[:, rows].reshape(256, 512)) + left(t("z1u"), rim)
        out = out.reshape(16, 16, 512)
        by = c // 2
        at = slice(16 * (c % 2), 16 * (c % 2) + 16)
        for bz in range(2):
            for bx in range(2):
                cols = slice(256 * bx, 256 * bx + 256)
                number = 4 * bz + 2 * by + bx
                if number:
                    mask = keep[number - 1, :, at].astype(F32)
                    part = out[8 * bz : 8 * bz + 8, :, cols] * mask
                else:
                    part = jnp.zeros((8, 16, 256), F32)
                kept[8 * bz : 8 * bz + 8, rows, cols] = part
    for n in range(5):
        plane = combine(SPREAD[:5, n], [lambda i=i: kept[i + 3] for i in range(5)])
        pz[n] = plane + combine(SPREAD[5:, n], [lambda i=i: kept[i + 11] for i in range(5)])
    for c in range(4):
        rows = slice(16 * c, 16 * c + 16)
        out = left(t("z1i"), kept[:, rows].reshape(256, 512))
        g[:, rows] = out.reshape(16, 16, 512)


def details_rim(g, pz, t, py, pc):
    for half in range(2):
        part = g[8 * half : 8 * half + 8].reshape(512, 512)
        py[half] = left(t("y1ut"), part)[:40]
    pc[...] = left(t("r5ut"), pz[...].reshape(320, 512))


def details_join(g, pz, py, pc, t, out):
    far = left(t("r5z"), pc[...])
    for half in range(2):
        rim = taller(py[half], 8) + far[48 * half : 48 * half + 48]
        extra = left(t("y1qt"), rim)
        for c in range(2):
            z = 8 * half + 4 * c
            planes = []
            for k in range(z, z + 4):
                plane = g[k]
                if k < 10:
                    plane = plane + combine(BASIS[:, k], [lambda n=n: pz[n] for n in range(5)])
                planes.append(plane)
            part = left(t("y1i"), jnp.concatenate(planes, axis=0))
            part = part + extra[256 * c : 256 * c + 256]
            out[z : z + 4] = right(part, t("x1i")).reshape(4, 64, 512)


def moved(value, by_z, by_y):
    pairs = [
        (z * GY + y, (z + by_z) % GZ * GY + (y + by_y) % GY) for z in range(GZ) for y in range(GY)
    ]
    return lax.ppermute(value, ("gz", "gy"), pairs)


def exchanged(pieces):
    out = [pieces[0]]
    for s in range(1, MEMBERS):
        pairs = [(z, z // MEMBERS * MEMBERS + (z + s) % MEMBERS) for z in range(GZ)]
        out.append(lax.ppermute(pieces[s], "gz", pairs))
    return out


def on_device(vorticity, keep_one, keep_two, keep_three, keep_four, keep_coarse):
    index = lax.rem(lax.axis_index("gz"), MEMBERS).astype(jnp.int32).reshape(1)
    piece, half = (64, 384), (40, 512)

    f, q, b, qa, qc = call(
        x_split,
        3.0,
        [(16, 64, 512), (2, 40, 512), (5, 64, 512), (5, 32, 256), (40, 256)],
        vorticity,
        shelves=[["x1f"], ["y1q"], ["r5l"]],
    )
    q, qa, qc = moved(q, 0, -1), moved(qa, -1, 0), moved(qc, -1, -1)
    own, m1, m2, m3 = call(
        deep_split,
        3.0,
        [(256, 384), (384, 128), (64, 128), (16, 128)],
        f,
        q,
        qa,
        qc,
        shelves=[["y34"], ["xmf"], ["y2", "y1l"], ["y1ul", "r5ul", "y2q"]],
        scratch=[(16, 32, 256), (8, 32, 256)],
    )
    m1, m2, m3 = moved(m1, 0, -1), moved(m2, 0, -2), moved(m3, 0, -3)

    masks = call(
        mask_pack,
        1.0,
        [(176, 128)] * 4,
        keep_two,
        keep_three,
        keep_four,
        keep_coarse,
        index=index,
        scratch=[(4, 176, 128)],
    )
    masks = exchanged(masks)
    qb, qd = call(
        rim_split, 1.0, [(5, 32, 768), (40, 256)], b, shelves=[["r5l"], ["r5h"]]
    )
    qb, qd = moved(qb, -1, 0), moved(qd, -1, -1)

    pieces = call(
        y_gather,
        0.7,
        [piece] * 4,
        own,
        m1,
        m2,
        m3,
        index=index,
        shelves=[["y2u", "y34p"]],
        scratch=[(256, 384)],
    )
    pieces = exchanged(pieces)
    own2, own34, n1, n2, n3 = call(
        z_split,
        0.5,
        [(256, 256), (128, 128), (208, 128), (16, 128), (8, 128)],
        *pieces,
        index=index,
        shelves=[["z2", "z34"], ["z2q"]],
        scratch=[(256, 384)],
    )
    n1, n2, n3 = moved(n1, -4, 0), moved(n2, -8, 0), moved(n3, -12, 0)

    g, pz = call(
        details,
        8.0,
        [(16, 64, 512), (5, 64, 512)],
        f,
        q,
        qa,
        qc,
        qb,
        qd,
        keep_one,
        shelves=[["y1f", "z1f", "z1i", "z1u"], ["y1u", "r5u"]],
        scratch=[(16, 64, 512)],
    )
    py, pc = call(
        details_rim, 1.0, [(2, 40, 512), half], g, pz, shelves=[["y1ut"], ["r5ut"]]
    )
    pz, py, pc = moved(pz, 1, 0), moved(py, 0, 1), moved(pc, 1, 1)
    (base,) = call(
        details_join,
        6.0,
        [(16, 64, 512)],
        g,
        pz,
        py,
        pc,
        shelves=[["x1i"], ["y1qt", "y1i"], ["r5z"]],
    )

    c2, c34, s1, s2, s3 = call(
        z_mask,
        0.7,
        [(256, 256), (128, 128), (208, 128), (16, 128), (8, 128)],
        own2,
        own34,
        n1,
        n2,
        n3,
        *masks,
        index=index,
        shelves=[["z2u"], ["z34p", "z34pt", "z2ut"]],
        scratch=[(4, 176, 128), (256, 256)],
    )
    s1, s2, s3 = moved(s1, 4, 0), moved(s2, 8, 0), moved(s3, 12, 0)
    pieces = call(
        z_join,
        0.8,
        [piece] * 4,
        c2,
        c34,
        s1,
        s2,
        s3,
        index=index,
        shelves=[["z2t", "z34t", "z2qt"]],
        scratch=[(256, 384)],
    )
    pieces = exchanged(pieces)
    w, m1, m2, m3 = call(
        y_send,
        0.4,
        [(256, 384), (384, 128), (64, 128), (16, 128)],
        *pieces,
        index=index,
        shelves=[["y2ut"], ["y34pt"]],
    )
    m1, m2, m3 = moved(m1, 0, 1), moved(m2, 0, 2), moved(m3, 0, 3)
    g, pz, py, pc = call(
        deep_join,
        2.5,
        [(16, 32, 256), (5, 32, 256), (2, 40, 256), (40, 256)],
        w,
        m1,
        m2,
        m3,
        shelves=[["y34t"], ["xmi", "y2t"], ["y2qt", "y1ult", "r5ult"]],
        scratch=[(8, 32, 256)],
    )
    pz, py, pc = moved(pz, 1, 0), moved(py, 0, 1), moved(pc, 1, 1)
    (out,) = call(
        finish,
        3.0,
        [(16, 64, 512)],
        base,
        g,
        pz,
        py,
        pc,
        shelves=[["x1l"], ["y1qt", "y1lt"], ["r5z"]],
    )
    return out


def solution(mesh):
    in_specs = (
        P("gz", "gy", None),
        P(None, "gz", "gy", None),
        P(None, "gz", "gy", None),
        P(None, "gz", "gy", None),
        P(None, "gz", "gy", None),
        P("gz", "gy", None),
    )
    out_specs = P("gz", "gy", None)
    return jax.shard_map(
        on_device, mesh=mesh, in_specs=in_specs, out_specs=out_specs, check_vma=False
    )
```

```python
import functools

import jax
import jax.numpy as jnp
import ml_dtypes
import numpy as np
from jax import lax
from jax.experimental import pallas as pl
from jax.experimental.pallas import tpu as pltpu
from jax.sharding import PartitionSpec as P

low_taps = (
    0.11154074335008017,
    0.4946238903983854,
    0.7511339080215775,
    0.3152503517092432,
    -0.22626469396516913,
    -0.12976686756709563,
    0.09750160558707936,
    0.02752286553001629,
    -0.031582039318031156,
    0.0005538422009938016,
    0.004777257511010651,
    -0.00107730108499558,
)
high_taps = tuple(((-1.0) ** k * low_taps[11 - k] for k in range(12)))

GZ, GY = 32, 8
MEMBERS = 4
F32, BF16 = jnp.float32, jnp.bfloat16


def tail_of(s):
    return (s + 11) // 2


def band(taps, n, s):
    t = tail_of(s)
    out = np.zeros((t + n // 2, s + n))
    for row in range(t + n // 2):
        for col in range(s + n):
            k = (col - s) - 2 * (row - t)
            if 0 <= k < 12:
                out[row, col] = taps[k]
    return out


def periodic(taps, n):
    out = np.zeros((n // 2, n))
    for i in range(n // 2):
        for k in range(12):
            out[i, (2 * i + k) % n] += taps[k]
    return out


def rank_five():
    block = np.concatenate([band(low_taps, 10, 0)[:5], band(high_taps, 10, 0)[:5]])
    u, sing, vt = np.linalg.svd(block)
    return u[:, :5] * sing[:5], vt[:5]


def pair(matrix):
    high = matrix.astype(ml_dtypes.bfloat16)
    low = (matrix - high.astype(np.float64)).astype(ml_dtypes.bfloat16)
    return np.stack([high, low])


def padded(matrix, rows, cols):
    out = np.zeros((rows, cols))
    out[: matrix.shape[0], : matrix.shape[1]] = matrix
    return out


@functools.lru_cache(None)
def tables():
    spread, basis = rank_five()
    mats = {}
    x1 = np.concatenate([periodic(low_taps, 512), periodic(high_taps, 512)])
    mats["x1f"], mats["x1i"], mats["x1l"] = x1.T, x1, x1[:256]
    lo2 = periodic(low_taps, 256)
    lo3 = periodic(low_taps, 128) @ lo2
    xm = np.concatenate(
        [
            lo2,
            periodic(high_taps, 256),
            lo3,
            periodic(high_taps, 128) @ lo2,
            periodic(low_taps, 64) @ lo3,
            periodic(high_taps, 64) @ lo3,
            np.zeros((64, 256)),
        ]
    )
    mats["xmf"], mats["xmi"] = xm.T, xm
    y1 = np.concatenate([band(low_taps, 64, 0)[5:], band(high_taps, 64, 0)[5:]])
    mats["y1f"] = np.kron(np.eye(4), y1)
    mats["y1i"] = mats["y1f"].T
    pick = padded(basis, 5, 64)
    mats["y1q"] = padded(np.kron(np.eye(8), pick), 48, 512)
    mats["y1qt"] = mats["y1q"].T
    put = np.zeros((64, 5))
    put[27:32], put[59:64] = spread[:5], spread[5:]
    mats["y1u"] = padded(np.kron(np.eye(8), put), 512, 48)
    mats["y1ut"] = mats["y1u"].T
    mats["y1l"] = np.kron(np.eye(4), y1[:32])
    mats["y1lt"] = mats["y1l"].T
    mats["y1ul"] = padded(np.kron(np.eye(8), put[:32]), 256, 48)
    mats["y1ult"] = mats["y1ul"].T
    corner = np.kron(np.eye(5), padded(pick, 8, 64))
    lows, highs = np.kron(np.eye(5), y1[:32]), np.kron(np.eye(5), y1[32:])
    mats["r5f"] = np.concatenate([lows, corner, highs])
    mats["r5i"] = np.kron(np.eye(5), y1.T)
    mats["r5u"] = np.kron(np.eye(5), padded(put, 64, 8))
    mats["r5ut"] = mats["r5u"].T
    mats["r5ul"] = np.kron(np.eye(5), padded(put[:32], 32, 8))
    mats["r5ult"] = mats["r5ul"].T
    far = np.zeros((2, 48, 40))
    for z in range(10):
        for k in range(5):
            far[z // 8, (z % 8) * 5 + k, k::8] = basis[:, z]
    mats["r5z"] = far.reshape(96, 40)
    z1 = np.concatenate([band(low_taps, 16, 0)[5:], band(high_taps, 16, 0)[5:]])
    mats["z1f"] = np.kron(z1, np.eye(16))
    mats["z1i"] = mats["z1f"].T
    zput = np.zeros((16, 5))
    zput[3:8], zput[11:16] = spread[:5], spread[5:]
    mats["z1u"] = np.kron(zput, np.eye(16))
    zpick = padded(basis, 5, 16)
    mats["z1qt"] = np.kron(zpick.T, np.eye(16))
    lo_a = band(low_taps, 32, 0)
    lo_b = band(low_taps, 16, 5) @ lo_a
    lev2 = [lo_a, band(high_taps, 32, 0)]
    lev3 = [lo_b, band(high_taps, 16, 5) @ lo_a]
    lev4 = [band(low_taps, 8, 8) @ lo_b, band(high_taps, 8, 8) @ lo_b]

    def row2(b, i):
        return lev2[b][i + 5]

    def row3(b, i):
        return lev3[b][i + 8]

    def row4(b, i):
        return lev4[b][i + 9]

    pick32 = padded(basis, 5, 32)
    put2 = np.zeros((2, 16, 5))
    put2[0, 11:], put2[1, 11:] = spread[:5], spread[5:]

    y2 = np.zeros((256, 256))
    y2u = np.zeros((256, 64))
    y34 = np.zeros((592, 512))
    y2q = np.kron(np.eye(8), padded(pick32, 8, 32))
    for m in range(4):
        for z in range(8):
            cells = slice(z * 32, z * 32 + 32)
            cells4 = slice(256 + z * 32, 256 + z * 32 + 32)
            for r in range(8):
                row = (m * 8 + z) * 8 + r
                y2[row, cells] = row2(r // 4, 4 * m + r % 4)
                y2u[row, z * 8 : z * 8 + 5] = put2[r // 4, 4 * m + r % 4]
                if r < 4:
                    y34[row, cells] = row3(r // 2, 2 * m + r % 2)
                    y34[256 + row, cells] = row3(r // 2, 2 * m + r % 2 - 8)
                elif r < 6:
                    y34[row, cells4] = row4(r - 4, m)
                    y34[256 + row, cells4] = row4(r - 4, m - 4)
    y34p = np.zeros((256, 80))
    for z in range(8):
        cells4 = slice(256 + z * 32, 256 + z * 32 + 32)
        for by in range(2):
            for i in range(4):
                y34[512 + z * 8 + by * 4 + i, cells4] = row4(by, i - 8)
                y34p[(i * 8 + z) * 8 + 4 + by, z * 8 + by * 4 + i] = 1.0
            y34[576 + z * 2 + by, cells4] = row4(by, -9)
            y34p[(3 * 8 + z) * 8 + 4 + by, 64 + z * 2 + by] = 1.0
    mats["y2"], mats["y2t"] = y2, y2.T
    mats["y2u"], mats["y2ut"] = y2u, y2u.T
    mats["y2q"], mats["y2qt"] = y2q, y2q.T
    mats["y34"], mats["y34t"] = y34, y34.T
    mats["y34p"], mats["y34pt"] = y34p, y34p.T

    eye8 = np.eye(8)
    z2 = np.kron(np.array([row2(b, i) for b in range(2) for i in range(16)]), eye8)
    z2q = padded(np.kron(pick32, eye8), 48, 256)
    z2u = padded(np.kron(put2.reshape(32, 5), eye8), 256, 48)
    z34 = np.zeros((288, 32, 8))
    z34p = np.zeros((128, 32))
    for b in range(2):
        for i in range(8):
            for r in range(4):
                z34[(b * 8 + i) * 8 + r, :, r] = row3(b, i)
                z34[128 + (b * 8 + i) * 8 + r, :, r] = row3(b, i - 8)
        for by in range(2):
            for i in range(4):
                slot = b * 4 + i
                z34[slot * 8 + 4 + by, :, 4 + by] = row4(b, i)
                z34[128 + slot * 8 + 4 + by, :, 4 + by] = row4(b, i - 4)
                z34[256 + slot * 2 + by, :, 4 + by] = row4(b, i - 8)
                z34p[slot * 8 + 4 + by, slot * 2 + by] = 1.0
            z34[272 + b * 2 + by, :, 4 + by] = row4(b, -9)
            z34p[(b * 4 + 3) * 8 + 4 + by, 16 + b * 2 + by] = 1.0
    z34 = z34.reshape(288, 256)
    mats["z2"], mats["z2t"] = z2, z2.T
    mats["z2q"], mats["z2qt"] = z2q, z2q.T
    mats["z2u"], mats["z2ut"] = z2u, z2u.T
    mats["z34"], mats["z34t"] = z34, z34.T
    mats["z34p"], mats["z34pt"] = z34p, z34p.T
    return mats


SPREAD, BASIS = rank_five()
Z1LO = band(low_taps, 16, 0)[5:]


def packed(shelves):
    mats = tables()
    places, rows, width = {}, 0, 0
    for shelf in shelves:
        col = tall = 0
        for name in shelf:
            height, wide = mats[name].shape
            places[name] = (rows, height, col, wide)
            col += -(-wide // 128) * 128
            tall = max(tall, -(-height // 16) * 16)
        rows, width = rows + tall, max(width, col)
    out = np.zeros((rows, width))
    for name, (row, height, col, wide) in places.items():
        out[row : row + height, col : col + wide] = mats[name]
    return pair(out), places


class Tables:
    def __init__(self, ref, places):
        self.ref, self.places = ref, places

    def __call__(self, name):
        row, height, col, wide = self.places[name]
        return [self.ref[k, row : row + height, col : col + wide] for k in range(2)]


SPREAD, BASIS = rank_five()
Z1LO = band(low_taps, 16, 0)[5:]


def halves(value):
    high = value.astype(BF16)
    return high, (value - high.astype(F32)).astype(BF16)


def dot(a, b):
    return lax.dot_general(a, b, (((1,), (0,)), ((), ())), preferred_element_type=F32)


def left(table, value):
    vh, vl = halves(value)
    return dot(table[0], vh) + dot(table[0], vl) + dot(table[1], vh)


def right(value, table):
    vh, vl = halves(value)
    return dot(vh, table[0]) + dot(vl, table[0]) + dot(vh, table[1])


def combine(weights, planes):
    total = None
    for weight, plane in zip(weights, planes):
        if weight == 0.0:
            continue
        term = float(weight) * plane()
        total = term if total is None else total + term
    return total


def taller(value, rows):
    return jnp.concatenate([value, jnp.zeros((rows, value.shape[1]), F32)], axis=0)


def call(kernel, micros, outs, *operands, shelves=None, index=None, scratch=(), streamed=None):
    spec, anywhere = pl.BlockSpec(memory_space=pltpu.VMEM), pl.BlockSpec(memory_space=pltpu.HBM)
    specs = [spec] * len(operands)
    out_specs = [spec] * len(outs)
    operands = list(operands)
    places = None
    scratch = [pltpu.VMEM(shape, F32) for shape in scratch]
    if index is not None:
        operands.append(index)
        specs.append(pl.BlockSpec(memory_space=pltpu.SMEM))
    if shelves is not None:
        table, places = packed(shelves)
        operands.append(jnp.asarray(table))
        specs.append(spec)
    if streamed == "in":
        specs[0] = specs[-1] = anywhere
        for at in (0, -1):
            operands[at] = pltpu.with_memory_space_constraint(operands[at], pltpu.HBM)
        scratch += [
            pltpu.VMEM(operands[0].shape, F32),
            pltpu.VMEM(operands[-1].shape, BF16),
            pltpu.SemaphoreType.DMA((6,)),
        ]
    if streamed == "out":
        out_specs = [anywhere] * len(outs)
        scratch += [pltpu.VMEM(outs[0], F32), pltpu.SemaphoreType.DMA((4,))]

    def body(*refs):
        refs = list(refs)
        count = len(operands)
        if streamed == "in":
            held, table_held, sems = refs[-3:]
            table_copies = []
            for k, (low, high) in enumerate(((0, 512), (512, table_held.shape[1]))):
                rows = pl.ds(low, high - low)
                table_copies.append(
                    pltpu.make_async_copy(
                        refs[count - 1].at[:, rows], table_held.at[:, rows], sems.at[4 + k]
                    )
                )
            chunks = []
            for c in range(4):
                rows = pl.ds(4 * c, 4)
                chunks.append(pltpu.make_async_copy(refs[0].at[rows], held.at[rows], sems.at[c]))
            chunks[0].start()
            table_copies[0].start()
            for copy in chunks[1:]:
                copy.start()
            table_copies[1].start()
            table_copies[0].wait()
            refs[0], refs[count - 1] = held, table_held
            refs = refs[:-3] + [chunks + table_copies[1:]]
        if streamed == "out":
            held, sems = refs[-2:]
            target = refs[count]
            chunks = []
            for c in range(4):
                rows = pl.ds(4 * c, 4)
                chunks.append(pltpu.make_async_copy(held.at[rows], target.at[rows], sems.at[c]))
            refs[count] = held
            refs = refs[:-2] + [chunks]
        if places is not None:
            refs[count - 1] = Tables(refs[count - 1], places)
        kernel(*refs)

    return pl.pallas_call(
        body,
        name=kernel.__name__,
        out_shape=[jax.ShapeDtypeStruct(shape, F32) for shape in outs],
        in_specs=specs,
        out_specs=out_specs,
        scratch_shapes=scratch,
        cost_estimate=pl.CostEstimate(
            flops=int(micros * 1.1e9), transcendentals=0, bytes_accessed=int(micros * 3.6e6)
        ),
        compiler_params=pltpu.CompilerParams(vmem_limit_bytes=24 * 2**20),
    )(*operands)


def member(index, by):
    return lax.rem(index[0] + by + MEMBERS, MEMBERS)


def block(index, by, rows=64):
    return pl.ds(pl.multiple_of(member(index, by) * rows, rows), rows)


def x_split(v, t, f, q, qz, qc, b, chunks):
    for c in range(4):
        chunks[c].wait()
        part = v[4 * c : 4 * c + 4].reshape(256, 512)
        f[4 * c : 4 * c + 4] = right(part, t("x1f")).reshape(4, 64, 512)
    for n in range(5):
        b[n] = combine(BASIS[n], [lambda j=j: f[j] for j in range(10)])
    chunks[4].wait()
    rim = left(t("r5f"), b[...].reshape(320, 512))
    qz[:, :32] = rim[:160].reshape(5, 32, 512)
    qc[...] = rim[160:200]
    qz[:, 32:] = rim[200:].reshape(5, 32, 512)
    for half in range(2):
        part = f[8 * half : 8 * half + 8].reshape(512, 512)
        q[half] = left(t("y1q"), part)[:40]


def deep_split(f, q, qz, qc, t, own, m1, m2, m3, g, low):
    for half in range(2):
        extra = left(t("y1ul"), taller(q[half, :, :256], 8))
        for c in range(2):
            z = 8 * half + 4 * c
            part = left(t("y1l"), f[z : z + 4, :, :256].reshape(256, 256))
            g[z : z + 4] = (part + extra[128 * c : 128 * c + 128]).reshape(4, 32, 256)
    rim = qz[:, :32, :256].reshape(160, 256) + left(t("r5ul"), qc[:, :256])
    rim = rim.reshape(5, 32, 256)
    for i in range(8):
        plane = combine(Z1LO[i], [lambda j=j: g[j] for j in range(16)])
        if i >= 3:
            plane = plane + combine(SPREAD[i - 3], [lambda n=n: rim[n] for n in range(5)])
        low[i] = plane
    wide = right(low[...].reshape(256, 256), t("xmf"))
    rim = left(t("y2q"), wide[:, :256])
    m1[256:320] = rim[:, :128]
    m1[320:384] = rim[:, 128:]
    rest = left(t("y34"), jnp.concatenate([wide[:, 256:384], wide[:, 384:]], axis=0))
    own[:, 256:] = rest[:256]
    m1[:256] = rest[256:512]
    m2[...] = rest[512:576]
    m3[...] = rest[576:592]
    own[:, :256] = left(t("y2"), wide[:, :256])


def y_gather(own, m1, m2, m3, index, t, p0, p1, p2, p3, w):
    rim = jnp.concatenate([m1[256:320], m1[320:384]], axis=1)
    w[:, :256] = own[:, :256] + left(t("y2u"), rim)
    far = jnp.concatenate([m2[...], m3[...]], axis=0)
    w[:, 256:] = own[:, 256:] + m1[:256] + left(t("y34p"), far)
    for s, piece in enumerate((p0, p1, p2, p3)):
        piece[...] = w[block(index, s)]


def z_split(p0, p1, p2, p3, index, t, own2, own34, n1, n2, n3, w):
    for s, piece in enumerate((p0, p1, p2, p3)):
        w[block(index, -s)] = piece[...]
    rim = left(t("z2q"), w[:, :256])
    n1[128:168] = rim[:40, :128]
    n1[168:208] = rim[:40, 128:]
    rest = left(t("z34"), w[:, 256:])
    own34[...] = rest[:128]
    n1[:128] = rest[128:256]
    n2[...] = rest[256:272]
    n3[...] = rest[272:280]
    own2[...] = left(t("z2"), w[:, :256])


def mask_pack(two, three, four, coarse, index, k0, k2, near, full):
    def plain(ref, b, z):
        if b == 0:
            return jnp.zeros(ref.shape[2:], F32)
        return ref[b - 1, z].astype(F32)

    for bz in range(2):
        for z in range(4):
            for bx in range(2):
                rows = [plain(two, 4 * bz + 2 * by + bx, z) for by in range(2)]
                at = bx * 64 + (bz * 4 + z) * 8
                for m in range(4):
                    full[m, at : at + 8] = jnp.concatenate(
                        [part[4 * m : 4 * m + 4] for part in rows], axis=0
                    )
        for z in range(2):
            rows = [
                jnp.concatenate([plain(three, 4 * bz + 2 * by + bx, z) for bx in range(2)], axis=1)
                for by in range(2)
            ]
            at = 128 + (bz * 2 + z) * 8
            for m in range(4):
                parts = [part[2 * m : 2 * m + 2] for part in rows]
                full[m, at : at + 8] = jnp.concatenate(parts + [jnp.zeros((4, 128), F32)], axis=0)
        rows = []
        for by in range(2):
            parts = [
                coarse[0].astype(F32) if bz + by + bx == 0 else plain(four, 4 * bz + 2 * by + bx, 0)
                for bx in range(2)
            ]
            rows.append(jnp.concatenate(parts + [jnp.zeros((4, 64), F32)], axis=1))
        at = 160 + bz * 8
        for m in range(4):
            parts = [jnp.zeros((4, 128), F32)] + [part[m : m + 1] for part in rows]
            full[m, at : at + 8] = jnp.concatenate(parts + [jnp.zeros((2, 128), F32)], axis=0)
    k0[...] = full[index[0]]
    k2[...] = full[lax.bitwise_xor(index[0], 2)]
    for n in range(2):
        near[n] = full[lax.bitwise_xor(index[0], 2 * n + 1)]


def z_mask(own2, own34, n1, n2, n3, k0, near, away, index, t, c2, c34, s1, s2, s3, full, keep2):
    full[index[0]] = k0[...]
    full[lax.bitwise_xor(index[0], 1)] = near[0]
    for n in range(2):
        full[lax.bitwise_xor(index[0], 2 + n)] = away[n]
    for a in range(4):
        for bz in range(2):
            for bx in range(2):
                at = bz * 128 + a * 32
                rows = full[a, bx * 64 + bz * 32 : bx * 64 + bz * 32 + 32]
                keep2[at : at + 32, bx * 128 : bx * 128 + 128] = rows
    tiles = []
    for slot in range(16):
        bz, a, z = slot // 8, slot // 2 % 4, slot % 2
        tile = full[a, 128 + (bz * 2 + z) * 8 : 136 + (bz * 2 + z) * 8]
        if slot < 8:
            bz, a = slot // 4, slot % 4
            tile = tile + full[a, 160 + bz * 8 : 168 + bz * 8]
        tiles.append(tile)
    keep34 = jnp.concatenate(tiles, axis=0)

    far = taller(jnp.concatenate([n2[...], n3[...]], axis=0), 8)
    part34 = (own34[...] + n1[:128] + left(t("z34p"), far)) * keep34
    c34[...] = part34
    s1[:128] = part34
    back = left(t("z34pt"), part34)
    s2[...] = back[:16]
    s3[...] = back[16:24]
    rim = taller(jnp.concatenate([n1[128:168], n1[168:208]], axis=1), 8)
    part2 = (own2[...] + left(t("z2u"), rim)) * keep2[...]
    c2[...] = part2
    back = left(t("z2ut"), part2)
    s1[128:168] = back[:40, :128]
    s1[168:208] = back[:40, 128:]


def z_join(c2, c34, s1, s2, s3, index, t, p0, p1, p2, p3, w):
    rim = taller(jnp.concatenate([s1[128:168], s1[168:208]], axis=1), 8)
    w[:, :256] = left(t("z2t"), c2[...]) + left(t("z2qt"), rim)
    rows = jnp.concatenate([c34[...], s1[:128], s2[...], s3[...]], axis=0)
    w[:, 256:] = left(t("z34t"), taller(rows, 8))
    for s, piece in enumerate((p0, p1, p2, p3)):
        piece[...] = w[block(index, s)]


def y_send(p0, p1, p2, p3, index, t, w, m1, m2, m3):
    for s, piece in enumerate((p0, p1, p2, p3)):
        w[block(index, -s)] = piece[...]
    m1[:256] = w[:, 256:]
    rim = left(t("y2ut"), w[:, :256])
    m1[256:320] = rim[:, :128]
    m1[320:384] = rim[:, 128:]
    far = left(t("y34pt"), w[:, 256:])
    m2[...] = far[:64]
    m3[...] = far[64:]


def deep_join(w, m1, m2, m3, dz, dy, dc, t, g, pz, py, pc, low):
    rim = jnp.concatenate([m1[256:320], m1[320:384]], axis=1)
    first = left(t("y2t"), w[:, :256]) + left(t("y2qt"), rim)
    rows = [w[:, 256:], m1[:256], m2[...], m3[...]]
    rest = left(t("y34t"), jnp.concatenate(rows, axis=0))
    wide = jnp.concatenate([first, rest[:256], rest[256:]], axis=1)
    low[...] = right(wide, t("xmi")).reshape(8, 32, 256)
    planes = [
        combine(SPREAD[:5, n], [lambda i=i: low[i + 3] for i in range(5)]) for n in range(5)
    ]
    pz[...] = dz[...]
    for n in range(5):
        pz[n, :32, :256] = dz[n, :32, :256] + planes[n]
    corner = left(t("r5ult"), jnp.concatenate(planes, axis=0))
    pc[:, :256] = dc[:, :256] + corner
    pc[:, 256:] = dc[:, 256:]
    for z in range(16):
        g[z] = combine(Z1LO[:, z], [lambda i=i: low[i] for i in range(8)])
    for half in range(2):
        part = g[8 * half : 8 * half + 8].reshape(256, 256)
        py[half, :, :256] = dy[half, :, :256] + left(t("y1ult"), part)[:40]
        py[half, :, 256:] = dy[half, :, 256:]


def own_join(g, low, t, out):
    for c in range(4):
        planes = []
        for z in range(4 * c, 4 * c + 4):
            corner = g[z, :32, :256] + low[z]
            top = jnp.concatenate([corner, g[z, :32, 256:]], axis=1)
            planes += [top, g[z, 32:]]
        part = left(t("y1i"), jnp.concatenate(planes, axis=0))
        out[4 * c : 4 * c + 4] = right(part, t("x1i")).reshape(4, 64, 512)


def finish(base, pz, py, pc, t, out, rz, chunks):
    far = left(t("r5z"), pc[...])
    rims = [taller(py[half], 8) + far[48 * half : 48 * half + 48] for half in range(2)]
    rims = [left(t("r5i"), pz[...].reshape(320, 512))] + rims
    rims = right(jnp.concatenate(rims, axis=0), t("x1i"))
    rz[...] = rims[:320].reshape(5, 64, 512)
    for half in range(2):
        extra = left(t("y1qt"), rims[320 + 48 * half : 368 + 48 * half]).reshape(8, 64, 512)
        for k in range(8):
            z = 8 * half + k
            plane = base[z] + extra[k]
            if z < 10:
                plane = plane + combine(BASIS[:, z], [lambda n=n: rz[n] for n in range(5)])
            out[z] = plane
            if z % 4 == 3:
                chunks[z // 4].start()
    for copy in chunks:
        copy.wait()


def details(f, q, qz, qc, keep, t, g, pz, kept):
    for half in range(2):
        extra = left(t("y1u"), taller(q[half], 8))
        for c in range(2):
            z = 8 * half + 4 * c
            part = left(t("y1f"), f[z : z + 4].reshape(256, 512))
            g[z : z + 4] = (part + extra[256 * c : 256 * c + 256]).reshape(4, 64, 512)
    corner = left(t("r5u"), qc[...]).reshape(5, 64, 512)
    for c in range(4):
        rows = slice(16 * c, 16 * c + 16)
        rim = (qz[:, rows] + corner[:, rows]).reshape(80, 512)
        out = left(t("z1f"), g[:, rows].reshape(256, 512)) + left(t("z1u"), rim)
        out = out.reshape(16, 16, 512)
        by = c // 2
        at = slice(16 * (c % 2), 16 * (c % 2) + 16)
        for bz in range(2):
            for bx in range(2):
                cols = slice(256 * bx, 256 * bx + 256)
                number = 4 * bz + 2 * by + bx
                if number:
                    mask = keep[number - 1, :, at].astype(F32)
                    part = out[8 * bz : 8 * bz + 8, :, cols] * mask
                else:
                    part = jnp.zeros((8, 16, 256), F32)
                kept[8 * bz : 8 * bz + 8, rows, cols] = part
    for n in range(5):
        plane = combine(SPREAD[:5, n], [lambda i=i: kept[i + 3] for i in range(5)])
        pz[n] = plane + combine(SPREAD[5:, n], [lambda i=i: kept[i + 11] for i in range(5)])
    for c in range(4):
        rows = slice(16 * c, 16 * c + 16)
        out = left(t("z1i"), kept[:, rows].reshape(256, 512))
        g[:, rows] = out.reshape(16, 16, 512)


def details_rim(g, pz, t, py, pc):
    for half in range(2):
        part = g[8 * half : 8 * half + 8].reshape(512, 512)
        py[half] = left(t("y1ut"), part)[:40]
    pc[...] = left(t("r5ut"), pz[...].reshape(320, 512))


def moved(value, by_z, by_y):
    pairs = [
        (z * GY + y, (z + by_z) % GZ * GY + (y + by_y) % GY) for z in range(GZ) for y in range(GY)
    ]
    return lax.ppermute(value, ("gz", "gy"), pairs)


def across(value, flip):
    return lax.ppermute(value, "gz", [(z, z ^ flip) for z in range(GZ)])


def exchanged(pieces):
    out = [pieces[0]]
    for s in range(1, MEMBERS):
        pairs = [(z, z // MEMBERS * MEMBERS + (z + s) % MEMBERS) for z in range(GZ)]
        out.append(lax.ppermute(pieces[s], "gz", pairs))
    return out


def on_device(vorticity, keep_one, keep_two, keep_three, keep_four, keep_coarse):
    index = lax.rem(lax.axis_index("gz"), MEMBERS).astype(jnp.int32).reshape(1)
    piece, half = (64, 384), (40, 512)

    f, q, qz, qc = call(
        x_split,
        3.0,
        [(16, 64, 512), (2, 40, 512), (5, 64, 512), half],
        vorticity,
        shelves=[["x1f"], ["y1q"], ["r5f"]],
        scratch=[(5, 64, 512)],
        streamed="in",
    )
    q, qz, qc = moved(q, 0, -1), moved(qz, -1, 0), moved(qc, -1, -1)
    own, m1, m2, m3 = call(
        deep_split,
        3.0,
        [(256, 384), (384, 128), (64, 128), (16, 128)],
        f,
        q,
        qz,
        qc,
        shelves=[["y34"], ["xmf"], ["y2", "y1l"], ["y1ul", "r5ul", "y2q"]],
        scratch=[(16, 32, 256), (8, 32, 256)],
    )
    f, late, m1, m2, m3 = lax.optimization_barrier((f, index, m1, m2, m3))
    m1, m2, m3 = moved(m1, 0, -1), moved(m2, 0, -2), moved(m3, 0, -3)
    g, dz = call(
        details,
        0.5,
        [(16, 64, 512), (5, 64, 512)],
        f,
        q,
        qz,
        qc,
        keep_one,
        shelves=[["y1f", "z1f", "z1i", "z1u"], ["y1u", "r5u"]],
        scratch=[(16, 64, 512)],
    )
    k0, k2, near = call(
        mask_pack,
        0.1,
        [(176, 128), (176, 128), (2, 176, 128)],
        keep_two,
        keep_three,
        keep_four,
        keep_coarse,
        index=late,
        scratch=[(4, 176, 128)],
    )
    near = across(near, 1)
    own, g, near = lax.optimization_barrier((own, g, near))
    away = jnp.stack([k2, near[1]])

    pieces = call(
        y_gather,
        0.7,
        [piece] * 4,
        own,
        m1,
        m2,
        m3,
        index=index,
        shelves=[["y2u", "y34p"]],
        scratch=[(256, 384)],
    )
    pieces = exchanged(pieces)
    own2, own34, n1, n2, n3 = call(
        z_split,
        0.5,
        [(256, 256), (128, 128), (208, 128), (16, 128), (8, 128)],
        *pieces,
        index=index,
        shelves=[["z2", "z34"], ["z2q"]],
        scratch=[(256, 384)],
    )
    away, n1, n2, n3 = lax.optimization_barrier((away, n1, n2, n3))
    n1, n2, n3 = moved(n1, -4, 0), moved(n2, -8, 0), moved(n3, -12, 0)
    away = across(away, 2)

    c2, c34, s1, s2, s3 = call(
        z_mask,
        0.7,
        [(256, 256), (128, 128), (208, 128), (16, 128), (8, 128)],
        own2,
        own34,
        n1,
        n2,
        n3,
        k0,
        near,
        away,
        index=index,
        shelves=[["z2u"], ["z34p", "z34pt", "z2ut"]],
        scratch=[(4, 176, 128), (256, 256)],
    )
    g, s1, s2, s3 = lax.optimization_barrier((g, s1, s2, s3))
    s1, s2, s3 = moved(s1, 4, 0), moved(s2, 8, 0), moved(s3, 12, 0)
    dy, dc = call(
        details_rim, 0.3, [(2, 40, 512), half], g, dz, shelves=[["y1ut"], ["r5ut"]]
    )
    c2, dy = lax.optimization_barrier((c2, dy))
    pieces = call(
        z_join,
        0.8,
        [piece] * 4,
        c2,
        c34,
        s1,
        s2,
        s3,
        index=index,
        shelves=[["z2t", "z34t", "z2qt"]],
        scratch=[(256, 384)],
    )
    pieces = exchanged(pieces)
    w, m1, m2, m3 = call(
        y_send,
        0.4,
        [(256, 384), (384, 128), (64, 128), (16, 128)],
        *pieces,
        index=index,
        shelves=[["y2ut"], ["y34pt"]],
    )
    m1, m2, m3 = moved(m1, 0, 1), moved(m2, 0, 2), moved(m3, 0, 3)
    low, pz, py, pc = call(
        deep_join,
        2.5,
        [(16, 32, 256), (5, 64, 512), (2, 40, 512), half],
        w,
        m1,
        m2,
        m3,
        dz,
        dy,
        dc,
        shelves=[["y34t"], ["xmi", "y2t"], ["y2qt", "y1ult", "r5ult"]],
        scratch=[(8, 32, 256)],
    )
    pz, py, pc = moved(pz, 1, 0), moved(py, 0, 1), moved(pc, 1, 1)
    (base,) = call(
        own_join, 0.5, [(16, 64, 512)], g, low, shelves=[["x1i"], ["y1i"]]
    )
    (out,) = call(
        finish,
        3.0,
        [(16, 64, 512)],
        base,
        pz,
        py,
        pc,
        shelves=[["x1i"], ["y1qt", "r5i"], ["r5z"]],
        scratch=[(5, 64, 512)],
        streamed="out",
    )
    return out


def solution(mesh):
    in_specs = (
        P("gz", "gy", None),
        P(None, "gz", "gy", None),
        P(None, "gz", "gy", None),
        P(None, "gz", "gy", None),
        P(None, "gz", "gy", None),
        P("gz", "gy", None),
    )
    out_specs = P("gz", "gy", None)
    return jax.shard_map(
        on_device, mesh=mesh, in_specs=in_specs, out_specs=out_specs, check_vma=False
    )
```

```python
import functools

import jax
import jax.numpy as jnp
import ml_dtypes
import numpy as np
from jax import lax
from jax.experimental import pallas as pl
from jax.experimental.pallas import tpu as pltpu
from jax.sharding import PartitionSpec as P

low_taps = (
    0.11154074335008017,
    0.4946238903983854,
    0.7511339080215775,
    0.3152503517092432,
    -0.22626469396516913,
    -0.12976686756709563,
    0.09750160558707936,
    0.02752286553001629,
    -0.031582039318031156,
    0.0005538422009938016,
    0.004777257511010651,
    -0.00107730108499558,
)
high_taps = tuple(((-1.0) ** k * low_taps[11 - k] for k in range(12)))

GZ, GY = 32, 8
MEMBERS = 4
F32, BF16 = jnp.float32, jnp.bfloat16


def tail_of(s):
    return (s + 11) // 2


def band(taps, n, s):
    t = tail_of(s)
    out = np.zeros((t + n // 2, s + n))
    for row in range(t + n // 2):
        for col in range(s + n):
            k = (col - s) - 2 * (row - t)
            if 0 <= k < 12:
                out[row, col] = taps[k]
    return out


def periodic(taps, n):
    out = np.zeros((n // 2, n))
    for i in range(n // 2):
        for k in range(12):
            out[i, (2 * i + k) % n] += taps[k]
    return out


def rank_five():
    block = np.concatenate([band(low_taps, 10, 0)[:5], band(high_taps, 10, 0)[:5]])
    u, sing, vt = np.linalg.svd(block)
    return u[:, :5] * sing[:5], vt[:5]


def pair(matrix):
    high = matrix.astype(ml_dtypes.bfloat16)
    low = (matrix - high.astype(np.float64)).astype(ml_dtypes.bfloat16)
    return np.stack([high, low])


def padded(matrix, rows, cols):
    out = np.zeros((rows, cols))
    out[: matrix.shape[0], : matrix.shape[1]] = matrix
    return out


@functools.lru_cache(None)
def tables():
    spread, basis = rank_five()
    mats = {}
    x1 = np.concatenate([periodic(low_taps, 512), periodic(high_taps, 512)])
    mats["x1f"], mats["x1i"], mats["x1l"] = x1.T, x1, x1[:256]
    lo2 = periodic(low_taps, 256)
    lo3 = periodic(low_taps, 128) @ lo2
    xm = np.concatenate(
        [
            lo2,
            periodic(high_taps, 256),
            lo3,
            periodic(high_taps, 128) @ lo2,
            periodic(low_taps, 64) @ lo3,
            periodic(high_taps, 64) @ lo3,
            np.zeros((64, 256)),
        ]
    )
    mats["xmf"], mats["xmi"] = xm.T, xm
    y1 = np.concatenate([band(low_taps, 64, 0)[5:], band(high_taps, 64, 0)[5:]])
    mats["y1f"] = np.kron(np.eye(4), y1)
    mats["y1i"] = mats["y1f"].T
    pick = padded(basis, 5, 64)
    mats["y1q"] = padded(np.kron(np.eye(8), pick), 48, 512)
    mats["y1qt"] = mats["y1q"].T
    put = np.zeros((64, 5))
    put[27:32], put[59:64] = spread[:5], spread[5:]
    mats["y1u"] = padded(np.kron(np.eye(8), put), 512, 48)
    mats["y1ut"] = mats["y1u"].T
    mats["y1l"] = np.kron(np.eye(4), y1[:32])
    mats["y1lt"] = mats["y1l"].T
    mats["y1ul"] = padded(np.kron(np.eye(8), put[:32]), 256, 48)
    mats["y1ult"] = mats["y1ul"].T
    corner = np.kron(np.eye(5), padded(pick, 8, 64))
    lows, highs = np.kron(np.eye(5), y1[:32]), np.kron(np.eye(5), y1[32:])
    mats["r5f"] = np.concatenate([lows, corner, highs])
    mats["r5i"] = np.kron(np.eye(5), y1.T)
    mats["r5il"] = np.kron(np.eye(5), y1[:32].T)
    mats["y1r"] = np.kron(np.eye(16), padded(basis, 5, 16))
    mats["r5u"] = np.kron(np.eye(5), padded(put, 64, 8))
    mats["r5ut"] = mats["r5u"].T
    mats["r5ul"] = np.kron(np.eye(5), padded(put[:32], 32, 8))
    mats["r5ult"] = mats["r5ul"].T
    far = np.zeros((2, 48, 40))
    for z in range(10):
        for k in range(5):
            far[z // 8, (z % 8) * 5 + k, k::8] = basis[:, z]
    mats["r5z"] = far.reshape(96, 40)
    z1 = np.concatenate([band(low_taps, 16, 0)[5:], band(high_taps, 16, 0)[5:]])
    mats["z1f"] = np.kron(z1, np.eye(16))
    mats["z1i"] = mats["z1f"].T
    zput = np.zeros((16, 5))
    zput[3:8], zput[11:16] = spread[:5], spread[5:]
    mats["z1u"] = np.kron(zput, np.eye(16))
    zpick = padded(basis, 5, 16)
    mats["z1qt"] = np.kron(zpick.T, np.eye(16))
    lo_a = band(low_taps, 32, 0)
    lo_b = band(low_taps, 16, 5) @ lo_a
    lev2 = [lo_a, band(high_taps, 32, 0)]
    lev3 = [lo_b, band(high_taps, 16, 5) @ lo_a]
    lev4 = [band(low_taps, 8, 8) @ lo_b, band(high_taps, 8, 8) @ lo_b]

    def row2(b, i):
        return lev2[b][i + 5]

    def row3(b, i):
        return lev3[b][i + 8]

    def row4(b, i):
        return lev4[b][i + 9]

    pick32 = padded(basis, 5, 32)
    put2 = np.zeros((2, 16, 5))
    put2[0, 11:], put2[1, 11:] = spread[:5], spread[5:]

    y2 = np.zeros((256, 256))
    y2u = np.zeros((256, 64))
    y34 = np.zeros((592, 512))
    y2q = np.kron(np.eye(8), padded(pick32, 8, 32))
    for m in range(4):
        for z in range(8):
            cells = slice(z * 32, z * 32 + 32)
            cells4 = slice(256 + z * 32, 256 + z * 32 + 32)
            for r in range(8):
                row = (m * 8 + z) * 8 + r
                y2[row, cells] = row2(r // 4, 4 * m + r % 4)
                y2u[row, z * 8 : z * 8 + 5] = put2[r // 4, 4 * m + r % 4]
                if r < 4:
                    y34[row, cells] = row3(r // 2, 2 * m + r % 2)
                    y34[256 + row, cells] = row3(r // 2, 2 * m + r % 2 - 8)
                elif r < 6:
                    y34[row, cells4] = row4(r - 4, m)
                    y34[256 + row, cells4] = row4(r - 4, m - 4)
    y34p = np.zeros((256, 80))
    for z in range(8):
        cells4 = slice(256 + z * 32, 256 + z * 32 + 32)
        for by in range(2):
            for i in range(4):
                y34[512 + z * 8 + by * 4 + i, cells4] = row4(by, i - 8)
                y34p[(i * 8 + z) * 8 + 4 + by, z * 8 + by * 4 + i] = 1.0
            y34[576 + z * 2 + by, cells4] = row4(by, -9)
            y34p[(3 * 8 + z) * 8 + 4 + by, 64 + z * 2 + by] = 1.0
    mats["y2"], mats["y2t"] = y2, y2.T
    mats["y2u"], mats["y2ut"] = y2u, y2u.T
    mats["y2q"], mats["y2qt"] = y2q, y2q.T
    mats["y34"], mats["y34t"] = y34, y34.T
    mats["y34p"], mats["y34pt"] = y34p, y34p.T

    eye8 = np.eye(8)
    z2 = np.kron(np.array([row2(b, i) for b in range(2) for i in range(16)]), eye8)
    z2q = padded(np.kron(pick32, eye8), 48, 256)
    z2u = padded(np.kron(put2.reshape(32, 5), eye8), 256, 48)
    z34 = np.zeros((288, 32, 8))
    z34p = np.zeros((128, 32))
    for b in range(2):
        for i in range(8):
            for r in range(4):
                z34[(b * 8 + i) * 8 + r, :, r] = row3(b, i)
                z34[128 + (b * 8 + i) * 8 + r, :, r] = row3(b, i - 8)
        for by in range(2):
            for i in range(4):
                slot = b * 4 + i
                z34[slot * 8 + 4 + by, :, 4 + by] = row4(b, i)
                z34[128 + slot * 8 + 4 + by, :, 4 + by] = row4(b, i - 4)
                z34[256 + slot * 2 + by, :, 4 + by] = row4(b, i - 8)
                z34p[slot * 8 + 4 + by, slot * 2 + by] = 1.0
            z34[272 + b * 2 + by, :, 4 + by] = row4(b, -9)
            z34p[(b * 4 + 3) * 8 + 4 + by, 16 + b * 2 + by] = 1.0
    z34 = z34.reshape(288, 256)
    mats["z2"], mats["z2t"] = z2, z2.T
    mats["z2q"], mats["z2qt"] = z2q, z2q.T
    mats["z2u"], mats["z2ut"] = z2u, z2u.T
    mats["z34"], mats["z34t"] = z34, z34.T
    mats["z34p"], mats["z34pt"] = z34p, z34p.T
    return mats


SPREAD, BASIS = rank_five()
Z1LO = band(low_taps, 16, 0)[5:]


def packed(shelves):
    mats = tables()
    places, rows, width = {}, 0, 0
    for shelf in shelves:
        col = tall = 0
        for name in shelf:
            height, wide = mats[name].shape
            places[name] = (rows, height, col, wide)
            col += -(-wide // 128) * 128
            tall = max(tall, -(-height // 16) * 16)
        rows, width = rows + tall, max(width, col)
    out = np.zeros((rows, width))
    for name, (row, height, col, wide) in places.items():
        out[row : row + height, col : col + wide] = mats[name]
    return pair(out), places


class Tables:
    def __init__(self, ref, places):
        self.ref, self.places = ref, places

    def __call__(self, name):
        row, height, col, wide = self.places[name]
        return [self.ref[k, row : row + height, col : col + wide] for k in range(2)]


SPREAD, BASIS = rank_five()
Z1LO = band(low_taps, 16, 0)[5:]


def halves(value):
    high = value.astype(BF16)
    return high, (value - high.astype(F32)).astype(BF16)


def dot(a, b):
    return lax.dot_general(a, b, (((1,), (0,)), ((), ())), preferred_element_type=F32)


def left(table, value):
    vh, vl = halves(value)
    return dot(table[0], vh) + dot(table[0], vl) + dot(table[1], vh)


def right(value, table):
    vh, vl = halves(value)
    return dot(vh, table[0]) + dot(vl, table[0]) + dot(vh, table[1])


def combine(weights, planes):
    total = None
    for weight, plane in zip(weights, planes):
        if weight == 0.0:
            continue
        term = float(weight) * plane()
        total = term if total is None else total + term
    return total


def taller(value, rows):
    return jnp.concatenate([value, jnp.zeros((rows, value.shape[1]), F32)], axis=0)


def call(kernel, micros, outs, *operands, shelves=None, index=None, scratch=(), table=None, streamed=False):
    spec, far = pl.BlockSpec(memory_space=pltpu.VMEM), pl.BlockSpec(memory_space=pltpu.HBM)
    specs = [spec] * len(operands)
    out_specs = [spec] * len(outs)
    operands = list(operands)
    places = None
    scratch = [pltpu.VMEM(shape, F32) for shape in scratch]
    if index is not None:
        operands.append(index)
        specs.append(pl.BlockSpec(memory_space=pltpu.SMEM))
    if shelves is not None:
        packed_table, places = packed(shelves)
        operands.append(jnp.asarray(packed_table) if table is None else table)
        specs.append(spec)
    if streamed:
        out_specs = [far] * len(outs)
        scratch += [pltpu.VMEM(outs[0], F32), pltpu.SemaphoreType.DMA((4,))]

    def body(*refs):
        refs = list(refs)
        count = len(operands)
        if streamed:
            held, sems = refs[-2:]
            target = refs[count]
            chunks = []
            for c in range(4):
                rows = pl.ds(4 * c, 4)
                chunks.append(pltpu.make_async_copy(held.at[rows], target.at[rows], sems.at[c]))
            refs[count] = held
            refs = refs[:-2] + [chunks]
        if places is not None:
            refs[count - 1] = Tables(refs[count - 1], places)
        kernel(*refs)

    return pl.pallas_call(
        body,
        name=kernel.__name__,
        out_shape=[jax.ShapeDtypeStruct(shape, F32) for shape in outs],
        in_specs=specs,
        out_specs=out_specs,
        scratch_shapes=scratch,
        cost_estimate=pl.CostEstimate(
            flops=int(micros * 1.1e9), transcendentals=0, bytes_accessed=int(micros * 3.6e6)
        ),
        compiler_params=pltpu.CompilerParams(vmem_limit_bytes=24 * 2**20),
    )(*operands)


def member(index, by):
    return lax.rem(index[0] + by + MEMBERS, MEMBERS)


def block(index, by, rows=64):
    return pl.ds(pl.multiple_of(member(index, by) * rows, rows), rows)


DEEP = [["y34"], ["xmf"], ["y2", "y1l"], ["y1ul", "r5ul", "y2q"]]


def x_rims(vorticity):
    table, places = packed([["x1f"], ["r5f"], ["y1r"]])
    deep_table, _ = packed(DEEP)
    operands = [vorticity, jnp.asarray(table), jnp.asarray(deep_table)]
    operands = [pltpu.with_memory_space_constraint(part, pltpu.HBM) for part in operands]
    outs = [(2, 40, 512), (5, 32, 256), (5, 32, 768), (40, 512), (16, 64, 512)]

    def kernel(v, small, large, q, qa, qb, qc, held, deep, small_held, b, sems):
        chunks = []
        for c in range(4):
            rows = pl.ds(4 * c, 4)
            chunks.append(pltpu.make_async_copy(v.at[rows], held.at[rows], sems.at[c]))
        small_copy = pltpu.make_async_copy(small, small_held, sems.at[4])
        deep_copy = pltpu.make_async_copy(large, deep, sems.at[5])
        for copy in chunks[:3] + [small_copy, chunks[3], deep_copy]:
            copy.start()
        for copy in chunks[:3]:
            copy.wait()
        t = Tables(small_held, places)
        for n in range(5):
            b[n] = combine(BASIS[n], [lambda j=j: held[j] for j in range(10)])
        small_copy.wait()
        chunks[3].wait()
        rim = left(t("r5f"), b[...].reshape(320, 512))
        rows = left(t("y1r"), held[:, :16].reshape(256, 512))
        rim = right(jnp.concatenate([rim, rows], axis=0), t("x1f"))
        q[...] = rim[360:].reshape(2, 40, 512)
        qc[...] = rim[160:200]
        qa[...] = rim[:160, :256].reshape(5, 32, 256)
        qb[:, :, :256] = rim[:160, 256:].reshape(5, 32, 256)
        qb[:, :, 256:] = rim[200:360].reshape(5, 32, 512)
        deep_copy.wait()

    spec, far = pl.BlockSpec(memory_space=pltpu.VMEM), pl.BlockSpec(memory_space=pltpu.HBM)
    shapes = [jax.ShapeDtypeStruct(shape, F32) for shape in outs]
    shapes.append(jax.ShapeDtypeStruct(deep_table.shape, BF16))
    return pl.pallas_call(
        kernel,
        name="x_rims",
        out_shape=shapes,
        in_specs=[far] * 3,
        out_specs=[spec] * 6,
        scratch_shapes=[
            pltpu.VMEM(table.shape, BF16),
            pltpu.VMEM((5, 64, 512), F32),
            pltpu.SemaphoreType.DMA((6,)),
        ],
        cost_estimate=pl.CostEstimate(flops=3 * 10**9, transcendentals=0, bytes_accessed=10**7),
        compiler_params=pltpu.CompilerParams(vmem_limit_bytes=24 * 2**20),
    )(*operands)


def x_split(v, t, f):
    for c in range(4):
        part = v[4 * c : 4 * c + 4].reshape(256, 512)
        f[4 * c : 4 * c + 4] = right(part, t("x1f")).reshape(4, 64, 512)


def deep_split(f, q, qa, qc, t, own, m1, m2, m3, g, low):
    for half in range(2):
        extra = left(t("y1ul"), taller(q[half, :, :256], 8))
        for c in range(2):
            z = 8 * half + 4 * c
            part = left(t("y1l"), f[z : z + 4, :, :256].reshape(256, 256))
            g[z : z + 4] = (part + extra[128 * c : 128 * c + 128]).reshape(4, 32, 256)
    rim = qa[...].reshape(160, 256) + left(t("r5ul"), qc[:, :256])
    rim = rim.reshape(5, 32, 256)
    for i in range(8):
        plane = combine(Z1LO[i], [lambda j=j: g[j] for j in range(16)])
        if i >= 3:
            plane = plane + combine(SPREAD[i - 3], [lambda n=n: rim[n] for n in range(5)])
        low[i] = plane
    wide = right(low[...].reshape(256, 256), t("xmf"))
    rim = left(t("y2q"), wide[:, :256])
    m1[256:320] = rim[:, :128]
    m1[320:384] = rim[:, 128:]
    rest = left(t("y34"), jnp.concatenate([wide[:, 256:384], wide[:, 384:]], axis=0))
    own[:, 256:] = rest[:256]
    m1[:256] = rest[256:512]
    m2[...] = rest[512:576]
    m3[...] = rest[576:592]
    own[:, :256] = left(t("y2"), wide[:, :256])


def y_gather(own, m1, m2, m3, index, t, p0, p1, p2, p3, w):
    rim = jnp.concatenate([m1[256:320], m1[320:384]], axis=1)
    w[:, :256] = own[:, :256] + left(t("y2u"), rim)
    far = jnp.concatenate([m2[...], m3[...]], axis=0)
    w[:, 256:] = own[:, 256:] + m1[:256] + left(t("y34p"), far)
    for s, piece in enumerate((p0, p1, p2, p3)):
        piece[...] = w[block(index, s)]


def z_split(p0, p1, p2, p3, index, t, own2, own34, n1, n2, n3, w):
    for s, piece in enumerate((p0, p1, p2, p3)):
        w[block(index, -s)] = piece[...]
    rim = left(t("z2q"), w[:, :256])
    n1[128:168] = rim[:40, :128]
    n1[168:208] = rim[:40, 128:]
    rest = left(t("z34"), w[:, 256:])
    own34[...] = rest[:128]
    n1[:128] = rest[128:256]
    n2[...] = rest[256:272]
    n3[...] = rest[272:280]
    own2[...] = left(t("z2"), w[:, :256])


def mask_pack(two, three, four, coarse, index, k0, k2, near, full):
    def plain(ref, b, z):
        if b == 0:
            return jnp.zeros(ref.shape[2:], F32)
        return ref[b - 1, z].astype(F32)

    for bz in range(2):
        for z in range(4):
            for bx in range(2):
                rows = [plain(two, 4 * bz + 2 * by + bx, z) for by in range(2)]
                at = bx * 64 + (bz * 4 + z) * 8
                for m in range(4):
                    full[m, at : at + 8] = jnp.concatenate(
                        [part[4 * m : 4 * m + 4] for part in rows], axis=0
                    )
        for z in range(2):
            rows = [
                jnp.concatenate([plain(three, 4 * bz + 2 * by + bx, z) for bx in range(2)], axis=1)
                for by in range(2)
            ]
            at = 128 + (bz * 2 + z) * 8
            for m in range(4):
                parts = [part[2 * m : 2 * m + 2] for part in rows]
                full[m, at : at + 8] = jnp.concatenate(parts + [jnp.zeros((4, 128), F32)], axis=0)
        rows = []
        for by in range(2):
            parts = [
                coarse[0].astype(F32) if bz + by + bx == 0 else plain(four, 4 * bz + 2 * by + bx, 0)
                for bx in range(2)
            ]
            rows.append(jnp.concatenate(parts + [jnp.zeros((4, 64), F32)], axis=1))
        at = 160 + bz * 8
        for m in range(4):
            parts = [jnp.zeros((4, 128), F32)] + [part[m : m + 1] for part in rows]
            full[m, at : at + 8] = jnp.concatenate(parts + [jnp.zeros((2, 128), F32)], axis=0)
    k0[...] = full[index[0]]
    k2[...] = full[lax.bitwise_xor(index[0], 2)]
    for n in range(2):
        near[n] = full[lax.bitwise_xor(index[0], 2 * n + 1)]


def z_mask(own2, own34, n1, n2, n3, k0, near, away, index, t, c2, c34, s1, s2, s3, full, keep2):
    full[index[0]] = k0[...]
    full[lax.bitwise_xor(index[0], 1)] = near[0]
    for n in range(2):
        full[lax.bitwise_xor(index[0], 2 + n)] = away[n]
    for a in range(4):
        for bz in range(2):
            for bx in range(2):
                at = bz * 128 + a * 32
                rows = full[a, bx * 64 + bz * 32 : bx * 64 + bz * 32 + 32]
                keep2[at : at + 32, bx * 128 : bx * 128 + 128] = rows
    tiles = []
    for slot in range(16):
        bz, a, z = slot // 8, slot // 2 % 4, slot % 2
        tile = full[a, 128 + (bz * 2 + z) * 8 : 136 + (bz * 2 + z) * 8]
        if slot < 8:
            bz, a = slot // 4, slot % 4
            tile = tile + full[a, 160 + bz * 8 : 168 + bz * 8]
        tiles.append(tile)
    keep34 = jnp.concatenate(tiles, axis=0)

    far = taller(jnp.concatenate([n2[...], n3[...]], axis=0), 8)
    part34 = (own34[...] + n1[:128] + left(t("z34p"), far)) * keep34
    c34[...] = part34
    s1[:128] = part34
    back = left(t("z34pt"), part34)
    s2[...] = back[:16]
    s3[...] = back[16:24]
    rim = taller(jnp.concatenate([n1[128:168], n1[168:208]], axis=1), 8)
    part2 = (own2[...] + left(t("z2u"), rim)) * keep2[...]
    c2[...] = part2
    back = left(t("z2ut"), part2)
    s1[128:168] = back[:40, :128]
    s1[168:208] = back[:40, 128:]


def z_join(c2, c34, s1, s2, s3, index, t, p0, p1, p2, p3, w):
    rim = taller(jnp.concatenate([s1[128:168], s1[168:208]], axis=1), 8)
    w[:, :256] = left(t("z2t"), c2[...]) + left(t("z2qt"), rim)
    rows = jnp.concatenate([c34[...], s1[:128], s2[...], s3[...]], axis=0)
    w[:, 256:] = left(t("z34t"), taller(rows, 8))
    for s, piece in enumerate((p0, p1, p2, p3)):
        piece[...] = w[block(index, s)]


def y_send(p0, p1, p2, p3, index, t, w, m1, m2, m3):
    for s, piece in enumerate((p0, p1, p2, p3)):
        w[block(index, -s)] = piece[...]
    m1[:256] = w[:, 256:]
    rim = left(t("y2ut"), w[:, :256])
    m1[256:320] = rim[:, :128]
    m1[320:384] = rim[:, 128:]
    far = left(t("y34pt"), w[:, 256:])
    m2[...] = far[:64]
    m3[...] = far[64:]


def deep_join(w, m1, m2, m3, dz, dy, dc, t, g, pz, py, pc, low):
    rim = jnp.concatenate([m1[256:320], m1[320:384]], axis=1)
    first = left(t("y2t"), w[:, :256]) + left(t("y2qt"), rim)
    rows = [w[:, 256:], m1[:256], m2[...], m3[...]]
    rest = left(t("y34t"), jnp.concatenate(rows, axis=0))
    wide = jnp.concatenate([first, rest[:256], rest[256:]], axis=1)
    low[...] = right(wide, t("xmi")).reshape(8, 32, 256)
    planes = [
        combine(SPREAD[:5, n], [lambda i=i: low[i + 3] for i in range(5)]) for n in range(5)
    ]
    for z in range(16):
        g[z] = combine(Z1LO[:, z], [lambda i=i: low[i] for i in range(8)])
    planes = jnp.concatenate(planes, axis=0)
    rims = [left(t("r5il"), planes)]
    for half in range(2):
        part = g[8 * half : 8 * half + 8].reshape(256, 256)
        rims.append(left(t("y1ult"), part)[:40])
    rims.append(left(t("r5ult"), planes))
    rims = right(jnp.concatenate(rims, axis=0), t("x1l"))
    pz[...] = dz[...] + rims[:320].reshape(5, 64, 512)
    py[...] = dy[...] + rims[320:400].reshape(2, 40, 512)
    pc[...] = dc[...] + rims[400:]


def own_join(g, low, t, out):
    for c in range(4):
        planes = []
        for z in range(4 * c, 4 * c + 4):
            corner = g[z, :32, :256] + low[z]
            top = jnp.concatenate([corner, g[z, :32, 256:]], axis=1)
            planes += [top, g[z, 32:]]
        part = left(t("y1i"), jnp.concatenate(planes, axis=0))
        out[4 * c : 4 * c + 4] = right(part, t("x1i")).reshape(4, 64, 512)


def finish(base, pz, py, pc, t, out, chunks):
    far = left(t("r5z"), pc[...])
    for half in range(2):
        rim = taller(py[half], 8) + far[48 * half : 48 * half + 48]
        extra = left(t("y1qt"), rim).reshape(8, 64, 512)
        for k in range(8):
            z = 8 * half + k
            plane = base[z] + extra[k]
            if z < 10:
                plane = plane + combine(BASIS[:, z], [lambda n=n: pz[n] for n in range(5)])
            out[z] = plane
            if z % 4 == 3:
                chunks[z // 4].start()
    for copy in chunks:
        copy.wait()


def details(f, q, qa, qb, qc, keep, t, g, pz, kept):
    for half in range(2):
        extra = left(t("y1u"), taller(q[half], 8))
        for c in range(2):
            z = 8 * half + 4 * c
            part = left(t("y1f"), f[z : z + 4].reshape(256, 512))
            g[z : z + 4] = (part + extra[256 * c : 256 * c + 256]).reshape(4, 64, 512)
    top = jnp.concatenate([qa[...], qb[:, :, :256]], axis=2)
    planes = jnp.concatenate([top, qb[:, :, 256:]], axis=1)
    planes = planes + left(t("r5u"), qc[...]).reshape(5, 64, 512)
    for c in range(4):
        rows = slice(16 * c, 16 * c + 16)
        rim = planes[:, rows].reshape(80, 512)
        out = left(t("z1f"), g[:, rows].reshape(256, 512)) + left(t("z1u"), rim)
        out = out.reshape(16, 16, 512)
        by = c // 2
        at = slice(16 * (c % 2), 16 * (c % 2) + 16)
        for bz in range(2):
            for bx in range(2):
                cols = slice(256 * bx, 256 * bx + 256)
                number = 4 * bz + 2 * by + bx
                if number:
                    mask = keep[number - 1, :, at].astype(F32)
                    part = out[8 * bz : 8 * bz + 8, :, cols] * mask
                else:
                    part = jnp.zeros((8, 16, 256), F32)
                kept[8 * bz : 8 * bz + 8, rows, cols] = part
    for n in range(5):
        plane = combine(SPREAD[:5, n], [lambda i=i: kept[i + 3] for i in range(5)])
        pz[n] = plane + combine(SPREAD[5:, n], [lambda i=i: kept[i + 11] for i in range(5)])
    for c in range(4):
        rows = slice(16 * c, 16 * c + 16)
        out = left(t("z1i"), kept[:, rows].reshape(256, 512))
        g[:, rows] = out.reshape(16, 16, 512)


def details_rim(g, dz, t, pz, py, pc):
    planes = dz[...].reshape(320, 512)
    rims = [left(t("r5i"), planes)]
    for half in range(2):
        part = g[8 * half : 8 * half + 8].reshape(512, 512)
        rims.append(left(t("y1ut"), part)[:40])
    rims.append(left(t("r5ut"), planes))
    rims = right(jnp.concatenate(rims, axis=0), t("x1i"))
    pz[...] = rims[:320].reshape(5, 64, 512)
    py[...] = rims[320:400].reshape(2, 40, 512)
    pc[...] = rims[400:]


def moved(value, by_z, by_y):
    pairs = [
        (z * GY + y, (z + by_z) % GZ * GY + (y + by_y) % GY) for z in range(GZ) for y in range(GY)
    ]
    return lax.ppermute(value, ("gz", "gy"), pairs)


def across(value, flip):
    return lax.ppermute(value, "gz", [(z, z ^ flip) for z in range(GZ)])


def exchanged(pieces):
    out = [pieces[0]]
    for s in range(1, MEMBERS):
        pairs = [(z, z // MEMBERS * MEMBERS + (z + s) % MEMBERS) for z in range(GZ)]
        out.append(lax.ppermute(pieces[s], "gz", pairs))
    return out


def on_device(vorticity, keep_one, keep_two, keep_three, keep_four, keep_coarse):
    index = lax.rem(lax.axis_index("gz"), MEMBERS).astype(jnp.int32).reshape(1)
    piece, half = (64, 384), (40, 512)

    q, qa, qb, qc, held, deep = x_rims(vorticity)
    held, q, qa, qc = lax.optimization_barrier((held, q, qa, qc))
    q, qa, qc = moved(q, 0, -1), moved(qa, -1, 0), moved(qc, -1, -1)
    (f,) = call(x_split, 0.5, [(16, 64, 512)], held, shelves=[["x1f"]])
    own, m1, m2, m3 = call(
        deep_split,
        3.0,
        [(256, 384), (384, 128), (64, 128), (16, 128)],
        f,
        q,
        qa,
        qc,
        shelves=DEEP,
        table=deep,
        scratch=[(16, 32, 256), (8, 32, 256)],
    )
    late, m1, m2, m3 = lax.optimization_barrier((index, m1, m2, m3))
    m1, m2, m3 = moved(m1, 0, -1), moved(m2, 0, -2), moved(m3, 0, -3)
    k0, k2, near = call(
        mask_pack,
        0.1,
        [(176, 128), (176, 128), (2, 176, 128)],
        keep_two,
        keep_three,
        keep_four,
        keep_coarse,
        index=late,
        scratch=[(4, 176, 128)],
    )
    near = across(near, 1)
    own, near = lax.optimization_barrier((own, near))
    away = jnp.stack([k2, near[1]])

    pieces = call(
        y_gather,
        0.7,
        [piece] * 4,
        own,
        m1,
        m2,
        m3,
        index=index,
        shelves=[["y2u", "y34p"]],
        scratch=[(256, 384)],
    )
    pieces = exchanged(pieces)
    own2, own34, n1, n2, n3 = call(
        z_split,
        0.5,
        [(256, 256), (128, 128), (208, 128), (16, 128), (8, 128)],
        *pieces,
        index=index,
        shelves=[["z2", "z34"], ["z2q"]],
        scratch=[(256, 384)],
    )
    away, qb, n1, n2, n3 = lax.optimization_barrier((away, qb, n1, n2, n3))
    n1, n2, n3 = moved(n1, -4, 0), moved(n2, -8, 0), moved(n3, -12, 0)
    away = across(away, 2)
    qb = moved(qb, -1, 0)

    c2, c34, s1, s2, s3 = call(
        z_mask,
        0.7,
        [(256, 256), (128, 128), (208, 128), (16, 128), (8, 128)],
        own2,
        own34,
        n1,
        n2,
        n3,
        k0,
        near,
        away,
        index=index,
        shelves=[["z2u"], ["z34p", "z34pt", "z2ut"]],
        scratch=[(4, 176, 128), (256, 256)],
    )
    f, s1, s2, s3 = lax.optimization_barrier((f, s1, s2, s3))
    s1, s2, s3 = moved(s1, 4, 0), moved(s2, 8, 0), moved(s3, 12, 0)
    g, dz = call(
        details,
        0.5,
        [(16, 64, 512), (5, 64, 512)],
        f,
        q,
        qa,
        qb,
        qc,
        keep_one,
        shelves=[["y1f", "z1f", "z1i", "z1u"], ["y1u", "r5u"]],
        scratch=[(16, 64, 512)],
    )
    c2, g = lax.optimization_barrier((c2, g))
    pieces = call(
        z_join,
        0.8,
        [piece] * 4,
        c2,
        c34,
        s1,
        s2,
        s3,
        index=index,
        shelves=[["z2t", "z34t", "z2qt"]],
        scratch=[(256, 384)],
    )
    pieces = exchanged(pieces)
    w, m1, m2, m3 = call(
        y_send,
        0.4,
        [(256, 384), (384, 128), (64, 128), (16, 128)],
        *pieces,
        index=index,
        shelves=[["y2ut"], ["y34pt"]],
    )
    g, m1, m2, m3 = lax.optimization_barrier((g, m1, m2, m3))
    m1, m2, m3 = moved(m1, 0, 1), moved(m2, 0, 2), moved(m3, 0, 3)
    dz, dy, dc = call(
        details_rim,
        0.5,
        [(5, 64, 512), (2, 40, 512), half],
        g,
        dz,
        shelves=[["x1i"], ["r5i"], ["y1ut"], ["r5ut"]],
    )
    low, pz, py, pc = call(
        deep_join,
        2.5,
        [(16, 32, 256), (5, 64, 512), (2, 40, 512), half],
        w,
        m1,
        m2,
        m3,
        dz,
        dy,
        dc,
        shelves=[["y34t"], ["xmi", "y2t"], ["x1l", "y2qt"], ["y1ult", "r5ult"], ["r5il"]],
        scratch=[(8, 32, 256)],
    )
    pz, py, pc = moved(pz, 1, 0), moved(py, 0, 1), moved(pc, 1, 1)
    (base,) = call(
        own_join, 0.5, [(16, 64, 512)], g, low, shelves=[["x1i"], ["y1i"]]
    )
    (out,) = call(
        finish,
        2.0,
        [(16, 64, 512)],
        base,
        pz,
        py,
        pc,
        shelves=[["y1qt", "r5z"]],
        streamed=True,
    )
    return out


def solution(mesh):
    in_specs = (
        P("gz", "gy", None),
        P(None, "gz", "gy", None),
        P(None, "gz", "gy", None),
        P(None, "gz", "gy", None),
        P(None, "gz", "gy", None),
        P("gz", "gy", None),
    )
    out_specs = P("gz", "gy", None)
    return jax.shard_map(
        on_device, mesh=mesh, in_specs=in_specs, out_specs=out_specs, check_vma=False
    )
```

```python
import functools

import jax
import jax.numpy as jnp
import ml_dtypes
import numpy as np
from jax import lax
from jax.experimental import pallas as pl
from jax.experimental.pallas import tpu as pltpu
from jax.sharding import PartitionSpec as P

low_taps = (
    0.11154074335008017,
    0.4946238903983854,
    0.7511339080215775,
    0.3152503517092432,
    -0.22626469396516913,
    -0.12976686756709563,
    0.09750160558707936,
    0.02752286553001629,
    -0.031582039318031156,
    0.0005538422009938016,
    0.004777257511010651,
    -0.00107730108499558,
)
high_taps = tuple(((-1.0) ** k * low_taps[11 - k] for k in range(12)))

GZ, GY = 32, 8
MEMBERS = 4
F32, BF16 = jnp.float32, jnp.bfloat16


def tail_of(s):
    return (s + 11) // 2


def band(taps, n, s):
    t = tail_of(s)
    out = np.zeros((t + n // 2, s + n))
    for row in range(t + n // 2):
        for col in range(s + n):
            k = (col - s) - 2 * (row - t)
            if 0 <= k < 12:
                out[row, col] = taps[k]
    return out


def periodic(taps, n):
    out = np.zeros((n // 2, n))
    for i in range(n // 2):
        for k in range(12):
            out[i, (2 * i + k) % n] += taps[k]
    return out


def rank_five():
    block = np.concatenate([band(low_taps, 10, 0)[:5], band(high_taps, 10, 0)[:5]])
    u, sing, vt = np.linalg.svd(block)
    return u[:, :5] * sing[:5], vt[:5]


def pair(matrix):
    high = matrix.astype(ml_dtypes.bfloat16)
    low = (matrix - high.astype(np.float64)).astype(ml_dtypes.bfloat16)
    return np.stack([high, low])


def padded(matrix, rows, cols):
    out = np.zeros((rows, cols))
    out[: matrix.shape[0], : matrix.shape[1]] = matrix
    return out


@functools.lru_cache(None)
def tables():
    spread, basis = rank_five()
    mats = {}
    x1 = np.concatenate([periodic(low_taps, 512), periodic(high_taps, 512)])
    mats["x1f"], mats["x1i"], mats["x1l"] = x1.T, x1, x1[:256]
    lo2 = periodic(low_taps, 256)
    lo3 = periodic(low_taps, 128) @ lo2
    xm = np.concatenate(
        [
            lo2,
            periodic(high_taps, 256),
            lo3,
            periodic(high_taps, 128) @ lo2,
            periodic(low_taps, 64) @ lo3,
            periodic(high_taps, 64) @ lo3,
            np.zeros((64, 256)),
        ]
    )
    mats["xmf"], mats["xmi"] = xm.T, xm
    y1 = np.concatenate([band(low_taps, 64, 0)[5:], band(high_taps, 64, 0)[5:]])
    mats["y1f"] = np.kron(np.eye(4), y1)
    mats["y1i"] = mats["y1f"].T
    pick = padded(basis, 5, 64)
    mats["y1q"] = padded(np.kron(np.eye(8), pick), 48, 512)
    mats["y1qt"] = mats["y1q"].T
    put = np.zeros((64, 5))
    put[27:32], put[59:64] = spread[:5], spread[5:]
    mats["y1u"] = padded(np.kron(np.eye(8), put), 512, 48)
    mats["y1ut"] = mats["y1u"].T
    mats["y1l"] = np.kron(np.eye(4), y1[:32])
    mats["y1lt"] = mats["y1l"].T
    mats["y1ul"] = padded(np.kron(np.eye(8), put[:32]), 256, 48)
    mats["y1ult"] = mats["y1ul"].T
    corner = np.kron(np.eye(5), padded(pick, 8, 64))
    lows, highs = np.kron(np.eye(5), y1[:32]), np.kron(np.eye(5), y1[32:])
    mats["r5f"] = np.concatenate([lows, corner, highs])
    mats["r5i"] = np.kron(np.eye(5), y1.T)
    mats["r5il"] = np.kron(np.eye(5), y1[:32].T)
    mats["y1r"] = np.kron(np.eye(16), padded(basis, 5, 16))
    mats["r5u"] = np.kron(np.eye(5), padded(put, 64, 8))
    mats["r5ut"] = mats["r5u"].T
    mats["r5ul"] = np.kron(np.eye(5), padded(put[:32], 32, 8))
    mats["r5ult"] = mats["r5ul"].T
    far = np.zeros((2, 48, 40))
    for z in range(10):
        for k in range(5):
            far[z // 8, (z % 8) * 5 + k, k::8] = basis[:, z]
    mats["r5z"] = far.reshape(96, 40)
    z1 = np.concatenate([band(low_taps, 16, 0)[5:], band(high_taps, 16, 0)[5:]])
    mats["z1f"] = np.kron(z1, np.eye(16))
    mats["z1i"] = mats["z1f"].T
    zput = np.zeros((16, 5))
    zput[3:8], zput[11:16] = spread[:5], spread[5:]
    mats["z1u"] = np.kron(zput, np.eye(16))
    zpick = padded(basis, 5, 16)
    mats["z1qt"] = np.kron(zpick.T, np.eye(16))
    lo_a = band(low_taps, 32, 0)
    lo_b = band(low_taps, 16, 5) @ lo_a
    lev2 = [lo_a, band(high_taps, 32, 0)]
    lev3 = [lo_b, band(high_taps, 16, 5) @ lo_a]
    lev4 = [band(low_taps, 8, 8) @ lo_b, band(high_taps, 8, 8) @ lo_b]

    def row2(b, i):
        return lev2[b][i + 5]

    def row3(b, i):
        return lev3[b][i + 8]

    def row4(b, i):
        return lev4[b][i + 9]

    pick32 = padded(basis, 5, 32)
    put2 = np.zeros((2, 16, 5))
    put2[0, 11:], put2[1, 11:] = spread[:5], spread[5:]

    y2 = np.zeros((256, 256))
    y2u = np.zeros((256, 64))
    y34 = np.zeros((592, 512))
    y2q = np.kron(np.eye(8), padded(pick32, 8, 32))
    for m in range(4):
        for z in range(8):
            cells = slice(z * 32, z * 32 + 32)
            cells4 = slice(256 + z * 32, 256 + z * 32 + 32)
            for r in range(8):
                row = (m * 8 + z) * 8 + r
                y2[row, cells] = row2(r // 4, 4 * m + r % 4)
                y2u[row, z * 8 : z * 8 + 5] = put2[r // 4, 4 * m + r % 4]
                if r < 4:
                    y34[row, cells] = row3(r // 2, 2 * m + r % 2)
                    y34[256 + row, cells] = row3(r // 2, 2 * m + r % 2 - 8)
                elif r < 6:
                    y34[row, cells4] = row4(r - 4, m)
                    y34[256 + row, cells4] = row4(r - 4, m - 4)
    y34p = np.zeros((256, 80))
    for z in range(8):
        cells4 = slice(256 + z * 32, 256 + z * 32 + 32)
        for by in range(2):
            for i in range(4):
                y34[512 + z * 8 + by * 4 + i, cells4] = row4(by, i - 8)
                y34p[(i * 8 + z) * 8 + 4 + by, z * 8 + by * 4 + i] = 1.0
            y34[576 + z * 2 + by, cells4] = row4(by, -9)
            y34p[(3 * 8 + z) * 8 + 4 + by, 64 + z * 2 + by] = 1.0
    mats["y2"], mats["y2t"] = y2, y2.T
    mats["y2u"], mats["y2ut"] = y2u, y2u.T
    mats["y2q"], mats["y2qt"] = y2q, y2q.T
    mats["y34"], mats["y34t"] = y34, y34.T
    mats["y34p"], mats["y34pt"] = y34p, y34p.T

    eye8 = np.eye(8)
    z2 = np.kron(np.array([row2(b, i) for b in range(2) for i in range(16)]), eye8)
    z2q = padded(np.kron(pick32, eye8), 48, 256)
    z2u = padded(np.kron(put2.reshape(32, 5), eye8), 256, 48)
    z34 = np.zeros((288, 32, 8))
    z34p = np.zeros((128, 32))
    for b in range(2):
        for i in range(8):
            for r in range(4):
                z34[(b * 8 + i) * 8 + r, :, r] = row3(b, i)
                z34[128 + (b * 8 + i) * 8 + r, :, r] = row3(b, i - 8)
        for by in range(2):
            for i in range(4):
                slot = b * 4 + i
                z34[slot * 8 + 4 + by, :, 4 + by] = row4(b, i)
                z34[128 + slot * 8 + 4 + by, :, 4 + by] = row4(b, i - 4)
                z34[256 + slot * 2 + by, :, 4 + by] = row4(b, i - 8)
                z34p[slot * 8 + 4 + by, slot * 2 + by] = 1.0
            z34[272 + b * 2 + by, :, 4 + by] = row4(b, -9)
            z34p[(b * 4 + 3) * 8 + 4 + by, 16 + b * 2 + by] = 1.0
    z34 = z34.reshape(288, 256)
    mats["z2"], mats["z2t"] = z2, z2.T
    mats["z2q"], mats["z2qt"] = z2q, z2q.T
    mats["z2u"], mats["z2ut"] = z2u, z2u.T
    mats["z34"], mats["z34t"] = z34, z34.T
    mats["z34p"], mats["z34pt"] = z34p, z34p.T
    return mats


SPREAD, BASIS = rank_five()
Z1LO = band(low_taps, 16, 0)[5:]


def packed(shelves):
    mats = tables()
    places, rows, width = {}, 0, 0
    for shelf in shelves:
        col = tall = 0
        for name in shelf:
            height, wide = mats[name].shape
            places[name] = (rows, height, col, wide)
            col += -(-wide // 128) * 128
            tall = max(tall, -(-height // 16) * 16)
        rows, width = rows + tall, max(width, col)
    out = np.zeros((rows, width))
    for name, (row, height, col, wide) in places.items():
        out[row : row + height, col : col + wide] = mats[name]
    return pair(out), places


class Tables:
    def __init__(self, ref, places):
        self.ref, self.places = ref, places

    def __call__(self, name):
        row, height, col, wide = self.places[name]
        return [self.ref[k, row : row + height, col : col + wide] for k in range(2)]


SPREAD, BASIS = rank_five()
Z1LO = band(low_taps, 16, 0)[5:]


def halves(value):
    high = value.astype(BF16)
    return high, (value - high.astype(F32)).astype(BF16)


def dot(a, b):
    return lax.dot_general(a, b, (((1,), (0,)), ((), ())), preferred_element_type=F32)


def left(table, value):
    vh, vl = halves(value)
    return dot(table[0], vh) + dot(table[0], vl) + dot(table[1], vh)


def right(value, table):
    vh, vl = halves(value)
    return dot(vh, table[0]) + dot(vl, table[0]) + dot(vh, table[1])


def combine(weights, planes):
    total = None
    for weight, plane in zip(weights, planes):
        if weight == 0.0:
            continue
        term = float(weight) * plane()
        total = term if total is None else total + term
    return total


def taller(value, rows):
    return jnp.concatenate([value, jnp.zeros((rows, value.shape[1]), F32)], axis=0)


def call(kernel, micros, outs, *operands, shelves=None, index=None, scratch=(), table=None, streamed=False):
    spec, far = pl.BlockSpec(memory_space=pltpu.VMEM), pl.BlockSpec(memory_space=pltpu.HBM)
    specs = [spec] * len(operands)
    out_specs = [spec] * len(outs)
    operands = list(operands)
    places = None
    scratch = [pltpu.VMEM(shape, F32) for shape in scratch]
    if index is not None:
        operands.append(index)
        specs.append(pl.BlockSpec(memory_space=pltpu.SMEM))
    if shelves is not None:
        packed_table, places = packed(shelves)
        operands.append(jnp.asarray(packed_table) if table is None else table)
        specs.append(spec)
    if streamed:
        out_specs = [far] * len(outs)
        scratch += [pltpu.VMEM(outs[0], F32), pltpu.SemaphoreType.DMA((4,))]

    def body(*refs):
        refs = list(refs)
        count = len(operands)
        if streamed:
            held, sems = refs[-2:]
            target = refs[count]
            chunks = []
            for c in range(4):
                rows = pl.ds(4 * c, 4)
                chunks.append(pltpu.make_async_copy(held.at[rows], target.at[rows], sems.at[c]))
            refs[count] = held
            refs = refs[:-2] + [chunks]
        if places is not None:
            refs[count - 1] = Tables(refs[count - 1], places)
        kernel(*refs)

    return pl.pallas_call(
        body,
        name=kernel.__name__,
        out_shape=[jax.ShapeDtypeStruct(shape, F32) for shape in outs],
        in_specs=specs,
        out_specs=out_specs,
        scratch_shapes=scratch,
        cost_estimate=pl.CostEstimate(
            flops=int(micros * 1.1e9), transcendentals=0, bytes_accessed=int(micros * 3.6e6)
        ),
        compiler_params=pltpu.CompilerParams(vmem_limit_bytes=24 * 2**20),
    )(*operands)


def member(index, by):
    return lax.rem(index[0] + by + MEMBERS, MEMBERS)


def block(index, by, rows=64):
    return pl.ds(pl.multiple_of(member(index, by) * rows, rows), rows)


DEEP = [["y34"], ["xmf"], ["y2", "y1l"], ["y1ul", "r5ul", "y2q"]]


def from_far(kernel, name, micros, outs, operands, scratch):
    spec, far = pl.BlockSpec(memory_space=pltpu.VMEM), pl.BlockSpec(memory_space=pltpu.HBM)
    operands = [pltpu.with_memory_space_constraint(part, pltpu.HBM) for part in operands]
    return pl.pallas_call(
        kernel,
        name=name,
        out_shape=outs,
        in_specs=[far] * len(operands),
        out_specs=[spec] * len(outs),
        scratch_shapes=scratch,
        cost_estimate=pl.CostEstimate(
            flops=int(micros * 1.1e9), transcendentals=0, bytes_accessed=int(micros * 3.6e6)
        ),
        compiler_params=pltpu.CompilerParams(vmem_limit_bytes=24 * 2**20),
    )(*operands)


def planes_in(v, held, sems):
    chunks = []
    for c in range(4):
        rows = pl.ds(4 * c, 4)
        chunks.append(pltpu.make_async_copy(v.at[rows], held.at[rows], sems.at[c]))
    return chunks


def x_rims(vorticity):
    table, places = packed([["x1f"], ["r5f"], ["y1r"]])
    outs = [(2, 40, 512), (5, 32, 256), (5, 32, 768), (40, 512)]

    def kernel(v, small, q, qa, qb, qc, held, small_held, b, sems):
        chunks = planes_in(v, held, sems)
        small_copy = pltpu.make_async_copy(small, small_held, sems.at[4])
        for copy in chunks[:3] + [small_copy, chunks[3]]:
            copy.start()
        for copy in chunks[:3]:
            copy.wait()
        t = Tables(small_held, places)
        for n in range(5):
            b[n] = combine(BASIS[n], [lambda j=j: held[j] for j in range(10)])
        small_copy.wait()
        chunks[3].wait()
        rim = left(t("r5f"), b[...].reshape(320, 512))
        rows = left(t("y1r"), held[:, :16].reshape(256, 512))
        rim = right(jnp.concatenate([rim, rows], axis=0), t("x1f"))
        q[...] = rim[360:].reshape(2, 40, 512)
        qc[...] = rim[160:200]
        qa[...] = rim[:160, :256].reshape(5, 32, 256)
        qb[:, :, :256] = rim[:160, 256:].reshape(5, 32, 256)
        qb[:, :, 256:] = rim[200:360].reshape(5, 32, 512)

    return from_far(
        kernel,
        "x_rims",
        3.0,
        [jax.ShapeDtypeStruct(shape, F32) for shape in outs],
        [vorticity, jnp.asarray(table)],
        [
            pltpu.VMEM(vorticity.shape, F32),
            pltpu.VMEM(table.shape, BF16),
            pltpu.VMEM((5, 64, 512), F32),
            pltpu.SemaphoreType.DMA((5,)),
        ],
    )


def x_split(vorticity):
    table, places = packed([["x1f"]])
    deep_table, _ = packed(DEEP)

    def kernel(v, small, large, f, deep, held, small_held, sems):
        chunks = planes_in(v, held, sems)
        small_copy = pltpu.make_async_copy(small, small_held, sems.at[4])
        deep_copy = pltpu.make_async_copy(large, deep, sems.at[5])
        for copy in [small_copy] + chunks + [deep_copy]:
            copy.start()
        small_copy.wait()
        t = Tables(small_held, places)
        for c in range(4):
            chunks[c].wait()
            part = held[4 * c : 4 * c + 4].reshape(256, 512)
            f[4 * c : 4 * c + 4] = right(part, t("x1f")).reshape(4, 64, 512)
        deep_copy.wait()

    return from_far(
        kernel,
        "x_split",
        0.5,
        [
            jax.ShapeDtypeStruct(vorticity.shape, F32),
            jax.ShapeDtypeStruct(deep_table.shape, BF16),
        ],
        [vorticity, jnp.asarray(table), jnp.asarray(deep_table)],
        [
            pltpu.VMEM(vorticity.shape, F32),
            pltpu.VMEM(table.shape, BF16),
            pltpu.SemaphoreType.DMA((6,)),
        ],
    )


def deep_split(f, q, qa, qc, t, own, m1, m2, m3, g, low):
    for half in range(2):
        extra = left(t("y1ul"), taller(q[half, :, :256], 8))
        for c in range(2):
            z = 8 * half + 4 * c
            part = left(t("y1l"), f[z : z + 4, :, :256].reshape(256, 256))
            g[z : z + 4] = (part + extra[128 * c : 128 * c + 128]).reshape(4, 32, 256)
    rim = qa[...].reshape(160, 256) + left(t("r5ul"), qc[:, :256])
    rim = rim.reshape(5, 32, 256)
    for i in range(8):
        plane = combine(Z1LO[i], [lambda j=j: g[j] for j in range(16)])
        if i >= 3:
            plane = plane + combine(SPREAD[i - 3], [lambda n=n: rim[n] for n in range(5)])
        low[i] = plane
    wide = right(low[...].reshape(256, 256), t("xmf"))
    rim = left(t("y2q"), wide[:, :256])
    m1[256:320] = rim[:, :128]
    m1[320:384] = rim[:, 128:]
    rest = left(t("y34"), jnp.concatenate([wide[:, 256:384], wide[:, 384:]], axis=0))
    own[:, 256:] = rest[:256]
    m1[:256] = rest[256:512]
    m2[...] = rest[512:576]
    m3[...] = rest[576:592]
    own[:, :256] = left(t("y2"), wide[:, :256])


def y_gather(own, m1, m2, m3, index, t, p0, p1, p2, p3, w):
    rim = jnp.concatenate([m1[256:320], m1[320:384]], axis=1)
    w[:, :256] = own[:, :256] + left(t("y2u"), rim)
    far = jnp.concatenate([m2[...], m3[...]], axis=0)
    w[:, 256:] = own[:, 256:] + m1[:256] + left(t("y34p"), far)
    for s, piece in enumerate((p0, p1, p2, p3)):
        piece[...] = w[block(index, s)]


def z_split(p0, p1, p2, p3, index, t, own2, own34, n1, n2, n3, w):
    for s, piece in enumerate((p0, p1, p2, p3)):
        w[block(index, -s)] = piece[...]
    rim = left(t("z2q"), w[:, :256])
    n1[128:168] = rim[:40, :128]
    n1[168:208] = rim[:40, 128:]
    rest = left(t("z34"), w[:, 256:])
    own34[...] = rest[:128]
    n1[:128] = rest[128:256]
    n2[...] = rest[256:272]
    n3[...] = rest[272:280]
    own2[...] = left(t("z2"), w[:, :256])


def mask_pack(two, three, four, coarse, index, k0, k2, near, full):
    def plain(ref, b, z):
        if b == 0:
            return jnp.zeros(ref.shape[2:], F32)
        return ref[b - 1, z].astype(F32)

    for bz in range(2):
        for z in range(4):
            for bx in range(2):
                rows = [plain(two, 4 * bz + 2 * by + bx, z) for by in range(2)]
                at = bx * 64 + (bz * 4 + z) * 8
                for m in range(4):
                    full[m, at : at + 8] = jnp.concatenate(
                        [part[4 * m : 4 * m + 4] for part in rows], axis=0
                    )
        for z in range(2):
            rows = [
                jnp.concatenate([plain(three, 4 * bz + 2 * by + bx, z) for bx in range(2)], axis=1)
                for by in range(2)
            ]
            at = 128 + (bz * 2 + z) * 8
            for m in range(4):
                parts = [part[2 * m : 2 * m + 2] for part in rows]
                full[m, at : at + 8] = jnp.concatenate(parts + [jnp.zeros((4, 128), F32)], axis=0)
        rows = []
        for by in range(2):
            parts = [
                coarse[0].astype(F32) if bz + by + bx == 0 else plain(four, 4 * bz + 2 * by + bx, 0)
                for bx in range(2)
            ]
            rows.append(jnp.concatenate(parts + [jnp.zeros((4, 64), F32)], axis=1))
        at = 160 + bz * 8
        for m in range(4):
            parts = [jnp.zeros((4, 128), F32)] + [part[m : m + 1] for part in rows]
            full[m, at : at + 8] = jnp.concatenate(parts + [jnp.zeros((2, 128), F32)], axis=0)
    k0[...] = full[index[0]]
    k2[...] = full[lax.bitwise_xor(index[0], 2)]
    for n in range(2):
        near[n] = full[lax.bitwise_xor(index[0], 2 * n + 1)]


def z_mask(own2, own34, n1, n2, n3, k0, near, away, index, t, c2, c34, s1, s2, s3, full, keep2):
    full[index[0]] = k0[...]
    full[lax.bitwise_xor(index[0], 1)] = near[0]
    for n in range(2):
        full[lax.bitwise_xor(index[0], 2 + n)] = away[n]
    for a in range(4):
        for bz in range(2):
            for bx in range(2):
                at = bz * 128 + a * 32
                rows = full[a, bx * 64 + bz * 32 : bx * 64 + bz * 32 + 32]
                keep2[at : at + 32, bx * 128 : bx * 128 + 128] = rows
    tiles = []
    for slot in range(16):
        bz, a, z = slot // 8, slot // 2 % 4, slot % 2
        tile = full[a, 128 + (bz * 2 + z) * 8 : 136 + (bz * 2 + z) * 8]
        if slot < 8:
            bz, a = slot // 4, slot % 4
            tile = tile + full[a, 160 + bz * 8 : 168 + bz * 8]
        tiles.append(tile)
    keep34 = jnp.concatenate(tiles, axis=0)

    far = taller(jnp.concatenate([n2[...], n3[...]], axis=0), 8)
    part34 = (own34[...] + n1[:128] + left(t("z34p"), far)) * keep34
    c34[...] = part34
    s1[:128] = part34
    back = left(t("z34pt"), part34)
    s2[...] = back[:16]
    s3[...] = back[16:24]
    rim = taller(jnp.concatenate([n1[128:168], n1[168:208]], axis=1), 8)
    part2 = (own2[...] + left(t("z2u"), rim)) * keep2[...]
    c2[...] = part2
    back = left(t("z2ut"), part2)
    s1[128:168] = back[:40, :128]
    s1[168:208] = back[:40, 128:]


def z_join(c2, c34, s1, s2, s3, index, t, p0, p1, p2, p3, w):
    rim = taller(jnp.concatenate([s1[128:168], s1[168:208]], axis=1), 8)
    w[:, :256] = left(t("z2t"), c2[...]) + left(t("z2qt"), rim)
    rows = jnp.concatenate([c34[...], s1[:128], s2[...], s3[...]], axis=0)
    w[:, 256:] = left(t("z34t"), taller(rows, 8))
    for s, piece in enumerate((p0, p1, p2, p3)):
        piece[...] = w[block(index, s)]


def y_send(p0, p1, p2, p3, index, t, w, m1, m2, m3):
    for s, piece in enumerate((p0, p1, p2, p3)):
        w[block(index, -s)] = piece[...]
    m1[:256] = w[:, 256:]
    rim = left(t("y2ut"), w[:, :256])
    m1[256:320] = rim[:, :128]
    m1[320:384] = rim[:, 128:]
    far = left(t("y34pt"), w[:, 256:])
    m2[...] = far[:64]
    m3[...] = far[64:]


def deep_join(w, m1, m2, m3, da, dy, dc, t, g, pa, py, pc, low):
    rim = jnp.concatenate([m1[256:320], m1[320:384]], axis=1)
    first = left(t("y2t"), w[:, :256]) + left(t("y2qt"), rim)
    rows = [w[:, 256:], m1[:256], m2[...], m3[...]]
    rest = left(t("y34t"), jnp.concatenate(rows, axis=0))
    wide = jnp.concatenate([first, rest[:256], rest[256:]], axis=1)
    low[...] = right(wide, t("xmi")).reshape(8, 32, 256)
    planes = [
        combine(SPREAD[:5, n], [lambda i=i: low[i + 3] for i in range(5)]) for n in range(5)
    ]
    for z in range(16):
        g[z] = combine(Z1LO[:, z], [lambda i=i: low[i] for i in range(8)])
    for n in range(5):
        pa[n] = da[n] + planes[n]
    corner = left(t("r5ult"), jnp.concatenate(planes, axis=0))
    pc[:, :256] = dc[:, :256] + corner
    pc[:, 256:] = dc[:, 256:]
    for half in range(2):
        part = g[8 * half : 8 * half + 8].reshape(256, 256)
        py[half, :, :256] = dy[half, :, :256] + left(t("y1ult"), part)[:40]
        py[half, :, 256:] = dy[half, :, 256:]


def own_join(g, low, pb, t, out):
    for c in range(4):
        planes = []
        for z in range(4 * c, 4 * c + 4):
            rest = [g[z, :32, 256:], g[z, 32:]]
            if z < 10:
                rim = combine(BASIS[:, z], [lambda n=n: pb[n] for n in range(5)])
                rest = [rest[0] + rim[:, :256], rest[1] + rim[:, 256:]]
            corner = g[z, :32, :256] + low[z]
            planes += [jnp.concatenate([corner, rest[0]], axis=1), rest[1]]
        part = left(t("y1i"), jnp.concatenate(planes, axis=0))
        out[4 * c : 4 * c + 4] = right(part, t("x1i")).reshape(4, 64, 512)


def finish(base, pa, py, pc, t, out, rz, chunks):
    x1l = [part[:256] for part in t("x1i")]
    rz[...] = right(left(t("r5il"), pa[...].reshape(160, 256)), x1l).reshape(5, 64, 512)
    far = left(t("r5z"), pc[...])
    rims = [taller(py[half], 8) + far[48 * half : 48 * half + 48] for half in range(2)]
    rims = right(jnp.concatenate(rims, axis=0), t("x1i"))
    for half in range(2):
        extra = left(t("y1qt"), rims[48 * half : 48 * half + 48]).reshape(8, 64, 512)
        for k in range(8):
            z = 8 * half + k
            plane = base[z] + extra[k]
            if z < 10:
                plane = plane + combine(BASIS[:, z], [lambda n=n: rz[n] for n in range(5)])
            out[z] = plane
            if z % 4 == 3:
                chunks[z // 4].start()
    for copy in chunks:
        copy.wait()


def details(f, q, qa, qb, qc, keep, t, g, da, db, kept):
    for half in range(2):
        extra = left(t("y1u"), taller(q[half], 8))
        for c in range(2):
            z = 8 * half + 4 * c
            part = left(t("y1f"), f[z : z + 4].reshape(256, 512))
            g[z : z + 4] = (part + extra[256 * c : 256 * c + 256]).reshape(4, 64, 512)
    top = jnp.concatenate([qa[...], qb[:, :, :256]], axis=2)
    planes = jnp.concatenate([top, qb[:, :, 256:]], axis=1)
    planes = planes + left(t("r5u"), qc[...]).reshape(5, 64, 512)
    for c in range(4):
        rows = slice(16 * c, 16 * c + 16)
        rim = planes[:, rows].reshape(80, 512)
        out = left(t("z1f"), g[:, rows].reshape(256, 512)) + left(t("z1u"), rim)
        out = out.reshape(16, 16, 512)
        by = c // 2
        at = slice(16 * (c % 2), 16 * (c % 2) + 16)
        for bz in range(2):
            for bx in range(2):
                cols = slice(256 * bx, 256 * bx + 256)
                number = 4 * bz + 2 * by + bx
                if number:
                    mask = keep[number - 1, :, at].astype(F32)
                    part = out[8 * bz : 8 * bz + 8, :, cols] * mask
                else:
                    part = jnp.zeros((8, 16, 256), F32)
                kept[8 * bz : 8 * bz + 8, rows, cols] = part
    for n in range(5):
        plane = combine(SPREAD[:5, n], [lambda i=i: kept[i + 3] for i in range(5)])
        plane = plane + combine(SPREAD[5:, n], [lambda i=i: kept[i + 11] for i in range(5)])
        da[n] = plane[:32, :256]
        db[n, :, :256] = plane[:32, 256:]
        db[n, :, 256:] = plane[32:]
    for c in range(4):
        rows = slice(16 * c, 16 * c + 16)
        out = left(t("z1i"), kept[:, rows].reshape(256, 512))
        g[:, rows] = out.reshape(16, 16, 512)


def details_rim(g, da, db, t, py, pc):
    top = jnp.concatenate([da[...], db[:, :, :256]], axis=2)
    planes = jnp.concatenate([top, db[:, :, 256:]], axis=1)
    pc[...] = left(t("r5ut"), planes.reshape(320, 512))
    for half in range(2):
        part = g[8 * half : 8 * half + 8].reshape(512, 512)
        py[half] = left(t("y1ut"), part)[:40]


def moved(value, by_z, by_y):
    pairs = [
        (z * GY + y, (z + by_z) % GZ * GY + (y + by_y) % GY) for z in range(GZ) for y in range(GY)
    ]
    return lax.ppermute(value, ("gz", "gy"), pairs)


def across(value, flip):
    return lax.ppermute(value, "gz", [(z, z ^ flip) for z in range(GZ)])


def exchanged(pieces):
    out = [pieces[0]]
    for s in range(1, MEMBERS):
        pairs = [(z, z // MEMBERS * MEMBERS + (z + s) % MEMBERS) for z in range(GZ)]
        out.append(lax.ppermute(pieces[s], "gz", pairs))
    return out


def on_device(vorticity, keep_one, keep_two, keep_three, keep_four, keep_coarse):
    index = lax.rem(lax.axis_index("gz"), MEMBERS).astype(jnp.int32).reshape(1)
    piece, half = (64, 384), (40, 512)

    q, qa, qb, qc = x_rims(vorticity)
    vorticity, q, qa, qb, qc = lax.optimization_barrier((vorticity, q, qa, qb, qc))
    q, qa, qc = moved(q, 0, -1), moved(qa, -1, 0), moved(qc, -1, -1)
    qb = moved(qb, -1, 0)
    f, deep = x_split(vorticity)
    own, m1, m2, m3 = call(
        deep_split,
        3.0,
        [(256, 384), (384, 128), (64, 128), (16, 128)],
        f,
        q,
        qa,
        qc,
        shelves=DEEP,
        table=deep,
        scratch=[(16, 32, 256), (8, 32, 256)],
    )
    f, late, m1, m2, m3 = lax.optimization_barrier((f, index, m1, m2, m3))
    m1, m2, m3 = moved(m1, 0, -1), moved(m2, 0, -2), moved(m3, 0, -3)
    g, da, db = call(
        details,
        0.5,
        [(16, 64, 512), (5, 32, 256), (5, 32, 768)],
        f,
        q,
        qa,
        qb,
        qc,
        keep_one,
        shelves=[["y1f", "z1f", "z1i", "z1u"], ["y1u", "r5u"]],
        scratch=[(16, 64, 512)],
    )
    k0, k2, near = call(
        mask_pack,
        0.1,
        [(176, 128), (176, 128), (2, 176, 128)],
        keep_two,
        keep_three,
        keep_four,
        keep_coarse,
        index=late,
        scratch=[(4, 176, 128)],
    )
    near = across(near, 1)
    own, g, near = lax.optimization_barrier((own, g, near))
    away = jnp.stack([k2, near[1]])

    pieces = call(
        y_gather,
        0.7,
        [piece] * 4,
        own,
        m1,
        m2,
        m3,
        index=index,
        shelves=[["y2u", "y34p"]],
        scratch=[(256, 384)],
    )
    pieces = exchanged(pieces)
    own2, own34, n1, n2, n3 = call(
        z_split,
        0.5,
        [(256, 256), (128, 128), (208, 128), (16, 128), (8, 128)],
        *pieces,
        index=index,
        shelves=[["z2", "z34"], ["z2q"]],
        scratch=[(256, 384)],
    )
    away, n1, n2, n3 = lax.optimization_barrier((away, n1, n2, n3))
    n1, n2, n3 = moved(n1, -4, 0), moved(n2, -8, 0), moved(n3, -12, 0)
    away = across(away, 2)

    c2, c34, s1, s2, s3 = call(
        z_mask,
        0.7,
        [(256, 256), (128, 128), (208, 128), (16, 128), (8, 128)],
        own2,
        own34,
        n1,
        n2,
        n3,
        k0,
        near,
        away,
        index=index,
        shelves=[["z2u"], ["z34p", "z34pt", "z2ut"]],
        scratch=[(4, 176, 128), (256, 256)],
    )
    g, s1, s2, s3 = lax.optimization_barrier((g, s1, s2, s3))
    s1, s2, s3 = moved(s1, 4, 0), moved(s2, 8, 0), moved(s3, 12, 0)
    dy, dc = call(
        details_rim, 0.3, [(2, 40, 512), half], g, da, db, shelves=[["y1ut"], ["r5ut"]]
    )
    c2, dy = lax.optimization_barrier((c2, dy))
    pieces = call(
        z_join,
        0.8,
        [piece] * 4,
        c2,
        c34,
        s1,
        s2,
        s3,
        index=index,
        shelves=[["z2t", "z34t", "z2qt"]],
        scratch=[(256, 384)],
    )
    pieces = exchanged(pieces)
    w, m1, m2, m3 = call(
        y_send,
        0.4,
        [(256, 384), (384, 128), (64, 128), (16, 128)],
        *pieces,
        index=index,
        shelves=[["y2ut"], ["y34pt"]],
    )
    db, m1, m2, m3 = lax.optimization_barrier((db, m1, m2, m3))
    m1, m2, m3 = moved(m1, 0, 1), moved(m2, 0, 2), moved(m3, 0, 3)
    pb = moved(db, 1, 0)
    low, pa, py, pc = call(
        deep_join,
        2.5,
        [(16, 32, 256), (5, 32, 256), (2, 40, 512), half],
        w,
        m1,
        m2,
        m3,
        da,
        dy,
        dc,
        shelves=[["y34t"], ["xmi", "y2t"], ["y2qt", "y1ult", "r5ult"]],
        scratch=[(8, 32, 256)],
    )
    pa, py, pc = moved(pa, 1, 0), moved(py, 0, 1), moved(pc, 1, 1)
    (base,) = call(
        own_join, 0.5, [(16, 64, 512)], g, low, pb, shelves=[["x1i"], ["y1i"]]
    )
    (out,) = call(
        finish,
        2.0,
        [(16, 64, 512)],
        base,
        pa,
        py,
        pc,
        shelves=[["x1i"], ["y1qt", "r5z"], ["r5il"]],
        scratch=[(5, 64, 512)],
        streamed=True,
    )
    return out


def solution(mesh):
    in_specs = (
        P("gz", "gy", None),
        P(None, "gz", "gy", None),
        P(None, "gz", "gy", None),
        P(None, "gz", "gy", None),
        P(None, "gz", "gy", None),
        P("gz", "gy", None),
    )
    out_specs = P("gz", "gy", None)
    return jax.shard_map(
        on_device, mesh=mesh, in_specs=in_specs, out_specs=out_specs, check_vma=False
    )
```

```python
import functools

import jax
import jax.numpy as jnp
import ml_dtypes
import numpy as np
from jax import lax
from jax.experimental import pallas as pl
from jax.experimental.pallas import tpu as pltpu
from jax.sharding import PartitionSpec as P

low_taps = (
    0.11154074335008017,
    0.4946238903983854,
    0.7511339080215775,
    0.3152503517092432,
    -0.22626469396516913,
    -0.12976686756709563,
    0.09750160558707936,
    0.02752286553001629,
    -0.031582039318031156,
    0.0005538422009938016,
    0.004777257511010651,
    -0.00107730108499558,
)
high_taps = tuple(((-1.0) ** k * low_taps[11 - k] for k in range(12)))

GZ, GY = 32, 8
MEMBERS = 4
F32, BF16 = jnp.float32, jnp.bfloat16


def tail_of(s):
    return (s + 11) // 2


def band(taps, n, s):
    t = tail_of(s)
    out = np.zeros((t + n // 2, s + n))
    for row in range(t + n // 2):
        for col in range(s + n):
            k = (col - s) - 2 * (row - t)
            if 0 <= k < 12:
                out[row, col] = taps[k]
    return out


def periodic(taps, n):
    out = np.zeros((n // 2, n))
    for i in range(n // 2):
        for k in range(12):
            out[i, (2 * i + k) % n] += taps[k]
    return out


def rank_five():
    block = np.concatenate([band(low_taps, 10, 0)[:5], band(high_taps, 10, 0)[:5]])
    u, sing, vt = np.linalg.svd(block)
    return u[:, :5] * sing[:5], vt[:5]


def pair(matrix):
    high = matrix.astype(ml_dtypes.bfloat16)
    low = (matrix - high.astype(np.float64)).astype(ml_dtypes.bfloat16)
    return np.stack([high, low])


def padded(matrix, rows, cols):
    out = np.zeros((rows, cols))
    out[: matrix.shape[0], : matrix.shape[1]] = matrix
    return out


@functools.lru_cache(None)
def tables():
    spread, basis = rank_five()
    mats = {}
    x1 = np.concatenate([periodic(low_taps, 512), periodic(high_taps, 512)])
    mats["x1f"], mats["x1i"] = x1.T, x1
    mats["x1fl"], mats["x1fh"] = x1[:256].T, x1[256:].T
    lo2 = periodic(low_taps, 256)
    lo3 = periodic(low_taps, 128) @ lo2
    xm = np.concatenate(
        [
            lo2,
            periodic(high_taps, 256),
            lo3,
            periodic(high_taps, 128) @ lo2,
            periodic(low_taps, 64) @ lo3,
            periodic(high_taps, 64) @ lo3,
            np.zeros((64, 256)),
        ]
    )
    mats["xmf"], mats["xmi"] = xm.T, xm
    y1 = np.concatenate([band(low_taps, 64, 0)[5:], band(high_taps, 64, 0)[5:]])
    mats["y1f"] = np.kron(np.eye(4), y1)
    mats["y1i"] = mats["y1f"].T
    pick = padded(basis, 5, 64)
    mats["y1q"] = padded(np.kron(np.eye(8), pick), 48, 512)
    mats["y1qt"] = mats["y1q"].T
    put = np.zeros((64, 5))
    put[27:32], put[59:64] = spread[:5], spread[5:]
    mats["y1u"] = padded(np.kron(np.eye(8), put), 512, 48)
    mats["y1ut"] = mats["y1u"].T
    mats["y1l"] = np.kron(np.eye(4), y1[:32])
    mats["y1lt"] = mats["y1l"].T
    mats["y1ul"] = padded(np.kron(np.eye(8), put[:32]), 256, 48)
    mats["y1ult"] = mats["y1ul"].T
    corner = np.kron(np.eye(5), padded(pick, 8, 64))
    lows, highs = np.kron(np.eye(5), y1[:32]), np.kron(np.eye(5), y1[32:])
    mats["r5f"] = np.concatenate([lows, corner, highs])
    mats["r5i"] = np.kron(np.eye(5), y1.T)
    mats["r5il"] = np.kron(np.eye(5), y1[:32].T)
    mats["y1r"] = np.kron(np.eye(16), padded(basis, 5, 16))
    mats["r5u"] = np.kron(np.eye(5), padded(put, 64, 8))
    mats["r5ut"] = mats["r5u"].T
    mats["r5ul"] = np.kron(np.eye(5), padded(put[:32], 32, 8))
    mats["r5ult"] = mats["r5ul"].T
    far = np.zeros((2, 48, 40))
    for z in range(10):
        for k in range(5):
            far[z // 8, (z % 8) * 5 + k, k::8] = basis[:, z]
    mats["r5z"] = far.reshape(96, 40)
    z1 = np.concatenate([band(low_taps, 16, 0)[5:], band(high_taps, 16, 0)[5:]])
    mats["z1f"] = np.kron(z1, np.eye(16))
    mats["z1i"] = mats["z1f"].T
    zput = np.zeros((16, 5))
    zput[3:8], zput[11:16] = spread[:5], spread[5:]
    mats["z1u"] = np.kron(zput, np.eye(16))
    zpick = padded(basis, 5, 16)
    mats["z1qt"] = np.kron(zpick.T, np.eye(16))
    lo_a = band(low_taps, 32, 0)
    lo_b = band(low_taps, 16, 5) @ lo_a
    lev2 = [lo_a, band(high_taps, 32, 0)]
    lev3 = [lo_b, band(high_taps, 16, 5) @ lo_a]
    lev4 = [band(low_taps, 8, 8) @ lo_b, band(high_taps, 8, 8) @ lo_b]

    def row2(b, i):
        return lev2[b][i + 5]

    def row3(b, i):
        return lev3[b][i + 8]

    def row4(b, i):
        return lev4[b][i + 9]

    pick32 = padded(basis, 5, 32)
    put2 = np.zeros((2, 16, 5))
    put2[0, 11:], put2[1, 11:] = spread[:5], spread[5:]

    y2 = np.zeros((256, 256))
    y2u = np.zeros((256, 64))
    y34 = np.zeros((592, 512))
    y2q = np.kron(np.eye(8), padded(pick32, 8, 32))
    for m in range(4):
        for z in range(8):
            cells = slice(z * 32, z * 32 + 32)
            cells4 = slice(256 + z * 32, 256 + z * 32 + 32)
            for r in range(8):
                row = (m * 8 + z) * 8 + r
                y2[row, cells] = row2(r // 4, 4 * m + r % 4)
                y2u[row, z * 8 : z * 8 + 5] = put2[r // 4, 4 * m + r % 4]
                if r < 4:
                    y34[row, cells] = row3(r // 2, 2 * m + r % 2)
                    y34[256 + row, cells] = row3(r // 2, 2 * m + r % 2 - 8)
                elif r < 6:
                    y34[row, cells4] = row4(r - 4, m)
                    y34[256 + row, cells4] = row4(r - 4, m - 4)
    y34p = np.zeros((256, 80))
    for z in range(8):
        cells4 = slice(256 + z * 32, 256 + z * 32 + 32)
        for by in range(2):
            for i in range(4):
                y34[512 + z * 8 + by * 4 + i, cells4] = row4(by, i - 8)
                y34p[(i * 8 + z) * 8 + 4 + by, z * 8 + by * 4 + i] = 1.0
            y34[576 + z * 2 + by, cells4] = row4(by, -9)
            y34p[(3 * 8 + z) * 8 + 4 + by, 64 + z * 2 + by] = 1.0
    mats["y2"], mats["y2t"] = y2, y2.T
    mats["y2u"], mats["y2ut"] = y2u, y2u.T
    mats["y2q"], mats["y2qt"] = y2q, y2q.T
    mats["y34"], mats["y34t"] = y34, y34.T
    mats["y34p"], mats["y34pt"] = y34p, y34p.T

    eye8 = np.eye(8)
    z2 = np.kron(np.array([row2(b, i) for b in range(2) for i in range(16)]), eye8)
    z2q = padded(np.kron(pick32, eye8), 48, 256)
    z2u = padded(np.kron(put2.reshape(32, 5), eye8), 256, 48)
    z34 = np.zeros((288, 32, 8))
    z34p = np.zeros((128, 32))
    for b in range(2):
        for i in range(8):
            for r in range(4):
                z34[(b * 8 + i) * 8 + r, :, r] = row3(b, i)
                z34[128 + (b * 8 + i) * 8 + r, :, r] = row3(b, i - 8)
        for by in range(2):
            for i in range(4):
                slot = b * 4 + i
                z34[slot * 8 + 4 + by, :, 4 + by] = row4(b, i)
                z34[128 + slot * 8 + 4 + by, :, 4 + by] = row4(b, i - 4)
                z34[256 + slot * 2 + by, :, 4 + by] = row4(b, i - 8)
                z34p[slot * 8 + 4 + by, slot * 2 + by] = 1.0
            z34[272 + b * 2 + by, :, 4 + by] = row4(b, -9)
            z34p[(b * 4 + 3) * 8 + 4 + by, 16 + b * 2 + by] = 1.0
    z34 = z34.reshape(288, 256)
    mats["z2"], mats["z2t"] = z2, z2.T
    mats["z2q"], mats["z2qt"] = z2q, z2q.T
    mats["z2u"], mats["z2ut"] = z2u, z2u.T
    mats["z34"], mats["z34t"] = z34, z34.T
    mats["z34p"], mats["z34pt"] = z34p, z34p.T
    return mats


SPREAD, BASIS = rank_five()
Z1LO = band(low_taps, 16, 0)[5:]


def packed(shelves):
    mats = tables()
    places, rows, width = {}, 0, 0
    for shelf in shelves:
        col = tall = 0
        for name in shelf:
            height, wide = mats[name].shape
            places[name] = (rows, height, col, wide)
            col += -(-wide // 128) * 128
            tall = max(tall, -(-height // 16) * 16)
        rows, width = rows + tall, max(width, col)
    out = np.zeros((rows, width))
    for name, (row, height, col, wide) in places.items():
        out[row : row + height, col : col + wide] = mats[name]
    return pair(out), places


class Tables:
    def __init__(self, ref, places):
        self.ref, self.places = ref, places

    def __call__(self, name):
        row, height, col, wide = self.places[name]
        return [self.ref[k, row : row + height, col : col + wide] for k in range(2)]


SPREAD, BASIS = rank_five()
Z1LO = band(low_taps, 16, 0)[5:]


def halves(value):
    high = value.astype(BF16)
    return high, (value - high.astype(F32)).astype(BF16)


def dot(a, b):
    return lax.dot_general(a, b, (((1,), (0,)), ((), ())), preferred_element_type=F32)


def left(table, value):
    vh, vl = halves(value)
    return dot(table[0], vh) + dot(table[0], vl) + dot(table[1], vh)


def right(value, table):
    vh, vl = halves(value)
    return dot(vh, table[0]) + dot(vl, table[0]) + dot(vh, table[1])


def combine(weights, planes):
    total = None
    for weight, plane in zip(weights, planes):
        if weight == 0.0:
            continue
        term = float(weight) * plane()
        total = term if total is None else total + term
    return total


def taller(value, rows):
    return jnp.concatenate([value, jnp.zeros((rows, value.shape[1]), F32)], axis=0)


def call(kernel, micros, outs, *operands, shelves=None, index=None, scratch=(), table=None, streamed=False):
    spec, far = pl.BlockSpec(memory_space=pltpu.VMEM), pl.BlockSpec(memory_space=pltpu.HBM)
    specs = [spec] * len(operands)
    out_specs = [spec] * len(outs)
    operands = list(operands)
    places = None
    scratch = [pltpu.VMEM(shape, F32) for shape in scratch]
    if index is not None:
        operands.append(index)
        specs.append(pl.BlockSpec(memory_space=pltpu.SMEM))
    if shelves is not None:
        packed_table, places = packed(shelves)
        operands.append(jnp.asarray(packed_table) if table is None else table)
        specs.append(spec)
    if streamed:
        out_specs = [far] * len(outs)
        scratch += [pltpu.VMEM(outs[0], F32), pltpu.SemaphoreType.DMA((4,))]

    def body(*refs):
        refs = list(refs)
        count = len(operands)
        if streamed:
            held, sems = refs[-2:]
            target = refs[count]
            chunks = []
            for c in range(4):
                rows = pl.ds(4 * c, 4)
                chunks.append(pltpu.make_async_copy(held.at[rows], target.at[rows], sems.at[c]))
            refs[count] = held
            refs = refs[:-2] + [chunks]
        if places is not None:
            refs[count - 1] = Tables(refs[count - 1], places)
        kernel(*refs)

    return pl.pallas_call(
        body,
        name=kernel.__name__,
        out_shape=[jax.ShapeDtypeStruct(shape, F32) for shape in outs],
        in_specs=specs,
        out_specs=out_specs,
        scratch_shapes=scratch,
        cost_estimate=pl.CostEstimate(
            flops=int(micros * 1.1e9), transcendentals=0, bytes_accessed=int(micros * 3.6e6)
        ),
        compiler_params=pltpu.CompilerParams(vmem_limit_bytes=24 * 2**20),
    )(*operands)


def member(index, by):
    return lax.rem(index[0] + by + MEMBERS, MEMBERS)


def block(index, by, rows=64):
    return pl.ds(pl.multiple_of(member(index, by) * rows, rows), rows)


DEEP = [["y34"], ["xmf"], ["y2", "y1l"], ["y1ul", "r5ul", "y2q"]]


def from_far(kernel, name, micros, outs, operands, scratch):
    spec, far = pl.BlockSpec(memory_space=pltpu.VMEM), pl.BlockSpec(memory_space=pltpu.HBM)
    operands = [pltpu.with_memory_space_constraint(part, pltpu.HBM) for part in operands]
    return pl.pallas_call(
        kernel,
        name=name,
        out_shape=outs,
        in_specs=[far] * len(operands),
        out_specs=[spec] * len(outs),
        scratch_shapes=scratch,
        cost_estimate=pl.CostEstimate(
            flops=int(micros * 1.1e9), transcendentals=0, bytes_accessed=int(micros * 3.6e6)
        ),
        compiler_params=pltpu.CompilerParams(vmem_limit_bytes=24 * 2**20),
    )(*operands)


def planes_in(v, held, sems):
    chunks = []
    for c in range(4):
        rows = pl.ds(4 * c, 4)
        chunks.append(pltpu.make_async_copy(v.at[rows], held.at[rows], sems.at[c]))
    return chunks


def x_rims(vorticity):
    table, places = packed([["x1f"], ["r5f"], ["y1r"]])
    outs = [(2, 40, 512), (5, 32, 256), (5, 32, 768), (40, 512)]

    def kernel(v, small, q, qa, qb, qc, held, small_held, b, sems):
        chunks = planes_in(v, held, sems)
        small_copy = pltpu.make_async_copy(small, small_held, sems.at[4])
        for copy in chunks[:3] + [small_copy, chunks[3]]:
            copy.start()
        for copy in chunks[:3]:
            copy.wait()
        t = Tables(small_held, places)
        for n in range(5):
            b[n] = combine(BASIS[n], [lambda j=j: held[j] for j in range(10)])
        small_copy.wait()
        chunks[3].wait()
        rim = left(t("r5f"), b[...].reshape(320, 512))
        rows = left(t("y1r"), held[:, :16].reshape(256, 512))
        rim = right(jnp.concatenate([rim, rows], axis=0), t("x1f"))
        q[...] = rim[360:].reshape(2, 40, 512)
        qc[...] = rim[160:200]
        qa[...] = rim[:160, :256].reshape(5, 32, 256)
        qb[:, :, :256] = rim[:160, 256:].reshape(5, 32, 256)
        qb[:, :, 256:] = rim[200:360].reshape(5, 32, 512)

    return from_far(
        kernel,
        "x_rims",
        3.0,
        [jax.ShapeDtypeStruct(shape, F32) for shape in outs],
        [vorticity, jnp.asarray(table)],
        [
            pltpu.VMEM(vorticity.shape, F32),
            pltpu.VMEM(table.shape, BF16),
            pltpu.VMEM((5, 64, 512), F32),
            pltpu.SemaphoreType.DMA((5,)),
        ],
    )


def x_low(vorticity):
    table, places = packed([["x1fl"]])
    deep_table, _ = packed(DEEP)

    def kernel(v, small, large, f, deep, held, small_held, sems):
        chunks = planes_in(v, held, sems)
        small_copy = pltpu.make_async_copy(small, small_held, sems.at[4])
        deep_copy = pltpu.make_async_copy(large, deep, sems.at[5])
        for copy in [small_copy] + chunks + [deep_copy]:
            copy.start()
        small_copy.wait()
        t = Tables(small_held, places)
        for c in range(4):
            chunks[c].wait()
            part = held[4 * c : 4 * c + 4].reshape(256, 512)
            f[4 * c : 4 * c + 4] = right(part, t("x1fl")).reshape(4, 64, 256)
        deep_copy.wait()

    return from_far(
        kernel,
        "x_low",
        0.5,
        [
            jax.ShapeDtypeStruct((16, 64, 256), F32),
            jax.ShapeDtypeStruct(deep_table.shape, BF16),
        ],
        [vorticity, jnp.asarray(table), jnp.asarray(deep_table)],
        [
            pltpu.VMEM(vorticity.shape, F32),
            pltpu.VMEM(table.shape, BF16),
            pltpu.SemaphoreType.DMA((6,)),
        ],
    )


def x_high(v, t, f):
    for c in range(4):
        part = v[4 * c : 4 * c + 4].reshape(256, 512)
        f[4 * c : 4 * c + 4] = right(part, t("x1fh")).reshape(4, 64, 256)


def deep_split(f, q, qa, qc, t, own, m1, m2, m3, g, low):
    for half in range(2):
        extra = left(t("y1ul"), taller(q[half, :, :256], 8))
        for c in range(2):
            z = 8 * half + 4 * c
            part = left(t("y1l"), f[z : z + 4].reshape(256, 256))
            g[z : z + 4] = (part + extra[128 * c : 128 * c + 128]).reshape(4, 32, 256)
    rim = qa[...].reshape(160, 256) + left(t("r5ul"), qc[:, :256])
    rim = rim.reshape(5, 32, 256)
    for i in range(8):
        plane = combine(Z1LO[i], [lambda j=j: g[j] for j in range(16)])
        if i >= 3:
            plane = plane + combine(SPREAD[i - 3], [lambda n=n: rim[n] for n in range(5)])
        low[i] = plane
    wide = right(low[...].reshape(256, 256), t("xmf"))
    rim = left(t("y2q"), wide[:, :256])
    m1[256:320] = rim[:, :128]
    m1[320:384] = rim[:, 128:]
    rest = left(t("y34"), jnp.concatenate([wide[:, 256:384], wide[:, 384:]], axis=0))
    own[:, 256:] = rest[:256]
    m1[:256] = rest[256:512]
    m2[...] = rest[512:576]
    m3[...] = rest[576:592]
    own[:, :256] = left(t("y2"), wide[:, :256])


def y_gather(own, m1, m2, m3, index, t, p0, p1, p2, p3, w):
    rim = jnp.concatenate([m1[256:320], m1[320:384]], axis=1)
    w[:, :256] = own[:, :256] + left(t("y2u"), rim)
    far = jnp.concatenate([m2[...], m3[...]], axis=0)
    w[:, 256:] = own[:, 256:] + m1[:256] + left(t("y34p"), far)
    for s, piece in enumerate((p0, p1, p2, p3)):
        piece[...] = w[block(index, s)]


def z_split(p0, p1, p2, p3, index, t, own2, own34, n1, n2, n3, w):
    for s, piece in enumerate((p0, p1, p2, p3)):
        w[block(index, -s)] = piece[...]
    rim = left(t("z2q"), w[:, :256])
    n1[128:168] = rim[:40, :128]
    n1[168:208] = rim[:40, 128:]
    rest = left(t("z34"), w[:, 256:])
    own34[...] = rest[:128]
    n1[:128] = rest[128:256]
    n2[...] = rest[256:272]
    n3[...] = rest[272:280]
    own2[...] = left(t("z2"), w[:, :256])


def mask_pack(two, three, four, coarse, index, k0, k2, near, full):
    def plain(ref, b, z):
        if b == 0:
            return jnp.zeros(ref.shape[2:], F32)
        return ref[b - 1, z].astype(F32)

    for bz in range(2):
        for z in range(4):
            for bx in range(2):
                rows = [plain(two, 4 * bz + 2 * by + bx, z) for by in range(2)]
                at = bx * 64 + (bz * 4 + z) * 8
                for m in range(4):
                    full[m, at : at + 8] = jnp.concatenate(
                        [part[4 * m : 4 * m + 4] for part in rows], axis=0
                    )
        for z in range(2):
            rows = [
                jnp.concatenate([plain(three, 4 * bz + 2 * by + bx, z) for bx in range(2)], axis=1)
                for by in range(2)
            ]
            at = 128 + (bz * 2 + z) * 8
            for m in range(4):
                parts = [part[2 * m : 2 * m + 2] for part in rows]
                full[m, at : at + 8] = jnp.concatenate(parts + [jnp.zeros((4, 128), F32)], axis=0)
        rows = []
        for by in range(2):
            parts = [
                coarse[0].astype(F32) if bz + by + bx == 0 else plain(four, 4 * bz + 2 * by + bx, 0)
                for bx in range(2)
            ]
            rows.append(jnp.concatenate(parts + [jnp.zeros((4, 64), F32)], axis=1))
        at = 160 + bz * 8
        for m in range(4):
            parts = [jnp.zeros((4, 128), F32)] + [part[m : m + 1] for part in rows]
            full[m, at : at + 8] = jnp.concatenate(parts + [jnp.zeros((2, 128), F32)], axis=0)
    k0[...] = full[index[0]]
    k2[...] = full[lax.bitwise_xor(index[0], 2)]
    for n in range(2):
        near[n] = full[lax.bitwise_xor(index[0], 2 * n + 1)]


def z_mask(own2, own34, n1, n2, n3, k0, near, away, index, t, c2, c34, s1, s2, s3, full, keep2):
    full[index[0]] = k0[...]
    full[lax.bitwise_xor(index[0], 1)] = near[0]
    for n in range(2):
        full[lax.bitwise_xor(index[0], 2 + n)] = away[n]
    for a in range(4):
        for bz in range(2):
            for bx in range(2):
                at = bz * 128 + a * 32
                rows = full[a, bx * 64 + bz * 32 : bx * 64 + bz * 32 + 32]
                keep2[at : at + 32, bx * 128 : bx * 128 + 128] = rows
    tiles = []
    for slot in range(16):
        bz, a, z = slot // 8, slot // 2 % 4, slot % 2
        tile = full[a, 128 + (bz * 2 + z) * 8 : 136 + (bz * 2 + z) * 8]
        if slot < 8:
            bz, a = slot // 4, slot % 4
            tile = tile + full[a, 160 + bz * 8 : 168 + bz * 8]
        tiles.append(tile)
    keep34 = jnp.concatenate(tiles, axis=0)

    far = taller(jnp.concatenate([n2[...], n3[...]], axis=0), 8)
    part34 = (own34[...] + n1[:128] + left(t("z34p"), far)) * keep34
    c34[...] = part34
    s1[:128] = part34
    back = left(t("z34pt"), part34)
    s2[...] = back[:16]
    s3[...] = back[16:24]
    rim = taller(jnp.concatenate([n1[128:168], n1[168:208]], axis=1), 8)
    part2 = (own2[...] + left(t("z2u"), rim)) * keep2[...]
    c2[...] = part2
    back = left(t("z2ut"), part2)
    s1[128:168] = back[:40, :128]
    s1[168:208] = back[:40, 128:]


def z_join(c2, c34, s1, s2, s3, index, t, p0, p1, p2, p3, w):
    rim = taller(jnp.concatenate([s1[128:168], s1[168:208]], axis=1), 8)
    w[:, :256] = left(t("z2t"), c2[...]) + left(t("z2qt"), rim)
    rows = jnp.concatenate([c34[...], s1[:128], s2[...], s3[...]], axis=0)
    w[:, 256:] = left(t("z34t"), taller(rows, 8))
    for s, piece in enumerate((p0, p1, p2, p3)):
        piece[...] = w[block(index, s)]


def y_send(p0, p1, p2, p3, index, t, w, m1, m2, m3):
    for s, piece in enumerate((p0, p1, p2, p3)):
        w[block(index, -s)] = piece[...]
    m1[:256] = w[:, 256:]
    rim = left(t("y2ut"), w[:, :256])
    m1[256:320] = rim[:, :128]
    m1[320:384] = rim[:, 128:]
    far = left(t("y34pt"), w[:, 256:])
    m2[...] = far[:64]
    m3[...] = far[64:]


def deep_join(w, m1, m2, m3, da, dy, dc, t, g, pa, py, pc, low):
    rim = jnp.concatenate([m1[256:320], m1[320:384]], axis=1)
    first = left(t("y2t"), w[:, :256]) + left(t("y2qt"), rim)
    rows = [w[:, 256:], m1[:256], m2[...], m3[...]]
    rest = left(t("y34t"), jnp.concatenate(rows, axis=0))
    wide = jnp.concatenate([first, rest[:256], rest[256:]], axis=1)
    low[...] = right(wide, t("xmi")).reshape(8, 32, 256)
    planes = [
        combine(SPREAD[:5, n], [lambda i=i: low[i + 3] for i in range(5)]) for n in range(5)
    ]
    for z in range(16):
        g[z] = combine(Z1LO[:, z], [lambda i=i: low[i] for i in range(8)])
    for n in range(5):
        pa[n] = da[n] + planes[n]
    corner = left(t("r5ult"), jnp.concatenate(planes, axis=0))
    pc[:, :256] = dc[:, :256] + corner
    pc[:, 256:] = dc[:, 256:]
    for half in range(2):
        part = g[8 * half : 8 * half + 8].reshape(256, 256)
        py[half, :, :256] = dy[half, :, :256] + left(t("y1ult"), part)[:40]
        py[half, :, 256:] = dy[half, :, 256:]


def own_join(g, low, pb, t, out):
    for c in range(4):
        planes = []
        for z in range(4 * c, 4 * c + 4):
            rest = [g[z, :32, 256:], g[z, 32:]]
            if z < 10:
                rim = combine(BASIS[:, z], [lambda n=n: pb[n] for n in range(5)])
                rest = [rest[0] + rim[:, :256], rest[1] + rim[:, 256:]]
            corner = g[z, :32, :256] + low[z]
            planes += [jnp.concatenate([corner, rest[0]], axis=1), rest[1]]
        part = left(t("y1i"), jnp.concatenate(planes, axis=0))
        out[4 * c : 4 * c + 4] = right(part, t("x1i")).reshape(4, 64, 512)


def finish(base, pa, py, pc, t, out, rz, chunks):
    x1l = [part[:256] for part in t("x1i")]
    rz[...] = right(left(t("r5il"), pa[...].reshape(160, 256)), x1l).reshape(5, 64, 512)
    far = left(t("r5z"), pc[...])
    rims = [taller(py[half], 8) + far[48 * half : 48 * half + 48] for half in range(2)]
    rims = right(jnp.concatenate(rims, axis=0), t("x1i"))
    for half in range(2):
        extra = left(t("y1qt"), rims[48 * half : 48 * half + 48]).reshape(8, 64, 512)
        for k in range(8):
            z = 8 * half + k
            plane = base[z] + extra[k]
            if z < 10:
                plane = plane + combine(BASIS[:, z], [lambda n=n: rz[n] for n in range(5)])
            out[z] = plane
            if z % 4 == 3:
                chunks[z // 4].start()
    for copy in chunks:
        copy.wait()


def details(fl, fh, q, qa, qb, qc, keep, t, g, da, db, kept):
    for half in range(2):
        extra = left(t("y1u"), taller(q[half], 8))
        for c in range(2):
            z = 8 * half + 4 * c
            part = jnp.concatenate([fl[z : z + 4], fh[z : z + 4]], axis=2)
            part = left(t("y1f"), part.reshape(256, 512))
            g[z : z + 4] = (part + extra[256 * c : 256 * c + 256]).reshape(4, 64, 512)
    top = jnp.concatenate([qa[...], qb[:, :, :256]], axis=2)
    planes = jnp.concatenate([top, qb[:, :, 256:]], axis=1)
    planes = planes + left(t("r5u"), qc[...]).reshape(5, 64, 512)
    for c in range(4):
        rows = slice(16 * c, 16 * c + 16)
        rim = planes[:, rows].reshape(80, 512)
        out = left(t("z1f"), g[:, rows].reshape(256, 512)) + left(t("z1u"), rim)
        out = out.reshape(16, 16, 512)
        by = c // 2
        at = slice(16 * (c % 2), 16 * (c % 2) + 16)
        for bz in range(2):
            for bx in range(2):
                cols = slice(256 * bx, 256 * bx + 256)
                number = 4 * bz + 2 * by + bx
                if number:
                    mask = keep[number - 1, :, at].astype(F32)
                    part = out[8 * bz : 8 * bz + 8, :, cols] * mask
                else:
                    part = jnp.zeros((8, 16, 256), F32)
                kept[8 * bz : 8 * bz + 8, rows, cols] = part
    for n in range(5):
        plane = combine(SPREAD[:5, n], [lambda i=i: kept[i + 3] for i in range(5)])
        plane = plane + combine(SPREAD[5:, n], [lambda i=i: kept[i + 11] for i in range(5)])
        da[n] = plane[:32, :256]
        db[n, :, :256] = plane[:32, 256:]
        db[n, :, 256:] = plane[32:]
    for c in range(4):
        rows = slice(16 * c, 16 * c + 16)
        out = left(t("z1i"), kept[:, rows].reshape(256, 512))
        g[:, rows] = out.reshape(16, 16, 512)


def details_rim(g, da, db, t, py, pc):
    top = jnp.concatenate([da[...], db[:, :, :256]], axis=2)
    planes = jnp.concatenate([top, db[:, :, 256:]], axis=1)
    pc[...] = left(t("r5ut"), planes.reshape(320, 512))
    for half in range(2):
        part = g[8 * half : 8 * half + 8].reshape(512, 512)
        py[half] = left(t("y1ut"), part)[:40]


def moved(value, by_z, by_y):
    pairs = [
        (z * GY + y, (z + by_z) % GZ * GY + (y + by_y) % GY) for z in range(GZ) for y in range(GY)
    ]
    return lax.ppermute(value, ("gz", "gy"), pairs)


def across(value, flip):
    return lax.ppermute(value, "gz", [(z, z ^ flip) for z in range(GZ)])


def exchanged(pieces):
    out = [pieces[0]]
    for s in range(1, MEMBERS):
        pairs = [(z, z // MEMBERS * MEMBERS + (z + s) % MEMBERS) for z in range(GZ)]
        out.append(lax.ppermute(pieces[s], "gz", pairs))
    return out


def on_device(vorticity, keep_one, keep_two, keep_three, keep_four, keep_coarse):
    index = lax.rem(lax.axis_index("gz"), MEMBERS).astype(jnp.int32).reshape(1)
    piece, half = (64, 384), (40, 512)

    q, qa, qb, qc = x_rims(vorticity)
    vorticity, q, qa, qb, qc = lax.optimization_barrier((vorticity, q, qa, qb, qc))
    q, qa, qc = moved(q, 0, -1), moved(qa, -1, 0), moved(qc, -1, -1)
    qb = moved(qb, -1, 0)
    f, deep = x_low(vorticity)
    own, m1, m2, m3 = call(
        deep_split,
        3.0,
        [(256, 384), (384, 128), (64, 128), (16, 128)],
        f,
        q,
        qa,
        qc,
        shelves=DEEP,
        table=deep,
        scratch=[(16, 32, 256), (8, 32, 256)],
    )
    vorticity, late, m1, m2, m3 = lax.optimization_barrier((vorticity, index, m1, m2, m3))
    m1, m2, m3 = moved(m1, 0, -1), moved(m2, 0, -2), moved(m3, 0, -3)
    (fh,) = call(x_high, 0.3, [(16, 64, 256)], vorticity, shelves=[["x1fh"]])
    g, da, db = call(
        details,
        0.5,
        [(16, 64, 512), (5, 32, 256), (5, 32, 768)],
        f,
        fh,
        q,
        qa,
        qb,
        qc,
        keep_one,
        shelves=[["y1f", "z1f", "z1i", "z1u"], ["y1u", "r5u"]],
        scratch=[(16, 64, 512)],
    )
    k0, k2, near = call(
        mask_pack,
        0.1,
        [(176, 128), (176, 128), (2, 176, 128)],
        keep_two,
        keep_three,
        keep_four,
        keep_coarse,
        index=late,
        scratch=[(4, 176, 128)],
    )
    near = across(near, 1)
    own, g, near = lax.optimization_barrier((own, g, near))
    away = jnp.stack([k2, near[1]])

    pieces = call(
        y_gather,
        0.7,
        [piece] * 4,
        own,
        m1,
        m2,
        m3,
        index=index,
        shelves=[["y2u", "y34p"]],
        scratch=[(256, 384)],
    )
    pieces = exchanged(pieces)
    own2, own34, n1, n2, n3 = call(
        z_split,
        0.5,
        [(256, 256), (128, 128), (208, 128), (16, 128), (8, 128)],
        *pieces,
        index=index,
        shelves=[["z2", "z34"], ["z2q"]],
        scratch=[(256, 384)],
    )
    away, n1, n2, n3 = lax.optimization_barrier((away, n1, n2, n3))
    n1, n2, n3 = moved(n1, -4, 0), moved(n2, -8, 0), moved(n3, -12, 0)
    away = across(away, 2)

    c2, c34, s1, s2, s3 = call(
        z_mask,
        0.7,
        [(256, 256), (128, 128), (208, 128), (16, 128), (8, 128)],
        own2,
        own34,
        n1,
        n2,
        n3,
        k0,
        near,
        away,
        index=index,
        shelves=[["z2u"], ["z34p", "z34pt", "z2ut"]],
        scratch=[(4, 176, 128), (256, 256)],
    )
    g, db, s1, s2, s3 = lax.optimization_barrier((g, db, s1, s2, s3))
    s1, s2, s3 = moved(s1, 4, 0), moved(s2, 8, 0), moved(s3, 12, 0)
    pb = moved(db, 1, 0)
    dy, dc = call(
        details_rim, 0.3, [(2, 40, 512), half], g, da, db, shelves=[["y1ut"], ["r5ut"]]
    )
    c2, dy, pb = lax.optimization_barrier((c2, dy, pb))
    pieces = call(
        z_join,
        0.8,
        [piece] * 4,
        c2,
        c34,
        s1,
        s2,
        s3,
        index=index,
        shelves=[["z2t", "z34t", "z2qt"]],
        scratch=[(256, 384)],
    )
    pieces = exchanged(pieces)
    w, m1, m2, m3 = call(
        y_send,
        0.4,
        [(256, 384), (384, 128), (64, 128), (16, 128)],
        *pieces,
        index=index,
        shelves=[["y2ut"], ["y34pt"]],
    )
    m1, m2, m3 = moved(m1, 0, 1), moved(m2, 0, 2), moved(m3, 0, 3)
    low, pa, py, pc = call(
        deep_join,
        2.5,
        [(16, 32, 256), (5, 32, 256), (2, 40, 512), half],
        w,
        m1,
        m2,
        m3,
        da,
        dy,
        dc,
        shelves=[["y34t"], ["xmi", "y2t"], ["y2qt", "y1ult", "r5ult"]],
        scratch=[(8, 32, 256)],
    )
    pa, py, pc = moved(pa, 1, 0), moved(py, 0, 1), moved(pc, 1, 1)
    (base,) = call(
        own_join, 0.5, [(16, 64, 512)], g, low, pb, shelves=[["x1i"], ["y1i"]]
    )
    (out,) = call(
        finish,
        2.0,
        [(16, 64, 512)],
        base,
        pa,
        py,
        pc,
        shelves=[["x1i"], ["y1qt", "r5z"], ["r5il"]],
        scratch=[(5, 64, 512)],
        streamed=True,
    )
    return out


def solution(mesh):
    in_specs = (
        P("gz", "gy", None),
        P(None, "gz", "gy", None),
        P(None, "gz", "gy", None),
        P(None, "gz", "gy", None),
        P(None, "gz", "gy", None),
        P("gz", "gy", None),
    )
    out_specs = P("gz", "gy", None)
    return jax.shard_map(
        on_device, mesh=mesh, in_specs=in_specs, out_specs=out_specs, check_vma=False
    )
```

```python
import functools

import jax
import jax.numpy as jnp
import ml_dtypes
import numpy as np
from jax import lax
from jax.experimental import pallas as pl
from jax.experimental.pallas import tpu as pltpu
from jax.sharding import PartitionSpec as P

low_taps = (
    0.11154074335008017,
    0.4946238903983854,
    0.7511339080215775,
    0.3152503517092432,
    -0.22626469396516913,
    -0.12976686756709563,
    0.09750160558707936,
    0.02752286553001629,
    -0.031582039318031156,
    0.0005538422009938016,
    0.004777257511010651,
    -0.00107730108499558,
)
high_taps = tuple(((-1.0) ** k * low_taps[11 - k] for k in range(12)))

GZ, GY = 32, 8
MEMBERS = 4
F32, BF16 = jnp.float32, jnp.bfloat16


def tail_of(s):
    return (s + 11) // 2


def band(taps, n, s):
    t = tail_of(s)
    out = np.zeros((t + n // 2, s + n))
    for row in range(t + n // 2):
        for col in range(s + n):
            k = (col - s) - 2 * (row - t)
            if 0 <= k < 12:
                out[row, col] = taps[k]
    return out


def periodic(taps, n):
    out = np.zeros((n // 2, n))
    for i in range(n // 2):
        for k in range(12):
            out[i, (2 * i + k) % n] += taps[k]
    return out


def rank_five():
    block = np.concatenate([band(low_taps, 10, 0)[:5], band(high_taps, 10, 0)[:5]])
    u, sing, vt = np.linalg.svd(block)
    return u[:, :5] * sing[:5], vt[:5]


def pair(matrix):
    high = matrix.astype(ml_dtypes.bfloat16)
    low = (matrix - high.astype(np.float64)).astype(ml_dtypes.bfloat16)
    return np.stack([high, low])


def padded(matrix, rows, cols):
    out = np.zeros((rows, cols))
    out[: matrix.shape[0], : matrix.shape[1]] = matrix
    return out


@functools.lru_cache(None)
def tables():
    spread, basis = rank_five()
    mats = {}
    x1 = np.concatenate([periodic(low_taps, 512), periodic(high_taps, 512)])
    mats["x1f"], mats["x1i"] = x1.T, x1
    mats["x1fl"], mats["x1fh"] = x1[:256].T, x1[256:].T
    lo2 = periodic(low_taps, 256)
    lo3 = periodic(low_taps, 128) @ lo2
    xm = np.concatenate(
        [
            lo2,
            periodic(high_taps, 256),
            lo3,
            periodic(high_taps, 128) @ lo2,
            periodic(low_taps, 64) @ lo3,
            periodic(high_taps, 64) @ lo3,
            np.zeros((64, 256)),
        ]
    )
    mats["xmf"], mats["xmi"] = xm.T, xm
    y1 = np.concatenate([band(low_taps, 64, 0)[5:], band(high_taps, 64, 0)[5:]])
    mats["y1f"] = np.kron(np.eye(4), y1)
    mats["y1i"] = mats["y1f"].T
    pick = padded(basis, 5, 64)
    mats["y1q"] = padded(np.kron(np.eye(8), pick), 48, 512)
    mats["y1qt"] = mats["y1q"].T
    put = np.zeros((64, 5))
    put[27:32], put[59:64] = spread[:5], spread[5:]
    mats["y1u"] = padded(np.kron(np.eye(8), put), 512, 48)
    mats["y1ut"] = mats["y1u"].T
    mats["y1l"] = np.kron(np.eye(4), y1[:32])
    mats["y1lt"] = mats["y1l"].T
    mats["y1ul"] = padded(np.kron(np.eye(8), put[:32]), 256, 48)
    mats["y1ult"] = mats["y1ul"].T
    corner = np.kron(np.eye(5), padded(pick, 8, 64))
    lows, highs = np.kron(np.eye(5), y1[:32]), np.kron(np.eye(5), y1[32:])
    mats["r5f"] = np.concatenate([lows, corner, highs])
    mats["r5i"] = np.kron(np.eye(5), y1.T)
    mats["r5il"] = np.kron(np.eye(5), y1[:32].T)
    mats["y1r"] = np.kron(np.eye(16), padded(basis, 5, 16))
    mats["r5u"] = np.kron(np.eye(5), padded(put, 64, 8))
    mats["r5ut"] = mats["r5u"].T
    mats["r5ul"] = np.kron(np.eye(5), padded(put[:32], 32, 8))
    mats["r5ult"] = mats["r5ul"].T
    far = np.zeros((2, 48, 40))
    for z in range(10):
        for k in range(5):
            far[z // 8, (z % 8) * 5 + k, k::8] = basis[:, z]
    mats["r5z"] = far.reshape(96, 40)
    z1 = np.concatenate([band(low_taps, 16, 0)[5:], band(high_taps, 16, 0)[5:]])
    mats["z1f"] = np.kron(z1, np.eye(16))
    mats["z1i"] = mats["z1f"].T
    zput = np.zeros((16, 5))
    zput[3:8], zput[11:16] = spread[:5], spread[5:]
    mats["z1u"] = np.kron(zput, np.eye(16))
    zpick = padded(basis, 5, 16)
    mats["z1qt"] = np.kron(zpick.T, np.eye(16))
    lo_a = band(low_taps, 32, 0)
    lo_b = band(low_taps, 16, 5) @ lo_a
    lev2 = [lo_a, band(high_taps, 32, 0)]
    lev3 = [lo_b, band(high_taps, 16, 5) @ lo_a]
    lev4 = [band(low_taps, 8, 8) @ lo_b, band(high_taps, 8, 8) @ lo_b]

    def row2(b, i):
        return lev2[b][i + 5]

    def row3(b, i):
        return lev3[b][i + 8]

    def row4(b, i):
        return lev4[b][i + 9]

    pick32 = padded(basis, 5, 32)
    put2 = np.zeros((2, 16, 5))
    put2[0, 11:], put2[1, 11:] = spread[:5], spread[5:]

    y2 = np.zeros((256, 256))
    y2u = np.zeros((256, 64))
    y34 = np.zeros((592, 512))
    y2q = np.kron(np.eye(8), padded(pick32, 8, 32))
    for m in range(4):
        for z in range(8):
            cells = slice(z * 32, z * 32 + 32)
            cells4 = slice(256 + z * 32, 256 + z * 32 + 32)
            for r in range(8):
                row = (m * 8 + z) * 8 + r
                y2[row, cells] = row2(r // 4, 4 * m + r % 4)
                y2u[row, z * 8 : z * 8 + 5] = put2[r // 4, 4 * m + r % 4]
                if r < 4:
                    y34[row, cells] = row3(r // 2, 2 * m + r % 2)
                    y34[256 + row, cells] = row3(r // 2, 2 * m + r % 2 - 8)
                elif r < 6:
                    y34[row, cells4] = row4(r - 4, m)
                    y34[256 + row, cells4] = row4(r - 4, m - 4)
    y34p = np.zeros((256, 80))
    for z in range(8):
        cells4 = slice(256 + z * 32, 256 + z * 32 + 32)
        for by in range(2):
            for i in range(4):
                y34[512 + z * 8 + by * 4 + i, cells4] = row4(by, i - 8)
                y34p[(i * 8 + z) * 8 + 4 + by, z * 8 + by * 4 + i] = 1.0
            y34[576 + z * 2 + by, cells4] = row4(by, -9)
            y34p[(3 * 8 + z) * 8 + 4 + by, 64 + z * 2 + by] = 1.0
    mats["y2"], mats["y2t"] = y2, y2.T
    mats["y2u"], mats["y2ut"] = y2u, y2u.T
    mats["y2q"], mats["y2qt"] = y2q, y2q.T
    mats["y34"], mats["y34t"] = y34, y34.T
    mats["y34p"], mats["y34pt"] = y34p, y34p.T

    eye8 = np.eye(8)
    z2 = np.kron(np.array([row2(b, i) for b in range(2) for i in range(16)]), eye8)
    z2q = padded(np.kron(pick32, eye8), 48, 256)
    z2u = padded(np.kron(put2.reshape(32, 5), eye8), 256, 48)
    z34 = np.zeros((288, 32, 8))
    z34p = np.zeros((128, 32))
    for b in range(2):
        for i in range(8):
            for r in range(4):
                z34[(b * 8 + i) * 8 + r, :, r] = row3(b, i)
                z34[128 + (b * 8 + i) * 8 + r, :, r] = row3(b, i - 8)
        for by in range(2):
            for i in range(4):
                slot = b * 4 + i
                z34[slot * 8 + 4 + by, :, 4 + by] = row4(b, i)
                z34[128 + slot * 8 + 4 + by, :, 4 + by] = row4(b, i - 4)
                z34[256 + slot * 2 + by, :, 4 + by] = row4(b, i - 8)
                z34p[slot * 8 + 4 + by, slot * 2 + by] = 1.0
            z34[272 + b * 2 + by, :, 4 + by] = row4(b, -9)
            z34p[(b * 4 + 3) * 8 + 4 + by, 16 + b * 2 + by] = 1.0
    z34 = z34.reshape(288, 256)
    mats["z2"], mats["z2t"] = z2, z2.T
    mats["z2q"], mats["z2qt"] = z2q, z2q.T
    mats["z2u"], mats["z2ut"] = z2u, z2u.T
    mats["z34"], mats["z34t"] = z34, z34.T
    mats["z34p"], mats["z34pt"] = z34p, z34p.T
    return mats


SPREAD, BASIS = rank_five()
Z1LO = band(low_taps, 16, 0)[5:]


def packed(shelves):
    mats = tables()
    places, rows, width = {}, 0, 0
    for shelf in shelves:
        col = tall = 0
        for name in shelf:
            height, wide = mats[name].shape
            places[name] = (rows, height, col, wide)
            col += -(-wide // 128) * 128
            tall = max(tall, -(-height // 16) * 16)
        rows, width = rows + tall, max(width, col)
    out = np.zeros((rows, width))
    for name, (row, height, col, wide) in places.items():
        out[row : row + height, col : col + wide] = mats[name]
    return pair(out), places


class Tables:
    def __init__(self, ref, places):
        self.ref, self.places = ref, places

    def __call__(self, name):
        row, height, col, wide = self.places[name]
        return [self.ref[k, row : row + height, col : col + wide] for k in range(2)]


SPREAD, BASIS = rank_five()
Z1LO = band(low_taps, 16, 0)[5:]


def halves(value):
    high = value.astype(BF16)
    return high, (value - high.astype(F32)).astype(BF16)


def dot(a, b):
    return lax.dot_general(a, b, (((1,), (0,)), ((), ())), preferred_element_type=F32)


def left(table, value):
    vh, vl = halves(value)
    return dot(table[0], vh) + dot(table[0], vl) + dot(table[1], vh)


def right(value, table):
    vh, vl = halves(value)
    return dot(vh, table[0]) + dot(vl, table[0]) + dot(vh, table[1])


def combine(weights, planes):
    total = None
    for weight, plane in zip(weights, planes):
        if weight == 0.0:
            continue
        term = float(weight) * plane()
        total = term if total is None else total + term
    return total


def taller(value, rows):
    return jnp.concatenate([value, jnp.zeros((rows, value.shape[1]), F32)], axis=0)


def call(kernel, micros, outs, *operands, shelves=None, index=None, scratch=(), table=None, streamed=False):
    spec, far = pl.BlockSpec(memory_space=pltpu.VMEM), pl.BlockSpec(memory_space=pltpu.HBM)
    specs = [spec] * len(operands)
    out_specs = [spec] * len(outs)
    operands = list(operands)
    places = None
    scratch = [pltpu.VMEM(shape, F32) for shape in scratch]
    if index is not None:
        operands.append(index)
        specs.append(pl.BlockSpec(memory_space=pltpu.SMEM))
    if shelves is not None:
        packed_table, places = packed(shelves)
        operands.append(jnp.asarray(packed_table) if table is None else table)
        specs.append(spec)
    if streamed:
        out_specs = [far] * len(outs)
        scratch += [pltpu.VMEM(outs[0], F32), pltpu.SemaphoreType.DMA((4,))]

    def body(*refs):
        refs = list(refs)
        count = len(operands)
        if streamed:
            held, sems = refs[-2:]
            target = refs[count]
            chunks = []
            for c in range(4):
                rows = pl.ds(4 * c, 4)
                chunks.append(pltpu.make_async_copy(held.at[rows], target.at[rows], sems.at[c]))
            refs[count] = held
            refs = refs[:-2] + [chunks]
        if places is not None:
            refs[count - 1] = Tables(refs[count - 1], places)
        kernel(*refs)

    return pl.pallas_call(
        body,
        name=kernel.__name__,
        out_shape=[jax.ShapeDtypeStruct(shape, F32) for shape in outs],
        in_specs=specs,
        out_specs=out_specs,
        scratch_shapes=scratch,
        cost_estimate=pl.CostEstimate(
            flops=int(micros * 1.1e9), transcendentals=0, bytes_accessed=int(micros * 3.6e6)
        ),
        compiler_params=pltpu.CompilerParams(vmem_limit_bytes=24 * 2**20),
    )(*operands)


def member(index, by):
    return lax.rem(index[0] + by + MEMBERS, MEMBERS)


def block(index, by, rows=64):
    return pl.ds(pl.multiple_of(member(index, by) * rows, rows), rows)


DEEP = [["y34"], ["xmf"], ["y2", "y1l"], ["y1ul", "r5ul", "y2q"]]


def from_far(kernel, name, micros, outs, operands, scratch):
    spec, far = pl.BlockSpec(memory_space=pltpu.VMEM), pl.BlockSpec(memory_space=pltpu.HBM)
    operands = [pltpu.with_memory_space_constraint(part, pltpu.HBM) for part in operands]
    return pl.pallas_call(
        kernel,
        name=name,
        out_shape=outs,
        in_specs=[far] * len(operands),
        out_specs=[spec] * len(outs),
        scratch_shapes=scratch,
        cost_estimate=pl.CostEstimate(
            flops=int(micros * 1.1e9), transcendentals=0, bytes_accessed=int(micros * 3.6e6)
        ),
        compiler_params=pltpu.CompilerParams(vmem_limit_bytes=24 * 2**20),
    )(*operands)


def planes_in(v, held, sems):
    chunks = []
    for c in range(4):
        rows = pl.ds(4 * c, 4)
        chunks.append(pltpu.make_async_copy(v.at[rows], held.at[rows], sems.at[c]))
    return chunks


def x_rims(vorticity):
    table, places = packed([["x1f"], ["r5f"], ["y1r"]])
    outs = [(2, 40, 512), (5, 32, 256), (5, 32, 768), (40, 512)]

    def kernel(v, small, q, qa, qb, qc, held, small_held, b, sems):
        chunks = planes_in(v, held, sems)
        small_copy = pltpu.make_async_copy(small, small_held, sems.at[4])
        for copy in chunks[:3] + [small_copy, chunks[3]]:
            copy.start()
        for copy in chunks[:3]:
            copy.wait()
        t = Tables(small_held, places)
        for n in range(5):
            b[n] = combine(BASIS[n], [lambda j=j: held[j] for j in range(10)])
        small_copy.wait()
        chunks[3].wait()
        rim = left(t("r5f"), b[...].reshape(320, 512))
        rows = left(t("y1r"), held[:, :16].reshape(256, 512))
        rim = right(jnp.concatenate([rim, rows], axis=0), t("x1f"))
        q[...] = rim[360:].reshape(2, 40, 512)
        qc[...] = rim[160:200]
        qa[...] = rim[:160, :256].reshape(5, 32, 256)
        qb[:, :, :256] = rim[:160, 256:].reshape(5, 32, 256)
        qb[:, :, 256:] = rim[200:360].reshape(5, 32, 512)

    return from_far(
        kernel,
        "x_rims",
        3.0,
        [jax.ShapeDtypeStruct(shape, F32) for shape in outs],
        [vorticity, jnp.asarray(table)],
        [
            pltpu.VMEM(vorticity.shape, F32),
            pltpu.VMEM(table.shape, BF16),
            pltpu.VMEM((5, 64, 512), F32),
            pltpu.SemaphoreType.DMA((5,)),
        ],
    )


def x_low(vorticity):
    table, places = packed([["x1fl"]])
    deep_table, _ = packed(DEEP)

    def kernel(v, small, large, f, deep, held, small_held, sems):
        chunks = planes_in(v, held, sems)
        small_copy = pltpu.make_async_copy(small, small_held, sems.at[4])
        deep_copy = pltpu.make_async_copy(large, deep, sems.at[5])
        for copy in [small_copy] + chunks + [deep_copy]:
            copy.start()
        small_copy.wait()
        t = Tables(small_held, places)
        for c in range(4):
            chunks[c].wait()
            part = held[4 * c : 4 * c + 4].reshape(256, 512)
            f[4 * c : 4 * c + 4] = right(part, t("x1fl")).reshape(4, 64, 256)
        deep_copy.wait()

    return from_far(
        kernel,
        "x_low",
        0.5,
        [
            jax.ShapeDtypeStruct((16, 64, 256), F32),
            jax.ShapeDtypeStruct(deep_table.shape, BF16),
        ],
        [vorticity, jnp.asarray(table), jnp.asarray(deep_table)],
        [
            pltpu.VMEM(vorticity.shape, F32),
            pltpu.VMEM(table.shape, BF16),
            pltpu.SemaphoreType.DMA((6,)),
        ],
    )


def x_high(v, t, f):
    for c in range(4):
        part = v[4 * c : 4 * c + 4].reshape(256, 512)
        f[4 * c : 4 * c + 4] = right(part, t("x1fh")).reshape(4, 64, 256)


def deep_split(f, q, qa, qc, t, own, m1, m2, m3, g, low):
    for half in range(2):
        extra = left(t("y1ul"), taller(q[half, :, :256], 8))
        for c in range(2):
            z = 8 * half + 4 * c
            part = left(t("y1l"), f[z : z + 4].reshape(256, 256))
            g[z : z + 4] = (part + extra[128 * c : 128 * c + 128]).reshape(4, 32, 256)
    rim = qa[...].reshape(160, 256) + left(t("r5ul"), qc[:, :256])
    rim = rim.reshape(5, 32, 256)
    for i in range(8):
        plane = combine(Z1LO[i], [lambda j=j: g[j] for j in range(16)])
        if i >= 3:
            plane = plane + combine(SPREAD[i - 3], [lambda n=n: rim[n] for n in range(5)])
        low[i] = plane
    wide = right(low[...].reshape(256, 256), t("xmf"))
    rim = left(t("y2q"), wide[:, :256])
    m1[256:320] = rim[:, :128]
    m1[320:384] = rim[:, 128:]
    rest = left(t("y34"), jnp.concatenate([wide[:, 256:384], wide[:, 384:]], axis=0))
    own[:, 256:] = rest[:256]
    m1[:256] = rest[256:512]
    m2[...] = rest[512:576]
    m3[...] = rest[576:592]
    own[:, :256] = left(t("y2"), wide[:, :256])


def y_gather(own, m1, m2, m3, index, t, p0, p1, p2, p3, w):
    rim = jnp.concatenate([m1[256:320], m1[320:384]], axis=1)
    w[:, :256] = own[:, :256] + left(t("y2u"), rim)
    far = jnp.concatenate([m2[...], m3[...]], axis=0)
    w[:, 256:] = own[:, 256:] + m1[:256] + left(t("y34p"), far)
    for s, piece in enumerate((p0, p1, p2, p3)):
        piece[...] = w[block(index, s)]


def z_split(p0, p1, p2, p3, index, t, own2, own34, n1, n2, n3, w):
    for s, piece in enumerate((p0, p1, p2, p3)):
        w[block(index, -s)] = piece[...]
    rim = left(t("z2q"), w[:, :256])
    n1[128:168] = rim[:40, :128]
    n1[168:208] = rim[:40, 128:]
    rest = left(t("z34"), w[:, 256:])
    own34[...] = rest[:128]
    n1[:128] = rest[128:256]
    n2[...] = rest[256:272]
    n3[...] = rest[272:280]
    own2[...] = left(t("z2"), w[:, :256])


def mask_pack(two, three, four, coarse, index, k0, k2, near, full):
    def plain(ref, b, z):
        if b == 0:
            return jnp.zeros(ref.shape[2:], F32)
        return ref[b - 1, z].astype(F32)

    for bz in range(2):
        for z in range(4):
            for bx in range(2):
                rows = [plain(two, 4 * bz + 2 * by + bx, z) for by in range(2)]
                at = bx * 64 + (bz * 4 + z) * 8
                for m in range(4):
                    full[m, at : at + 8] = jnp.concatenate(
                        [part[4 * m : 4 * m + 4] for part in rows], axis=0
                    )
        for z in range(2):
            rows = [
                jnp.concatenate([plain(three, 4 * bz + 2 * by + bx, z) for bx in range(2)], axis=1)
                for by in range(2)
            ]
            at = 128 + (bz * 2 + z) * 8
            for m in range(4):
                parts = [part[2 * m : 2 * m + 2] for part in rows]
                full[m, at : at + 8] = jnp.concatenate(parts + [jnp.zeros((4, 128), F32)], axis=0)
        rows = []
        for by in range(2):
            parts = [
                coarse[0].astype(F32) if bz + by + bx == 0 else plain(four, 4 * bz + 2 * by + bx, 0)
                for bx in range(2)
            ]
            rows.append(jnp.concatenate(parts + [jnp.zeros((4, 64), F32)], axis=1))
        at = 160 + bz * 8
        for m in range(4):
            parts = [jnp.zeros((4, 128), F32)] + [part[m : m + 1] for part in rows]
            full[m, at : at + 8] = jnp.concatenate(parts + [jnp.zeros((2, 128), F32)], axis=0)
    k0[...] = full[index[0]]
    k2[...] = full[lax.bitwise_xor(index[0], 2)]
    for n in range(2):
        near[n] = full[lax.bitwise_xor(index[0], 2 * n + 1)]


def z_mask(own2, own34, n1, n2, n3, k0, near, away, index, t, c2, c34, s1, s2, s3, full, keep2):
    full[index[0]] = k0[...]
    full[lax.bitwise_xor(index[0], 1)] = near[0]
    for n in range(2):
        full[lax.bitwise_xor(index[0], 2 + n)] = away[n]
    for a in range(4):
        for bz in range(2):
            for bx in range(2):
                at = bz * 128 + a * 32
                rows = full[a, bx * 64 + bz * 32 : bx * 64 + bz * 32 + 32]
                keep2[at : at + 32, bx * 128 : bx * 128 + 128] = rows
    tiles = []
    for slot in range(16):
        bz, a, z = slot // 8, slot // 2 % 4, slot % 2
        tile = full[a, 128 + (bz * 2 + z) * 8 : 136 + (bz * 2 + z) * 8]
        if slot < 8:
            bz, a = slot // 4, slot % 4
            tile = tile + full[a, 160 + bz * 8 : 168 + bz * 8]
        tiles.append(tile)
    keep34 = jnp.concatenate(tiles, axis=0)

    far = taller(jnp.concatenate([n2[...], n3[...]], axis=0), 8)
    part34 = (own34[...] + n1[:128] + left(t("z34p"), far)) * keep34
    c34[...] = part34
    s1[:128] = part34
    back = left(t("z34pt"), part34)
    s2[...] = back[:16]
    s3[...] = back[16:24]
    rim = taller(jnp.concatenate([n1[128:168], n1[168:208]], axis=1), 8)
    part2 = (own2[...] + left(t("z2u"), rim)) * keep2[...]
    c2[...] = part2
    back = left(t("z2ut"), part2)
    s1[128:168] = back[:40, :128]
    s1[168:208] = back[:40, 128:]


def z_join(c2, c34, s1, s2, s3, index, t, p0, p1, p2, p3, w):
    rim = taller(jnp.concatenate([s1[128:168], s1[168:208]], axis=1), 8)
    w[:, :256] = left(t("z2t"), c2[...]) + left(t("z2qt"), rim)
    rows = jnp.concatenate([c34[...], s1[:128], s2[...], s3[...]], axis=0)
    w[:, 256:] = left(t("z34t"), taller(rows, 8))
    for s, piece in enumerate((p0, p1, p2, p3)):
        piece[...] = w[block(index, s)]


def y_send(p0, p1, p2, p3, index, t, w, m1, m2, m3):
    for s, piece in enumerate((p0, p1, p2, p3)):
        w[block(index, -s)] = piece[...]
    m1[:256] = w[:, 256:]
    rim = left(t("y2ut"), w[:, :256])
    m1[256:320] = rim[:, :128]
    m1[320:384] = rim[:, 128:]
    far = left(t("y34pt"), w[:, 256:])
    m2[...] = far[:64]
    m3[...] = far[64:]


def deep_join(w, m1, m2, m3, da, dy, dc, t, g, pa, py, pc, low):
    rim = jnp.concatenate([m1[256:320], m1[320:384]], axis=1)
    first = left(t("y2t"), w[:, :256]) + left(t("y2qt"), rim)
    rows = [w[:, 256:], m1[:256], m2[...], m3[...]]
    rest = left(t("y34t"), jnp.concatenate(rows, axis=0))
    wide = jnp.concatenate([first, rest[:256], rest[256:]], axis=1)
    low[...] = right(wide, t("xmi")).reshape(8, 32, 256)
    planes = [
        combine(SPREAD[:5, n], [lambda i=i: low[i + 3] for i in range(5)]) for n in range(5)
    ]
    for z in range(16):
        g[z] = combine(Z1LO[:, z], [lambda i=i: low[i] for i in range(8)])
    for n in range(5):
        pa[n] = da[n] + planes[n]
    corner = left(t("r5ult"), jnp.concatenate(planes, axis=0))
    pc[:, :256] = dc[:, :256] + corner
    pc[:, 256:] = dc[:, 256:]
    for half in range(2):
        part = g[8 * half : 8 * half + 8].reshape(256, 256)
        py[half, :, :256] = dy[half, :, :256] + left(t("y1ult"), part)[:40]
        py[half, :, 256:] = dy[half, :, 256:]


def own_join(g, low, pb, t, out):
    for c in range(4):
        planes = []
        for z in range(4 * c, 4 * c + 4):
            rest = [g[z, :32, 256:], g[z, 32:]]
            if z < 10:
                rim = combine(BASIS[:, z], [lambda n=n: pb[n] for n in range(5)])
                rest = [rest[0] + rim[:, :256], rest[1] + rim[:, 256:]]
            corner = g[z, :32, :256] + low[z]
            planes += [jnp.concatenate([corner, rest[0]], axis=1), rest[1]]
        part = left(t("y1i"), jnp.concatenate(planes, axis=0))
        out[4 * c : 4 * c + 4] = right(part, t("x1i")).reshape(4, 64, 512)


def finish(base, pa, py, pc, t, out, rz, chunks):
    x1l = [part[:256] for part in t("x1i")]
    rz[...] = right(left(t("r5il"), pa[...].reshape(160, 256)), x1l).reshape(5, 64, 512)
    far = left(t("r5z"), pc[...])
    rims = [taller(py[half], 8) + far[48 * half : 48 * half + 48] for half in range(2)]
    rims = right(jnp.concatenate(rims, axis=0), t("x1i"))
    for half in range(2):
        extra = left(t("y1qt"), rims[48 * half : 48 * half + 48]).reshape(8, 64, 512)
        for k in range(8):
            z = 8 * half + k
            plane = base[z] + extra[k]
            if z < 10:
                plane = plane + combine(BASIS[:, z], [lambda n=n: rz[n] for n in range(5)])
            out[z] = plane
            if z % 4 == 3:
                chunks[z // 4].start()
    for copy in chunks:
        copy.wait()


def details(fl, fh, q, qa, qb, qc, keep, t, g, da, db, kept):
    for half in range(2):
        extra = left(t("y1u"), taller(q[half], 8))
        for c in range(2):
            z = 8 * half + 4 * c
            part = jnp.concatenate([fl[z : z + 4], fh[z : z + 4]], axis=2)
            part = left(t("y1f"), part.reshape(256, 512))
            g[z : z + 4] = (part + extra[256 * c : 256 * c + 256]).reshape(4, 64, 512)
    top = jnp.concatenate([qa[...], qb[:, :, :256]], axis=2)
    planes = jnp.concatenate([top, qb[:, :, 256:]], axis=1)
    planes = planes + left(t("r5u"), qc[...]).reshape(5, 64, 512)
    for c in range(4):
        rows = slice(16 * c, 16 * c + 16)
        rim = planes[:, rows].reshape(80, 512)
        out = left(t("z1f"), g[:, rows].reshape(256, 512)) + left(t("z1u"), rim)
        out = out.reshape(16, 16, 512)
        by = c // 2
        at = slice(16 * (c % 2), 16 * (c % 2) + 16)
        for bz in range(2):
            for bx in range(2):
                cols = slice(256 * bx, 256 * bx + 256)
                number = 4 * bz + 2 * by + bx
                if number:
                    mask = keep[number - 1, :, at].astype(F32)
                    part = out[8 * bz : 8 * bz + 8, :, cols] * mask
                else:
                    part = jnp.zeros((8, 16, 256), F32)
                kept[8 * bz : 8 * bz + 8, rows, cols] = part
    for n in range(5):
        plane = combine(SPREAD[:5, n], [lambda i=i: kept[i + 3] for i in range(5)])
        plane = plane + combine(SPREAD[5:, n], [lambda i=i: kept[i + 11] for i in range(5)])
        da[n] = plane[:32, :256]
        db[n, :, :256] = plane[:32, 256:]
        db[n, :, 256:] = plane[32:]
    for c in range(4):
        rows = slice(16 * c, 16 * c + 16)
        out = left(t("z1i"), kept[:, rows].reshape(256, 512))
        g[:, rows] = out.reshape(16, 16, 512)


def details_rim(g, da, db, t, py, pc):
    top = jnp.concatenate([da[...], db[:, :, :256]], axis=2)
    planes = jnp.concatenate([top, db[:, :, 256:]], axis=1)
    pc[...] = left(t("r5ut"), planes.reshape(320, 512))
    for half in range(2):
        part = g[8 * half : 8 * half + 8].reshape(512, 512)
        py[half] = left(t("y1ut"), part)[:40]


def moved(value, by_z, by_y):
    pairs = [
        (z * GY + y, (z + by_z) % GZ * GY + (y + by_y) % GY) for z in range(GZ) for y in range(GY)
    ]
    return lax.ppermute(value, ("gz", "gy"), pairs)


def across(value, flip):
    return lax.ppermute(value, "gz", [(z, z ^ flip) for z in range(GZ)])


def exchanged(pieces):
    out = [pieces[0]]
    for s in range(1, MEMBERS):
        pairs = [(z, z // MEMBERS * MEMBERS + (z + s) % MEMBERS) for z in range(GZ)]
        out.append(lax.ppermute(pieces[s], "gz", pairs))
    return out


def on_device(vorticity, keep_one, keep_two, keep_three, keep_four, keep_coarse):
    index = lax.rem(lax.axis_index("gz"), MEMBERS).astype(jnp.int32).reshape(1)
    piece, half = (64, 384), (40, 512)

    q, qa, qb, qc = x_rims(vorticity)
    vorticity, q, qa, qb, qc = lax.optimization_barrier((vorticity, q, qa, qb, qc))
    q, qa, qc = moved(q, 0, -1), moved(qa, -1, 0), moved(qc, -1, -1)
    qb = moved(qb, -1, 0)
    f, deep = x_low(vorticity)
    own, m1, m2, m3 = call(
        deep_split,
        3.0,
        [(256, 384), (384, 128), (64, 128), (16, 128)],
        f,
        q,
        qa,
        qc,
        shelves=DEEP,
        table=deep,
        scratch=[(16, 32, 256), (8, 32, 256)],
    )
    vorticity, late, m1, m2, m3 = lax.optimization_barrier((vorticity, index, m1, m2, m3))
    m1, m2, m3 = moved(m1, 0, -1), moved(m2, 0, -2), moved(m3, 0, -3)
    (fh,) = call(x_high, 0.3, [(16, 64, 256)], vorticity, shelves=[["x1fh"]])
    k0, k2, near = call(
        mask_pack,
        0.1,
        [(176, 128), (176, 128), (2, 176, 128)],
        keep_two,
        keep_three,
        keep_four,
        keep_coarse,
        index=late,
        scratch=[(4, 176, 128)],
    )
    near = across(near, 1)
    own, fh, near = lax.optimization_barrier((own, fh, near))
    away = jnp.stack([k2, near[1]])

    pieces = call(
        y_gather,
        0.7,
        [piece] * 4,
        own,
        m1,
        m2,
        m3,
        index=index,
        shelves=[["y2u", "y34p"]],
        scratch=[(256, 384)],
    )
    pieces = exchanged(pieces)
    own2, own34, n1, n2, n3 = call(
        z_split,
        0.5,
        [(256, 256), (128, 128), (208, 128), (16, 128), (8, 128)],
        *pieces,
        index=index,
        shelves=[["z2", "z34"], ["z2q"]],
        scratch=[(256, 384)],
    )
    fh, away, n1, n2, n3 = lax.optimization_barrier((fh, away, n1, n2, n3))
    n1, n2, n3 = moved(n1, -4, 0), moved(n2, -8, 0), moved(n3, -12, 0)
    away = across(away, 2)
    g, da, db = call(
        details,
        0.5,
        [(16, 64, 512), (5, 32, 256), (5, 32, 768)],
        f,
        fh,
        q,
        qa,
        qb,
        qc,
        keep_one,
        shelves=[["y1f", "z1f", "z1i", "z1u"], ["y1u", "r5u"]],
        scratch=[(16, 64, 512)],
    )
    own2, g = lax.optimization_barrier((own2, g))

    c2, c34, s1, s2, s3 = call(
        z_mask,
        0.7,
        [(256, 256), (128, 128), (208, 128), (16, 128), (8, 128)],
        own2,
        own34,
        n1,
        n2,
        n3,
        k0,
        near,
        away,
        index=index,
        shelves=[["z2u"], ["z34p", "z34pt", "z2ut"]],
        scratch=[(4, 176, 128), (256, 256)],
    )
    g, db, s1, s2, s3 = lax.optimization_barrier((g, db, s1, s2, s3))
    s1, s2, s3 = moved(s1, 4, 0), moved(s2, 8, 0), moved(s3, 12, 0)
    pb = moved(db, 1, 0)
    dy, dc = call(
        details_rim, 0.3, [(2, 40, 512), half], g, da, db, shelves=[["y1ut"], ["r5ut"]]
    )
    c2, dy, pb = lax.optimization_barrier((c2, dy, pb))
    pieces = call(
        z_join,
        0.8,
        [piece] * 4,
        c2,
        c34,
        s1,
        s2,
        s3,
        index=index,
        shelves=[["z2t", "z34t", "z2qt"]],
        scratch=[(256, 384)],
    )
    pieces = exchanged(pieces)
    w, m1, m2, m3 = call(
        y_send,
        0.4,
        [(256, 384), (384, 128), (64, 128), (16, 128)],
        *pieces,
        index=index,
        shelves=[["y2ut"], ["y34pt"]],
    )
    m1, m2, m3 = moved(m1, 0, 1), moved(m2, 0, 2), moved(m3, 0, 3)
    low, pa, py, pc = call(
        deep_join,
        2.5,
        [(16, 32, 256), (5, 32, 256), (2, 40, 512), half],
        w,
        m1,
        m2,
        m3,
        da,
        dy,
        dc,
        shelves=[["y34t"], ["xmi", "y2t"], ["y2qt", "y1ult", "r5ult"]],
        scratch=[(8, 32, 256)],
    )
    pa, py, pc = moved(pa, 1, 0), moved(py, 0, 1), moved(pc, 1, 1)
    (base,) = call(
        own_join, 0.5, [(16, 64, 512)], g, low, pb, shelves=[["x1i"], ["y1i"]]
    )
    (out,) = call(
        finish,
        2.0,
        [(16, 64, 512)],
        base,
        pa,
        py,
        pc,
        shelves=[["x1i"], ["y1qt", "r5z"], ["r5il"]],
        scratch=[(5, 64, 512)],
        streamed=True,
    )
    return out


def solution(mesh):
    in_specs = (
        P("gz", "gy", None),
        P(None, "gz", "gy", None),
        P(None, "gz", "gy", None),
        P(None, "gz", "gy", None),
        P(None, "gz", "gy", None),
        P("gz", "gy", None),
    )
    out_specs = P("gz", "gy", None)
    return jax.shard_map(
        on_device, mesh=mesh, in_specs=in_specs, out_specs=out_specs, check_vma=False
    )
```

```python
import functools

import jax
import jax.numpy as jnp
import ml_dtypes
import numpy as np
from jax import lax
from jax.experimental import pallas as pl
from jax.experimental.pallas import tpu as pltpu
from jax.sharding import PartitionSpec as P

low_taps = (
    0.11154074335008017,
    0.4946238903983854,
    0.7511339080215775,
    0.3152503517092432,
    -0.22626469396516913,
    -0.12976686756709563,
    0.09750160558707936,
    0.02752286553001629,
    -0.031582039318031156,
    0.0005538422009938016,
    0.004777257511010651,
    -0.00107730108499558,
)
high_taps = tuple(((-1.0) ** k * low_taps[11 - k] for k in range(12)))

GZ, GY = 32, 8
MEMBERS = 4
F32, BF16 = jnp.float32, jnp.bfloat16


def tail_of(s):
    return (s + 11) // 2


def band(taps, n, s):
    t = tail_of(s)
    out = np.zeros((t + n // 2, s + n))
    for row in range(t + n // 2):
        for col in range(s + n):
            k = (col - s) - 2 * (row - t)
            if 0 <= k < 12:
                out[row, col] = taps[k]
    return out


def periodic(taps, n):
    out = np.zeros((n // 2, n))
    for i in range(n // 2):
        for k in range(12):
            out[i, (2 * i + k) % n] += taps[k]
    return out


def rank_five():
    block = np.concatenate([band(low_taps, 10, 0)[:5], band(high_taps, 10, 0)[:5]])
    u, sing, vt = np.linalg.svd(block)
    return u[:, :5] * sing[:5], vt[:5]


def pair(matrix):
    high = matrix.astype(ml_dtypes.bfloat16)
    low = (matrix - high.astype(np.float64)).astype(ml_dtypes.bfloat16)
    return np.stack([high, low])


def padded(matrix, rows, cols):
    out = np.zeros((rows, cols))
    out[: matrix.shape[0], : matrix.shape[1]] = matrix
    return out


@functools.lru_cache(None)
def tables():
    spread, basis = rank_five()
    mats = {}
    x1 = np.concatenate([periodic(low_taps, 512), periodic(high_taps, 512)])
    mats["x1f"], mats["x1i"], mats["x1l"] = x1.T, x1, x1[:256]
    lo2 = periodic(low_taps, 256)
    lo3 = periodic(low_taps, 128) @ lo2
    xm = np.concatenate(
        [
            lo2,
            periodic(high_taps, 256),
            lo3,
            periodic(high_taps, 128) @ lo2,
            periodic(low_taps, 64) @ lo3,
            periodic(high_taps, 64) @ lo3,
            np.zeros((64, 256)),
        ]
    )
    mats["xmf"], mats["xmi"] = xm.T, xm
    y1 = np.concatenate([band(low_taps, 64, 0)[5:], band(high_taps, 64, 0)[5:]])
    mats["y1f"] = np.kron(np.eye(4), y1)
    mats["y1i"] = mats["y1f"].T
    pick = padded(basis, 5, 64)
    mats["y1q"] = padded(np.kron(np.eye(8), pick), 48, 512)
    mats["y1qt"] = mats["y1q"].T
    put = np.zeros((64, 5))
    put[27:32], put[59:64] = spread[:5], spread[5:]
    mats["y1u"] = padded(np.kron(np.eye(8), put), 512, 48)
    mats["y1ut"] = mats["y1u"].T
    mats["y1l"] = np.kron(np.eye(4), y1[:32])
    mats["y1lt"] = mats["y1l"].T
    mats["y1ul"] = padded(np.kron(np.eye(8), put[:32]), 256, 48)
    mats["y1ult"] = mats["y1ul"].T
    corner = np.kron(np.eye(5), padded(pick, 8, 64))
    lows, highs = np.kron(np.eye(5), y1[:32]), np.kron(np.eye(5), y1[32:])
    mats["r5f"] = np.concatenate([lows, corner, highs])
    mats["r5i"] = np.kron(np.eye(5), y1.T)
    mats["r5il"] = np.kron(np.eye(5), y1[:32].T)
    mats["y1r"] = np.kron(np.eye(16), padded(basis, 5, 16))
    mats["r5u"] = np.kron(np.eye(5), padded(put, 64, 8))
    mats["r5ut"] = mats["r5u"].T
    mats["r5ul"] = np.kron(np.eye(5), padded(put[:32], 32, 8))
    mats["r5ult"] = mats["r5ul"].T
    far = np.zeros((2, 48, 40))
    for z in range(10):
        for k in range(5):
            far[z // 8, (z % 8) * 5 + k, k::8] = basis[:, z]
    mats["r5z"] = far.reshape(96, 40)
    z1 = np.concatenate([band(low_taps, 16, 0)[5:], band(high_taps, 16, 0)[5:]])
    mats["z1f"] = np.kron(z1, np.eye(16))
    mats["z1i"] = mats["z1f"].T
    zput = np.zeros((16, 5))
    zput[3:8], zput[11:16] = spread[:5], spread[5:]
    mats["z1u"] = np.kron(zput, np.eye(16))
    zpick = padded(basis, 5, 16)
    mats["z1qt"] = np.kron(zpick.T, np.eye(16))
    lo_a = band(low_taps, 32, 0)
    lo_b = band(low_taps, 16, 5) @ lo_a
    lev2 = [lo_a, band(high_taps, 32, 0)]
    lev3 = [lo_b, band(high_taps, 16, 5) @ lo_a]
    lev4 = [band(low_taps, 8, 8) @ lo_b, band(high_taps, 8, 8) @ lo_b]

    def row2(b, i):
        return lev2[b][i + 5]

    def row3(b, i):
        return lev3[b][i + 8]

    def row4(b, i):
        return lev4[b][i + 9]

    pick32 = padded(basis, 5, 32)
    put2 = np.zeros((2, 16, 5))
    put2[0, 11:], put2[1, 11:] = spread[:5], spread[5:]

    y2 = np.zeros((256, 256))
    y2u = np.zeros((256, 64))
    y34 = np.zeros((592, 512))
    y2q = np.kron(np.eye(8), padded(pick32, 8, 32))
    for m in range(4):
        for z in range(8):
            cells = slice(z * 32, z * 32 + 32)
            cells4 = slice(256 + z * 32, 256 + z * 32 + 32)
            for r in range(8):
                row = (m * 8 + z) * 8 + r
                y2[row, cells] = row2(r // 4, 4 * m + r % 4)
                y2u[row, z * 8 : z * 8 + 5] = put2[r // 4, 4 * m + r % 4]
                if r < 4:
                    y34[row, cells] = row3(r // 2, 2 * m + r % 2)
                    y34[256 + row, cells] = row3(r // 2, 2 * m + r % 2 - 8)
                elif r < 6:
                    y34[row, cells4] = row4(r - 4, m)
                    y34[256 + row, cells4] = row4(r - 4, m - 4)
    y34p = np.zeros((256, 80))
    for z in range(8):
        cells4 = slice(256 + z * 32, 256 + z * 32 + 32)
        for by in range(2):
            for i in range(4):
                y34[512 + z * 8 + by * 4 + i, cells4] = row4(by, i - 8)
                y34p[(i * 8 + z) * 8 + 4 + by, z * 8 + by * 4 + i] = 1.0
            y34[576 + z * 2 + by, cells4] = row4(by, -9)
            y34p[(3 * 8 + z) * 8 + 4 + by, 64 + z * 2 + by] = 1.0
    mats["y2"], mats["y2t"] = y2, y2.T
    mats["y2u"], mats["y2ut"] = y2u, y2u.T
    mats["y2q"], mats["y2qt"] = y2q, y2q.T
    mats["y34"], mats["y34t"] = y34, y34.T
    mats["y34p"], mats["y34pt"] = y34p, y34p.T

    eye8 = np.eye(8)
    z2 = np.kron(np.array([row2(b, i) for b in range(2) for i in range(16)]), eye8)
    z2q = padded(np.kron(pick32, eye8), 48, 256)
    z2u = padded(np.kron(put2.reshape(32, 5), eye8), 256, 48)
    z34 = np.zeros((288, 32, 8))
    z34p = np.zeros((128, 32))
    for b in range(2):
        for i in range(8):
            for r in range(4):
                z34[(b * 8 + i) * 8 + r, :, r] = row3(b, i)
                z34[128 + (b * 8 + i) * 8 + r, :, r] = row3(b, i - 8)
        for by in range(2):
            for i in range(4):
                slot = b * 4 + i
                z34[slot * 8 + 4 + by, :, 4 + by] = row4(b, i)
                z34[128 + slot * 8 + 4 + by, :, 4 + by] = row4(b, i - 4)
                z34[256 + slot * 2 + by, :, 4 + by] = row4(b, i - 8)
                z34p[slot * 8 + 4 + by, slot * 2 + by] = 1.0
            z34[272 + b * 2 + by, :, 4 + by] = row4(b, -9)
            z34p[(b * 4 + 3) * 8 + 4 + by, 16 + b * 2 + by] = 1.0
    z34 = z34.reshape(288, 256)
    mats["z2"], mats["z2t"] = z2, z2.T
    mats["z2q"], mats["z2qt"] = z2q, z2q.T
    mats["z2u"], mats["z2ut"] = z2u, z2u.T
    mats["z34"], mats["z34t"] = z34, z34.T
    mats["z34p"], mats["z34pt"] = z34p, z34p.T
    return mats


SPREAD, BASIS = rank_five()
Z1LO = band(low_taps, 16, 0)[5:]


def packed(shelves):
    mats = tables()
    places, rows, width = {}, 0, 0
    for shelf in shelves:
        col = tall = 0
        for name in shelf:
            height, wide = mats[name].shape
            places[name] = (rows, height, col, wide)
            col += -(-wide // 128) * 128
            tall = max(tall, -(-height // 16) * 16)
        rows, width = rows + tall, max(width, col)
    out = np.zeros((rows, width))
    for name, (row, height, col, wide) in places.items():
        out[row : row + height, col : col + wide] = mats[name]
    return pair(out), places


class Tables:
    def __init__(self, ref, places):
        self.ref, self.places = ref, places

    def __call__(self, name):
        row, height, col, wide = self.places[name]
        return [self.ref[k, row : row + height, col : col + wide] for k in range(2)]


SPREAD, BASIS = rank_five()
Z1LO = band(low_taps, 16, 0)[5:]


def halves(value):
    high = value.astype(BF16)
    return high, (value - high.astype(F32)).astype(BF16)


def dot(a, b):
    return lax.dot_general(a, b, (((1,), (0,)), ((), ())), preferred_element_type=F32)


def left(table, value):
    vh, vl = halves(value)
    return dot(table[0], vh) + dot(table[0], vl) + dot(table[1], vh)


def right(value, table):
    vh, vl = halves(value)
    return dot(vh, table[0]) + dot(vl, table[0]) + dot(vh, table[1])


def combine(weights, planes):
    total = None
    for weight, plane in zip(weights, planes):
        if weight == 0.0:
            continue
        term = float(weight) * plane()
        total = term if total is None else total + term
    return total


def taller(value, rows):
    return jnp.concatenate([value, jnp.zeros((rows, value.shape[1]), F32)], axis=0)


def call(kernel, micros, outs, *operands, shelves=None, index=None, scratch=(), table=None, streamed=False):
    spec, far = pl.BlockSpec(memory_space=pltpu.VMEM), pl.BlockSpec(memory_space=pltpu.HBM)
    specs = [spec] * len(operands)
    out_specs = [spec] * len(outs)
    operands = list(operands)
    places = None
    scratch = [pltpu.VMEM(shape, F32) for shape in scratch]
    if index is not None:
        operands.append(index)
        specs.append(pl.BlockSpec(memory_space=pltpu.SMEM))
    if shelves is not None:
        packed_table, places = packed(shelves)
        operands.append(jnp.asarray(packed_table) if table is None else table)
        specs.append(spec)
    if streamed:
        out_specs = [far] * len(outs)
        scratch += [pltpu.VMEM(outs[0], F32), pltpu.SemaphoreType.DMA((4,))]

    def body(*refs):
        refs = list(refs)
        count = len(operands)
        if streamed:
            held, sems = refs[-2:]
            target = refs[count]
            chunks = []
            for c in range(4):
                rows = pl.ds(4 * c, 4)
                chunks.append(pltpu.make_async_copy(held.at[rows], target.at[rows], sems.at[c]))
            refs[count] = held
            refs = refs[:-2] + [chunks]
        if places is not None:
            refs[count - 1] = Tables(refs[count - 1], places)
        kernel(*refs)

    return pl.pallas_call(
        body,
        name=kernel.__name__,
        out_shape=[jax.ShapeDtypeStruct(shape, F32) for shape in outs],
        in_specs=specs,
        out_specs=out_specs,
        scratch_shapes=scratch,
        cost_estimate=pl.CostEstimate(
            flops=int(micros * 1.1e9), transcendentals=0, bytes_accessed=int(micros * 3.6e6)
        ),
        compiler_params=pltpu.CompilerParams(vmem_limit_bytes=24 * 2**20),
    )(*operands)


def member(index, by):
    return lax.rem(index[0] + by + MEMBERS, MEMBERS)


def block(index, by, rows=64):
    return pl.ds(pl.multiple_of(member(index, by) * rows, rows), rows)


DEEP = [["y34"], ["xmf"], ["y2", "y1l"], ["y1ul", "r5ul", "y2q"]]


def from_far(kernel, name, micros, outs, operands, scratch):
    spec, far = pl.BlockSpec(memory_space=pltpu.VMEM), pl.BlockSpec(memory_space=pltpu.HBM)
    operands = [pltpu.with_memory_space_constraint(part, pltpu.HBM) for part in operands]
    return pl.pallas_call(
        kernel,
        name=name,
        out_shape=outs,
        in_specs=[far] * len(operands),
        out_specs=[spec] * len(outs),
        scratch_shapes=scratch,
        cost_estimate=pl.CostEstimate(
            flops=int(micros * 1.1e9), transcendentals=0, bytes_accessed=int(micros * 3.6e6)
        ),
        compiler_params=pltpu.CompilerParams(vmem_limit_bytes=24 * 2**20),
    )(*operands)


def planes_in(v, held, sems):
    chunks = []
    for c in range(4):
        rows = pl.ds(4 * c, 4)
        chunks.append(pltpu.make_async_copy(v.at[rows], held.at[rows], sems.at[c]))
    return chunks


def x_rims(vorticity):
    table, places = packed([["x1f"], ["r5f"], ["y1r"]])
    outs = [(2, 40, 512), (5, 32, 256), (5, 32, 768), (40, 512)]

    def kernel(v, small, q, qa, qb, qc, held, small_held, b, sems):
        chunks = planes_in(v, held, sems)
        small_copy = pltpu.make_async_copy(small, small_held, sems.at[4])
        for copy in chunks[:3] + [small_copy, chunks[3]]:
            copy.start()
        for copy in chunks[:3]:
            copy.wait()
        t = Tables(small_held, places)
        for n in range(5):
            b[n] = combine(BASIS[n], [lambda j=j: held[j] for j in range(10)])
        small_copy.wait()
        chunks[3].wait()
        rim = left(t("r5f"), b[...].reshape(320, 512))
        rows = left(t("y1r"), held[:, :16].reshape(256, 512))
        rim = right(jnp.concatenate([rim, rows], axis=0), t("x1f"))
        q[...] = rim[360:].reshape(2, 40, 512)
        qc[...] = rim[160:200]
        qa[...] = rim[:160, :256].reshape(5, 32, 256)
        qb[:, :, :256] = rim[:160, 256:].reshape(5, 32, 256)
        qb[:, :, 256:] = rim[200:360].reshape(5, 32, 512)

    return from_far(
        kernel,
        "x_rims",
        3.0,
        [jax.ShapeDtypeStruct(shape, F32) for shape in outs],
        [vorticity, jnp.asarray(table)],
        [
            pltpu.VMEM(vorticity.shape, F32),
            pltpu.VMEM(table.shape, BF16),
            pltpu.VMEM((5, 64, 512), F32),
            pltpu.SemaphoreType.DMA((5,)),
        ],
    )


def x_split(vorticity):
    table, places = packed([["x1f"]])
    deep_table, _ = packed(DEEP)

    def kernel(v, small, large, f, deep, held, small_held, sems):
        chunks = planes_in(v, held, sems)
        small_copy = pltpu.make_async_copy(small, small_held, sems.at[4])
        deep_copy = pltpu.make_async_copy(large, deep, sems.at[5])
        for copy in [small_copy] + chunks + [deep_copy]:
            copy.start()
        small_copy.wait()
        t = Tables(small_held, places)
        for c in range(4):
            chunks[c].wait()
            part = held[4 * c : 4 * c + 4].reshape(256, 512)
            f[4 * c : 4 * c + 4] = right(part, t("x1f")).reshape(4, 64, 512)
        deep_copy.wait()

    return from_far(
        kernel,
        "x_split",
        0.5,
        [
            jax.ShapeDtypeStruct(vorticity.shape, F32),
            jax.ShapeDtypeStruct(deep_table.shape, BF16),
        ],
        [vorticity, jnp.asarray(table), jnp.asarray(deep_table)],
        [
            pltpu.VMEM(vorticity.shape, F32),
            pltpu.VMEM(table.shape, BF16),
            pltpu.SemaphoreType.DMA((6,)),
        ],
    )


def deep_split(f, q, qa, qc, t, own, m1, m2, m3, g, low):
    for half in range(2):
        extra = left(t("y1ul"), taller(q[half, :, :256], 8))
        for c in range(2):
            z = 8 * half + 4 * c
            part = left(t("y1l"), f[z : z + 4, :, :256].reshape(256, 256))
            g[z : z + 4] = (part + extra[128 * c : 128 * c + 128]).reshape(4, 32, 256)
    rim = qa[...].reshape(160, 256) + left(t("r5ul"), qc[:, :256])
    rim = rim.reshape(5, 32, 256)
    for i in range(8):
        plane = combine(Z1LO[i], [lambda j=j: g[j] for j in range(16)])
        if i >= 3:
            plane = plane + combine(SPREAD[i - 3], [lambda n=n: rim[n] for n in range(5)])
        low[i] = plane
    wide = right(low[...].reshape(256, 256), t("xmf"))
    rim = left(t("y2q"), wide[:, :256])
    m1[256:320] = rim[:, :128]
    m1[320:384] = rim[:, 128:]
    rest = left(t("y34"), jnp.concatenate([wide[:, 256:384], wide[:, 384:]], axis=0))
    own[:, 256:] = rest[:256]
    m1[:256] = rest[256:512]
    m2[...] = rest[512:576]
    m3[...] = rest[576:592]
    own[:, :256] = left(t("y2"), wide[:, :256])


def y_gather(own, m1, m2, m3, index, t, p0, p1, p2, p3, w):
    rim = jnp.concatenate([m1[256:320], m1[320:384]], axis=1)
    w[:, :256] = own[:, :256] + left(t("y2u"), rim)
    far = jnp.concatenate([m2[...], m3[...]], axis=0)
    w[:, 256:] = own[:, 256:] + m1[:256] + left(t("y34p"), far)
    for s, piece in enumerate((p0, p1, p2, p3)):
        piece[...] = w[block(index, s)]


def z_split(p0, p1, p2, p3, index, t, own2, own34, n1, n2, n3, w):
    for s, piece in enumerate((p0, p1, p2, p3)):
        w[block(index, -s)] = piece[...]
    rim = left(t("z2q"), w[:, :256])
    n1[128:168] = rim[:40, :128]
    n1[168:208] = rim[:40, 128:]
    rest = left(t("z34"), w[:, 256:])
    own34[...] = rest[:128]
    n1[:128] = rest[128:256]
    n2[...] = rest[256:272]
    n3[...] = rest[272:280]
    own2[...] = left(t("z2"), w[:, :256])


def mask_pack(two, three, four, coarse, index, k0, k2, near, full):
    def plain(ref, b, z):
        if b == 0:
            return jnp.zeros(ref.shape[2:], F32)
        return ref[b - 1, z].astype(F32)

    for bz in range(2):
        for z in range(4):
            for bx in range(2):
                rows = [plain(two, 4 * bz + 2 * by + bx, z) for by in range(2)]
                at = bx * 64 + (bz * 4 + z) * 8
                for m in range(4):
                    full[m, at : at + 8] = jnp.concatenate(
                        [part[4 * m : 4 * m + 4] for part in rows], axis=0
                    )
        for z in range(2):
            rows = [
                jnp.concatenate([plain(three, 4 * bz + 2 * by + bx, z) for bx in range(2)], axis=1)
                for by in range(2)
            ]
            at = 128 + (bz * 2 + z) * 8
            for m in range(4):
                parts = [part[2 * m : 2 * m + 2] for part in rows]
                full[m, at : at + 8] = jnp.concatenate(parts + [jnp.zeros((4, 128), F32)], axis=0)
        rows = []
        for by in range(2):
            parts = [
                coarse[0].astype(F32) if bz + by + bx == 0 else plain(four, 4 * bz + 2 * by + bx, 0)
                for bx in range(2)
            ]
            rows.append(jnp.concatenate(parts + [jnp.zeros((4, 64), F32)], axis=1))
        at = 160 + bz * 8
        for m in range(4):
            parts = [jnp.zeros((4, 128), F32)] + [part[m : m + 1] for part in rows]
            full[m, at : at + 8] = jnp.concatenate(parts + [jnp.zeros((2, 128), F32)], axis=0)
    k0[...] = full[index[0]]
    k2[...] = full[lax.bitwise_xor(index[0], 2)]
    for n in range(2):
        near[n] = full[lax.bitwise_xor(index[0], 2 * n + 1)]


def z_mask(own2, own34, n1, n2, n3, k0, near, away, index, t, c2, c34, s1, s2, s3, full, keep2):
    full[index[0]] = k0[...]
    full[lax.bitwise_xor(index[0], 1)] = near[0]
    for n in range(2):
        full[lax.bitwise_xor(index[0], 2 + n)] = away[n]
    for a in range(4):
        for bz in range(2):
            for bx in range(2):
                at = bz * 128 + a * 32
                rows = full[a, bx * 64 + bz * 32 : bx * 64 + bz * 32 + 32]
                keep2[at : at + 32, bx * 128 : bx * 128 + 128] = rows
    tiles = []
    for slot in range(16):
        bz, a, z = slot // 8, slot // 2 % 4, slot % 2
        tile = full[a, 128 + (bz * 2 + z) * 8 : 136 + (bz * 2 + z) * 8]
        if slot < 8:
            bz, a = slot // 4, slot % 4
            tile = tile + full[a, 160 + bz * 8 : 168 + bz * 8]
        tiles.append(tile)
    keep34 = jnp.concatenate(tiles, axis=0)

    far = taller(jnp.concatenate([n2[...], n3[...]], axis=0), 8)
    part34 = (own34[...] + n1[:128] + left(t("z34p"), far)) * keep34
    c34[...] = part34
    s1[:128] = part34
    back = left(t("z34pt"), part34)
    s2[...] = back[:16]
    s3[...] = back[16:24]
    rim = taller(jnp.concatenate([n1[128:168], n1[168:208]], axis=1), 8)
    part2 = (own2[...] + left(t("z2u"), rim)) * keep2[...]
    c2[...] = part2
    back = left(t("z2ut"), part2)
    s1[128:168] = back[:40, :128]
    s1[168:208] = back[:40, 128:]


def z_join(c2, c34, s1, s2, s3, index, t, p0, p1, p2, p3, w):
    rim = taller(jnp.concatenate([s1[128:168], s1[168:208]], axis=1), 8)
    w[:, :256] = left(t("z2t"), c2[...]) + left(t("z2qt"), rim)
    rows = jnp.concatenate([c34[...], s1[:128], s2[...], s3[...]], axis=0)
    w[:, 256:] = left(t("z34t"), taller(rows, 8))
    for s, piece in enumerate((p0, p1, p2, p3)):
        piece[...] = w[block(index, s)]


def y_send(p0, p1, p2, p3, index, t, w, m1, m2, m3):
    for s, piece in enumerate((p0, p1, p2, p3)):
        w[block(index, -s)] = piece[...]
    m1[:256] = w[:, 256:]
    rim = left(t("y2ut"), w[:, :256])
    m1[256:320] = rim[:, :128]
    m1[320:384] = rim[:, 128:]
    far = left(t("y34pt"), w[:, 256:])
    m2[...] = far[:64]
    m3[...] = far[64:]


def deep_join(w, m1, m2, m3, dz, dy, dc, t, g, pz, py, pc, low):
    rim = jnp.concatenate([m1[256:320], m1[320:384]], axis=1)
    first = left(t("y2t"), w[:, :256]) + left(t("y2qt"), rim)
    rows = [w[:, 256:], m1[:256], m2[...], m3[...]]
    rest = left(t("y34t"), jnp.concatenate(rows, axis=0))
    wide = jnp.concatenate([first, rest[:256], rest[256:]], axis=1)
    low[...] = right(wide, t("xmi")).reshape(8, 32, 256)
    planes = [
        combine(SPREAD[:5, n], [lambda i=i: low[i + 3] for i in range(5)]) for n in range(5)
    ]
    for z in range(16):
        g[z] = combine(Z1LO[:, z], [lambda i=i: low[i] for i in range(8)])
    planes = jnp.concatenate(planes, axis=0)
    rims = [left(t("r5il"), planes)]
    for half in range(2):
        part = g[8 * half : 8 * half + 8].reshape(256, 256)
        rims.append(left(t("y1ult"), part)[:40])
    rims.append(left(t("r5ult"), planes))
    rims = right(jnp.concatenate(rims, axis=0), t("x1l"))
    pz[...] = dz[...] + rims[:320].reshape(5, 64, 512)
    py[...] = dy[...] + rims[320:400].reshape(2, 40, 512)
    pc[...] = dc[...] + rims[400:]


def own_join(g, low, t, out):
    for c in range(4):
        planes = []
        for z in range(4 * c, 4 * c + 4):
            corner = g[z, :32, :256] + low[z]
            top = jnp.concatenate([corner, g[z, :32, 256:]], axis=1)
            planes += [top, g[z, 32:]]
        part = left(t("y1i"), jnp.concatenate(planes, axis=0))
        out[4 * c : 4 * c + 4] = right(part, t("x1i")).reshape(4, 64, 512)


def finish(base, pz, py, pc, t, out, chunks):
    far = left(t("r5z"), pc[...])
    for half in range(2):
        rim = taller(py[half], 8) + far[48 * half : 48 * half + 48]
        extra = left(t("y1qt"), rim).reshape(8, 64, 512)
        for k in range(8):
            z = 8 * half + k
            plane = base[z] + extra[k]
            if z < 10:
                plane = plane + combine(BASIS[:, z], [lambda n=n: pz[n] for n in range(5)])
            out[z] = plane
            if z % 4 == 3:
                chunks[z // 4].start()
    for copy in chunks:
        copy.wait()


def details(f, q, qa, qb, qc, keep, t, g, pz, kept):
    for half in range(2):
        extra = left(t("y1u"), taller(q[half], 8))
        for c in range(2):
            z = 8 * half + 4 * c
            part = left(t("y1f"), f[z : z + 4].reshape(256, 512))
            g[z : z + 4] = (part + extra[256 * c : 256 * c + 256]).reshape(4, 64, 512)
    top = jnp.concatenate([qa[...], qb[:, :, :256]], axis=2)
    planes = jnp.concatenate([top, qb[:, :, 256:]], axis=1)
    planes = planes + left(t("r5u"), qc[...]).reshape(5, 64, 512)
    for c in range(4):
        rows = slice(16 * c, 16 * c + 16)
        rim = planes[:, rows].reshape(80, 512)
        out = left(t("z1f"), g[:, rows].reshape(256, 512)) + left(t("z1u"), rim)
        out = out.reshape(16, 16, 512)
        by = c // 2
        at = slice(16 * (c % 2), 16 * (c % 2) + 16)
        for bz in range(2):
            for bx in range(2):
                cols = slice(256 * bx, 256 * bx + 256)
                number = 4 * bz + 2 * by + bx
                if number:
                    mask = keep[number - 1, :, at].astype(F32)
                    part = out[8 * bz : 8 * bz + 8, :, cols] * mask
                else:
                    part = jnp.zeros((8, 16, 256), F32)
                kept[8 * bz : 8 * bz + 8, rows, cols] = part
    for n in range(5):
        plane = combine(SPREAD[:5, n], [lambda i=i: kept[i + 3] for i in range(5)])
        pz[n] = plane + combine(SPREAD[5:, n], [lambda i=i: kept[i + 11] for i in range(5)])
    for c in range(4):
        rows = slice(16 * c, 16 * c + 16)
        out = left(t("z1i"), kept[:, rows].reshape(256, 512))
        g[:, rows] = out.reshape(16, 16, 512)


def details_rim(g, dz, t, pz, py, pc):
    planes = dz[...].reshape(320, 512)
    rims = [left(t("r5i"), planes)]
    for half in range(2):
        part = g[8 * half : 8 * half + 8].reshape(512, 512)
        rims.append(left(t("y1ut"), part)[:40])
    rims.append(left(t("r5ut"), planes))
    rims = right(jnp.concatenate(rims, axis=0), t("x1i"))
    pz[...] = rims[:320].reshape(5, 64, 512)
    py[...] = rims[320:400].reshape(2, 40, 512)
    pc[...] = rims[400:]


def moved(value, by_z, by_y):
    pairs = [
        (z * GY + y, (z + by_z) % GZ * GY + (y + by_y) % GY) for z in range(GZ) for y in range(GY)
    ]
    return lax.ppermute(value, ("gz", "gy"), pairs)


def across(value, flip):
    return lax.ppermute(value, "gz", [(z, z ^ flip) for z in range(GZ)])


def exchanged(pieces):
    out = [pieces[0]]
    for s in range(1, MEMBERS):
        pairs = [(z, z // MEMBERS * MEMBERS + (z + s) % MEMBERS) for z in range(GZ)]
        out.append(lax.ppermute(pieces[s], "gz", pairs))
    return out


def on_device(vorticity, keep_one, keep_two, keep_three, keep_four, keep_coarse):
    index = lax.rem(lax.axis_index("gz"), MEMBERS).astype(jnp.int32).reshape(1)
    piece, half = (64, 384), (40, 512)

    q, qa, qb, qc = x_rims(vorticity)
    vorticity, q, qa, qc = lax.optimization_barrier((vorticity, q, qa, qc))
    q, qa, qc = moved(q, 0, -1), moved(qa, -1, 0), moved(qc, -1, -1)
    f, deep = x_split(vorticity)
    own, m1, m2, m3 = call(
        deep_split,
        3.0,
        [(256, 384), (384, 128), (64, 128), (16, 128)],
        f,
        q,
        qa,
        qc,
        shelves=DEEP,
        table=deep,
        scratch=[(16, 32, 256), (8, 32, 256)],
    )
    late, m1, m2, m3 = lax.optimization_barrier((index, m1, m2, m3))
    m1, m2, m3 = moved(m1, 0, -1), moved(m2, 0, -2), moved(m3, 0, -3)
    k0, k2, near = call(
        mask_pack,
        0.1,
        [(176, 128), (176, 128), (2, 176, 128)],
        keep_two,
        keep_three,
        keep_four,
        keep_coarse,
        index=late,
        scratch=[(4, 176, 128)],
    )
    near = across(near, 1)
    own, near = lax.optimization_barrier((own, near))
    away = jnp.stack([k2, near[1]])

    pieces = call(
        y_gather,
        0.7,
        [piece] * 4,
        own,
        m1,
        m2,
        m3,
        index=index,
        shelves=[["y2u", "y34p"]],
        scratch=[(256, 384)],
    )
    pieces = exchanged(pieces)
    own2, own34, n1, n2, n3 = call(
        z_split,
        0.5,
        [(256, 256), (128, 128), (208, 128), (16, 128), (8, 128)],
        *pieces,
        index=index,
        shelves=[["z2", "z34"], ["z2q"]],
        scratch=[(256, 384)],
    )
    away, qb, n1, n2, n3 = lax.optimization_barrier((away, qb, n1, n2, n3))
    n1, n2, n3 = moved(n1, -4, 0), moved(n2, -8, 0), moved(n3, -12, 0)
    away = across(away, 2)
    qb = moved(qb, -1, 0)

    c2, c34, s1, s2, s3 = call(
        z_mask,
        0.7,
        [(256, 256), (128, 128), (208, 128), (16, 128), (8, 128)],
        own2,
        own34,
        n1,
        n2,
        n3,
        k0,
        near,
        away,
        index=index,
        shelves=[["z2u"], ["z34p", "z34pt", "z2ut"]],
        scratch=[(4, 176, 128), (256, 256)],
    )
    f, s1, s2, s3 = lax.optimization_barrier((f, s1, s2, s3))
    s1, s2, s3 = moved(s1, 4, 0), moved(s2, 8, 0), moved(s3, 12, 0)
    g, dz = call(
        details,
        0.5,
        [(16, 64, 512), (5, 64, 512)],
        f,
        q,
        qa,
        qb,
        qc,
        keep_one,
        shelves=[["y1f", "z1f", "z1i", "z1u"], ["y1u", "r5u"]],
        scratch=[(16, 64, 512)],
    )
    c2, g = lax.optimization_barrier((c2, g))
    pieces = call(
        z_join,
        0.8,
        [piece] * 4,
        c2,
        c34,
        s1,
        s2,
        s3,
        index=index,
        shelves=[["z2t", "z34t", "z2qt"]],
        scratch=[(256, 384)],
    )
    pieces = exchanged(pieces)
    w, m1, m2, m3 = call(
        y_send,
        0.4,
        [(256, 384), (384, 128), (64, 128), (16, 128)],
        *pieces,
        index=index,
        shelves=[["y2ut"], ["y34pt"]],
    )
    g, m1, m2, m3 = lax.optimization_barrier((g, m1, m2, m3))
    m1, m2, m3 = moved(m1, 0, 1), moved(m2, 0, 2), moved(m3, 0, 3)
    dz, dy, dc = call(
        details_rim,
        0.5,
        [(5, 64, 512), (2, 40, 512), half],
        g,
        dz,
        shelves=[["x1i"], ["r5i"], ["y1ut"], ["r5ut"]],
    )
    low, pz, py, pc = call(
        deep_join,
        2.5,
        [(16, 32, 256), (5, 64, 512), (2, 40, 512), half],
        w,
        m1,
        m2,
        m3,
        dz,
        dy,
        dc,
        shelves=[["y34t"], ["xmi", "y2t"], ["x1l", "y2qt"], ["y1ult", "r5ult"], ["r5il"]],
        scratch=[(8, 32, 256)],
    )
    pz, py, pc = moved(pz, 1, 0), moved(py, 0, 1), moved(pc, 1, 1)
    (base,) = call(
        own_join, 0.5, [(16, 64, 512)], g, low, shelves=[["x1i"], ["y1i"]]
    )
    (out,) = call(
        finish,
        2.0,
        [(16, 64, 512)],
        base,
        pz,
        py,
        pc,
        shelves=[["y1qt", "r5z"]],
        streamed=True,
    )
    return out


def solution(mesh):
    in_specs = (
        P("gz", "gy", None),
        P(None, "gz", "gy", None),
        P(None, "gz", "gy", None),
        P(None, "gz", "gy", None),
        P(None, "gz", "gy", None),
        P("gz", "gy", None),
    )
    out_specs = P("gz", "gy", None)
    return jax.shard_map(
        on_device, mesh=mesh, in_specs=in_specs, out_specs=out_specs, check_vma=False
    )
```
